32 devices in a mesh: grp: 2 (over x), seq: 8 (over z, y), col: 2 (over core).
Axes of the slice: x: 2, y: 2, z: 4, core: 2. Of those that a mesh axis runs over, the one named last changes fastest.
Arguments:
- signal: bfloat16 [8192, 1408], P(('grp', 'seq'), 'col'), parts along dimension 0, may hold values from -6 to 6
- conv_weight: bfloat16 [5, 1408, 1408], P(None, None, 'col'), may hold values from -0.15625 to 0.15625
- conv_gain: float32 [1408], replicated, may hold values from 0.1 to 1.9
- embed_weight: bfloat16 [1408, 1536], P('col', 'seq'), may hold values from -0.15625 to 0.15625
- attn_gain: float32 [1536], replicated, may hold values from 0.1 to 1.9
- query_weight: bfloat16 [1536, 1024], P('seq'), may hold values from -4 to 4
- keyvalue_weight: bfloat16 [1536, 320], P('seq'), may hold values from -4 to 4
- output_weight: bfloat16 [1536, 1536], P(None, 'seq'), may hold values from -0.15625 to 0.15625
- rowcol_weight: bfloat16 [1536, 256], replicated, may hold values from -0.15625 to 0.15625
- pair_weight: bfloat16 [128, 128], replicated, may hold values from -0.5 to 0.5
Outputs:
- tokens: bfloat16 [2048, 1536], P(('grp', 'seq', 'col')), parts along dimension 0
- pair_out: bfloat16 [128, 64, 128], P(('grp', 'seq'), 'col'), parts along dimension 0
The draws below stay inside these ranges and needn't reach their ends.
There are 2 independent parts, one for each index of `grp`. The reference program is written for one: setup_inputs(seed, part) draws one part's arguments, and reference() takes and returns one part's arrays. A program takes and returns all parts, laid end to end along the dimension named above; an argument that names none is the same for every part. Nothing has to cross between parts.
All inputs are finite; a program needn't handle non-finite values.
Results may differ from the reference program's by a relative error of at most 0.015.
Values may be sent and summed in bfloat16 or wider, within the bound.
No kernel may reach another device: no remote copies, remote signals or barrier semaphores. Data moves between devices by JAX's collectives and lax.ppermute only.
A program may use at most 128 MiB of HBM per device.

```python
import math
import jax
import jax.numpy as jnp
from jax import lax

C = 1408
D = 1536
H = 8
DK = 128
DV = 192
F = 128
TAPS = 5
POOL = 4
PAIR_POOL = 16
L = 4096


def key_matrix(key):
    return jax.random.truncated_normal(jax.random.fold_in(key, 11), -6.0, 6.0, (D, DK), jnp.float32) / math.sqrt(D)


def draw_keyvalue_weight(key, part):
    keys = key_matrix(key)
    values = jax.random.truncated_normal(jax.random.fold_in(key, 12), -6.0, 6.0, (D, DV), jnp.float32) / math.sqrt(D)
    return jnp.clip(jnp.concatenate([keys, values], axis=1), -4.0, 4.0).astype(jnp.bfloat16)


def draw_query_weight(key, part):
    noise = jax.random.truncated_normal(jax.random.fold_in(key, 13), -6.0, 6.0, (D, H * DK), jnp.float32) * (2.0 / math.sqrt(D))
    result = noise
    return jnp.clip(result, -4.0, 4.0).astype(jnp.bfloat16)


def block_scale(stream_key, shape, split, least, top_value):
    loudness = 1.0
    for dim, shards_of in split:
        heights = jax.random.uniform(jax.random.fold_in(jax.random.fold_in(stream_key, 6), dim), (shards_of,), jnp.float32, least / len(split), top_value / len(split))
        loudness = loudness * jnp.repeat(jnp.exp(heights), shape[dim] // shards_of).reshape((-1,) + (1,) * (len(shape) - 1 - dim))
    return loudness


def scatter_about(key, shape, scale, most, cuts=(), kind=jnp.bfloat16):
    gain = block_scale(key, shape, cuts, -0.22, 0.18) if cuts else 1.0
    values = jax.random.normal(key, shape, jnp.float32) * scale * gain
    return jnp.minimum(jnp.maximum(values, -most), most).astype(kind)


def setup_inputs(seed: int = 0, part: int = 0) -> dict:
    arg_keys = jax.random.split(jax.random.key(seed), 11)
    own_keys = jax.random.split(jax.random.fold_in(arg_keys[10], part), 11)
    return {
        "signal": scatter_about(own_keys[0], (L, C), 1.0, 6.0, ((0, 8), (1, 2))),
        "conv_weight": scatter_about(arg_keys[1], (TAPS, C, C), C ** -0.5, 0.15625, ((2, 2),)),
        "conv_gain": jnp.clip(1.0 + 0.18 * jax.random.normal(arg_keys[2], (C,), jnp.float32), 0.1, 1.9),
        "embed_weight": scatter_about(arg_keys[3], (C, D), C ** -0.5, 0.15625, ((0, 2), (1, 8))),
        "attn_gain": jnp.clip(1.0 + 0.18 * jax.random.normal(arg_keys[4], (D,), jnp.float32), 0.1, 1.9),
        "query_weight": draw_query_weight(jax.random.fold_in(arg_keys[10], 71), part),
        "keyvalue_weight": draw_keyvalue_weight(jax.random.fold_in(arg_keys[10], 71), part),
        "output_weight": scatter_about(arg_keys[7], (H * DV, D), (H * DV) ** -0.5, 0.15625, ((1, 8),)),
        "rowcol_weight": scatter_about(arg_keys[8], (D, 2 * F), D ** -0.5, 0.15625),
        "pair_weight": scatter_about(arg_keys[9], (F, F), F ** -0.5, 0.5),
    }


def rms_scale(values, gain_vector):
    return values * lax.rsqrt(lax.optimization_barrier(jnp.mean(values * values, axis=-1, keepdims=True)) + 1e-06) * gain_vector

def reference(signal, conv_weight, conv_gain, embed_weight, attn_gain, query_weight, keyvalue_weight, output_weight, rowcol_weight, pair_weight):
    length = signal.shape[0]
    features_in = signal.astype(jnp.float32)
    activated = jax.nn.gelu(rms_scale(features_in, conv_gain.astype(jnp.float32)), approximate=True).astype(jnp.bfloat16)
    half_width = TAPS // 2
    padded = jnp.pad(activated, ((half_width, half_width), (0, 0)))
    summed = features_in
    for tap_index in range(TAPS):
        summed = summed + jnp.dot(padded[tap_index:tap_index + length], conv_weight[tap_index], preferred_element_type=jnp.float32)
    pooled = lax.optimization_barrier(jnp.mean(summed.reshape(length // POOL, POOL, -1), axis=1)).astype(jnp.bfloat16)
    embedded = jnp.dot(pooled, embed_weight, preferred_element_type=jnp.float32).astype(jnp.bfloat16)
    normed = rms_scale(embedded.astype(jnp.float32), attn_gain.astype(jnp.float32)).astype(jnp.bfloat16)
    queries = (jnp.dot(normed, query_weight, preferred_element_type=jnp.float32) * DK ** (-0.5)).astype(jnp.bfloat16)
    keyvalue = jnp.dot(normed, keyvalue_weight, preferred_element_type=jnp.float32).astype(jnp.bfloat16)
    keys = keyvalue[:, :DK]
    values = keyvalue[:, DK:]
    token_count = queries.shape[0]
    per_head = jnp.transpose(queries.reshape(token_count, H, DK), (1, 0, 2))

    def one_head(head_queries):
        scores = lax.dot_general(head_queries, keys, (((1,), (1,)), ((), ())), preferred_element_type=jnp.float32)
        peak = lax.optimization_barrier(jnp.max(scores, axis=1, keepdims=True))
        weights = jnp.exp(scores - peak)
        total = lax.optimization_barrier(jnp.sum(weights, axis=1, keepdims=True))
        mixed = jnp.dot(weights.astype(jnp.bfloat16), values, preferred_element_type=jnp.float32) / total
        return mixed.astype(jnp.bfloat16)
    attended = lax.map(one_head, per_head)
    attended = jnp.transpose(attended, (1, 0, 2)).reshape(token_count, H * DV)
    attention_out = jnp.dot(attended, output_weight, preferred_element_type=jnp.float32)
    tokens = (embedded.astype(jnp.float32) + attention_out).astype(jnp.bfloat16)
    pair_pool = lax.optimization_barrier(jnp.mean(tokens.astype(jnp.float32).reshape(token_count // PAIR_POOL, PAIR_POOL, -1), axis=1)).astype(jnp.bfloat16)
    projected = jnp.dot(pair_pool, rowcol_weight, preferred_element_type=jnp.float32).astype(jnp.bfloat16)
    row_part = projected[:, :F].astype(jnp.float32)
    column_part = projected[:, F:].astype(jnp.float32)
    hidden = jax.nn.gelu(row_part[:, None, :] + column_part[None, :, :], approximate=True).astype(jnp.bfloat16)
    pair_rows = hidden.shape[0]
    pair_out = jnp.dot(hidden.reshape(-1, F), pair_weight, preferred_element_type=jnp.float32).astype(jnp.bfloat16)
    return (tokens, pair_out.reshape(pair_rows, pair_rows, F))
```

```python
import functools
import math

import jax
import jax.numpy as jnp
import numpy as np
from jax import lax
from jax.experimental import pallas as pl
from jax.experimental.pallas import tpu as pltpu
from jax.sharding import PartitionSpec as P

DK = 128
DV = 192
POOL = 4
PAIR_POOL = 16
EPS = 1e-06
VMEM = pltpu.VMEM
F32 = jnp.float32
BF16 = jnp.bfloat16


def gelu(x):
    return 0.5 * x * (1.0 + jnp.tanh(math.sqrt(2.0 / math.pi) * (x + 0.044715 * (x * x * x))))


def dot_nt(a, b):
    return lax.dot_general(a, b, (((1,), (1,)), ((), ())), preferred_element_type=F32)


def dot_nn(a, b):
    return lax.dot_general(a, b, (((1,), (0,)), ((), ())), preferred_element_type=F32)


def params(mib, **kw):
    return pltpu.CompilerParams(vmem_limit_bytes=mib << 20, **kw)


def vspec(n):
    return [pl.BlockSpec(memory_space=VMEM)] * n


def ring_order(rows):
    evens = [i for i in range(rows) if i % 2 == 1]
    odds = [i for i in range(rows) if i % 2 == 0 and i > 0]
    return [0] + evens + odds[::-1]


def gather_plan(count):
    if count % 2 or count > 16:
        return None
    return ring_order(count // 2)


def pick(index, table):
    value = jnp.int32(table[0])
    for i, entry in enumerate(table[1:], 1):
        value = jnp.where(index == i, jnp.int32(entry), value)
    return value


def owners(count):
    ring = gather_plan(count)
    if ring is None:
        return [jnp.int32(0)]
    me = lax.axis_index("seq")
    row, side = me // 2, me % 2
    rows = len(ring)
    place = pick(row, [ring.index(i) for i in range(rows)])
    result = []
    for step in range(rows):
        source = pick(lax.rem(place + rows - step, rows), ring)
        result.append(source * 2 + side)
        result.append(source * 2 + 1 - side)
    return result


def gather_blocks(own, count):
    ring = gather_plan(count)
    if ring is None:
        return [lax.all_gather(own, "seq", axis=0, tiled=True)]
    rows = len(ring)
    step_pairs = []
    for k in range(rows):
        a, b = ring[k], ring[(k + 1) % rows]
        step_pairs += [(2 * a + s, 2 * b + s) for s in range(2)]
    side_pairs = [(i, i ^ 1) for i in range(count)]
    pieces = []
    held = own
    for step in range(rows):
        ahead = lax.ppermute(held, "seq", step_pairs) if step < rows - 1 else None
        pieces += [held, lax.ppermute(held, "seq", side_pairs)]
        held = ahead
    return pieces


def conv_kernel(own_ref, other_ref, halo_ref, gaincol_ref, gainrow_ref, pool_ref, poolhalo_ref, weight_hbm,
                out_ref, act, slabs, weights, sems):
    taps, width, channels = weights.shape
    copies = [pltpu.make_async_copy(weight_hbm.at[t], weights.at[t], sems.at[t]) for t in range(taps)]
    for c in copies:
        c.start()
    col = lax.axis_index("col")
    half, positions = own_ref.shape
    tokens = out_ref.shape[0]
    step = 64
    halves = ((own_ref, col), (other_ref, 1 - col))
    squares = jnp.zeros((8, positions), F32)
    for ref, _ in halves:
        for j in range(half // step):
            x = ref[j * step:(j + 1) * step, :].astype(F32)
            x = x * x
            for i in range(step // 8):
                squares = squares + x[i * 8:(i + 1) * 8]
    scale = lax.rsqrt(jnp.sum(squares, axis=0, keepdims=True) / channels + EPS)
    for ref, index in halves:
        for j in range(half // step):
            start = pl.multiple_of(index * half + j * step, step)
            x = ref[j * step:(j + 1) * step, :].astype(F32)
            x = x * scale * gaincol_ref[pl.ds(start, step), :]
            act[pl.ds(start, step), :] = gelu(x).astype(BF16)
    h = halo_ref[...].astype(F32)
    h = h * lax.rsqrt(jnp.sum(h * h, axis=1, keepdims=True) / channels + EPS) * gainrow_ref[...]
    h = gelu(h).astype(BF16)
    for t in range(taps):
        rows = slice(t * tokens, (t + 1) * tokens)
        slabs[t] = (dot_nt(pool_ref[rows], act[...]) + dot_nn(poolhalo_ref[rows], h)).astype(BF16)
    total = dot_nt(pool_ref[(taps // 2) * tokens:(taps // 2 + 1) * tokens], own_ref[...])
    for t in range(taps):
        copies[t].wait()
        total = total + dot_nt(slabs[t], weights[t])
    out_ref[...] = total.astype(BF16)


def embed_kernel(pieces, pooled_ref, *refs):
    blocks, out_ref = refs[:pieces], refs[pieces]
    for ref, owner in zip(blocks, owners(lax.axis_size("seq"))):
        out_ref[owner] = dot_nt(pooled_ref[...], ref[...]).astype(BF16)


def embedded_of(a_ref, b_ref, rows=slice(None)):
    return (a_ref[:, rows].astype(F32) + b_ref[:, rows].astype(F32)).astype(BF16).astype(F32)


def query_kernel(pieces, features, part_ref, other_ref, gain_ref, *refs):
    blocks, (query_ref, kv_ref, normed) = refs[:pieces], refs[pieces:]
    embedded = embedded_of(part_ref, other_ref)
    count, _, width = embedded.shape
    squares = jnp.sum(jnp.sum(embedded * embedded, axis=0), axis=1, keepdims=True)
    scale = lax.rsqrt(squares / (count * width) + EPS)
    normed[...] = (embedded * scale[None] * gain_ref[...]).astype(BF16)
    total = None
    for ref, owner in zip(blocks, owners(lax.axis_size("seq"))):
        part = dot_nn(normed[owner], ref[...])
        total = part if total is None else total + part
    query_ref[...] = (total[:, :features] * DK ** (-0.5)).astype(BF16)
    kv = total[:, features:].astype(BF16)
    for i in range(kv_ref.shape[0]):
        kv_ref[i] = kv


def attend_kernel(query_ref, key_ref, value_ref, out_ref):
    tokens, features = query_ref.shape
    keys = key_ref[:, :DK]
    values = value_ref[...]
    for h in range(features // DK):
        scores = dot_nt(query_ref[:, h * DK:(h + 1) * DK], keys)
        weights = jnp.exp(scores - jnp.max(scores, axis=1, keepdims=True))
        total = jnp.sum(weights, axis=1, keepdims=True)
        out_ref[h] = (dot_nn(weights.astype(BF16), values) / total).astype(BF16)


def output_kernel(pieces, attended_ref, *refs):
    blocks, (mine_ref, theirs_ref, whole) = refs[:pieces], refs[pieces:]
    heads = attended_ref.shape[0]
    flat = jnp.concatenate([attended_ref[h] for h in range(heads)], axis=1)
    for ref, owner in zip(blocks, owners(lax.axis_size("seq"))):
        whole[owner] = dot_nt(flat, ref[...])
    col = lax.axis_index("col")
    rows = mine_ref.shape[1]
    mine_ref[...] = whole[:, pl.ds(pl.multiple_of(col * rows, rows), rows)]
    theirs_ref[...] = whole[:, pl.ds(pl.multiple_of((1 - col) * rows, rows), rows)].astype(BF16)


def token_kernel(part_ref, other_ref, mine_ref, theirs_ref, weight_ref, token_ref, send_ref):
    col = lax.axis_index("col")
    count, rows, width = mine_ref.shape
    rows_here = pl.ds(pl.multiple_of(col * rows, rows), rows)
    embedded = embedded_of(part_ref, other_ref, rows_here)
    tokens = (embedded + mine_ref[...] + theirs_ref[...].astype(F32)).astype(BF16)
    token_ref[...] = jnp.concatenate([tokens[s] for s in range(count)], axis=1)
    projected = None
    for s in range(count):
        pooled = jnp.mean(tokens[s].astype(F32).reshape(rows // PAIR_POOL, PAIR_POOL, width), axis=1).astype(BF16)
        part = dot_nn(pooled, weight_ref[s * width:(s + 1) * width])
        projected = part if projected is None else projected + part
    projected = projected.astype(BF16)
    for i in range(send_ref.shape[0]):
        send_ref[i] = projected


def pair_kernel(all_ref, weight_ref, out_ref, rows_here, columns_here):
    seq, col = lax.axis_index("seq"), lax.axis_index("col")
    devices, each, _ = all_ref.shape
    features = weight_ref.shape[0]
    cols = lax.axis_size("col")
    for c in range(cols):
        rows_here[c * each:(c + 1) * each] = all_ref[seq * cols + c].astype(F32)[:, :features]
    span = devices // cols
    for j in range(span):
        columns_here[j * each:(j + 1) * each] = all_ref[col * span + j].astype(F32)[:, features:]
    hidden = gelu(rows_here[...][:, None, :] + columns_here[...][None, :, :])
    r, c, f = hidden.shape
    out_ref[...] = dot_nn(hidden.reshape(r * c, f).astype(BF16), weight_ref[...]).reshape(r, c, f).astype(BF16)


def pooling_matrices(positions, taps):
    tokens, reach = positions // POOL, taps // 2
    main = np.zeros((taps, tokens, positions), np.float32)
    halo = np.zeros((taps, tokens, 16), np.float32)
    for t in range(taps):
        for i in range(tokens):
            for j in range(POOL):
                p = POOL * i + j + t - reach
                if p < 0:
                    halo[t, i, p + reach] += 1.0 / POOL
                elif p >= positions:
                    halo[t, i, reach + p - positions] += 1.0 / POOL
                else:
                    main[t, i, p] += 1.0 / POOL
    as_rows = lambda a: jnp.asarray(a.reshape(taps * tokens, -1), BF16)
    return as_rows(main), as_rows(halo)


def cost(flops, size):
    return pl.CostEstimate(flops=int(flops), bytes_accessed=int(size), transcendentals=0)


def on_device(signal, conv_weight, conv_gain, embed_weight, attn_gain, query_weight, keyvalue_weight,
              output_weight, rowcol_weight, pair_weight):
    col = lax.axis_index("col")
    count, cols = lax.axis_size("seq"), lax.axis_size("col")
    positions, half = signal.shape
    taps, channels, _ = conv_weight.shape
    reach = taps // 2
    tokens = positions // POOL
    width = embed_weight.shape[1] * count
    features = query_weight.shape[1] // cols
    heads = features // DK
    swap = [(i, (i + 1) % cols) for i in range(cols)]
    shape = jax.ShapeDtypeStruct

    signal_t = signal.T
    other_t = lax.ppermute(signal_t, "col", swap)
    first, last = signal[:reach], signal[positions - reach:]

    def shifted(rows, by, across):
        pairs = [
            (s * cols + c, (s + by) * cols + ((c + 1) % cols if across else c))
            for s in range(count) for c in range(cols) if 0 <= s + by < count
        ]
        return lax.ppermute(rows, ("seq", "col"), pairs)

    own_halo = jnp.concatenate([shifted(last, 1, False), shifted(first, -1, False)], axis=0)
    other_halo = jnp.concatenate([shifted(last, 1, True), shifted(first, -1, True)], axis=0)
    halo = jnp.where(
        col == 0, jnp.concatenate([own_halo, other_halo], axis=1), jnp.concatenate([other_halo, own_halo], axis=1)
    )
    halo = jnp.pad(halo, ((0, 16 - 2 * reach), (0, 0)))

    embed_blocks = gather_blocks(embed_weight.T, count)
    query_own = jnp.concatenate(
        [
            lax.dynamic_slice_in_dim(query_weight, col * features, features, 1),
            lax.dynamic_slice_in_dim(keyvalue_weight, col * DK, DV, 1),
        ],
        axis=1,
    )
    query_blocks = gather_blocks(query_own, count)
    output_own = lax.dynamic_slice_in_dim(output_weight.T, col * heads * DV, heads * DV, 1)
    output_blocks = gather_blocks(output_own, count)
    pieces = len(embed_blocks)
    block = width // pieces

    pool_main, pool_halo = pooling_matrices(positions, taps)
    pooled = pl.pallas_call(
        conv_kernel,
        out_shape=shape((tokens, half), BF16),
        in_specs=vspec(7) + [pl.BlockSpec(memory_space=pl.ANY)],
        out_specs=pl.BlockSpec(memory_space=VMEM),
        scratch_shapes=[
            pltpu.VMEM((channels, positions), BF16),
            pltpu.VMEM((taps, tokens, channels), BF16),
            pltpu.VMEM((taps, half, channels), BF16),
            pltpu.SemaphoreType.DMA((taps,)),
        ],
        compiler_params=params(36),
        cost_estimate=cost(2 * taps * tokens * channels * (half + positions), 2 * taps * channels * half * 2),
        name="conv",
    )(
        signal_t, other_t, halo, conv_gain.reshape(channels, 1), conv_gain.reshape(1, channels),
        pool_main, pool_halo, conv_weight.transpose(0, 2, 1),
    )

    part = pl.pallas_call(
        functools.partial(embed_kernel, pieces),
        out_shape=shape((pieces, tokens, block), BF16),
        in_specs=vspec(1 + pieces),
        out_specs=pl.BlockSpec(memory_space=VMEM),
        compiler_params=params(16),
        cost_estimate=cost(2 * tokens * half * width, 2 * half * width),
        name="embed",
    )(pooled, *embed_blocks)
    other_part = lax.ppermute(part, "col", swap)

    queries, keyvalue = pl.pallas_call(
        functools.partial(query_kernel, pieces, features),
        out_shape=(shape((tokens, features), BF16), shape((count, tokens, DV), BF16)),
        in_specs=vspec(3 + pieces),
        out_specs=vspec(2),
        scratch_shapes=[pltpu.VMEM((pieces, tokens, block), BF16)],
        compiler_params=params(32),
        cost_estimate=cost(2 * tokens * width * (features + DV), 2 * width * (features + DV)),
        name="query",
    )(part, other_part, attn_gain.reshape(pieces, 1, block), *query_blocks)

    gathered = lax.all_to_all(keyvalue, "seq", 0, 0).reshape(count * tokens, DV)
    gathered_other = lax.ppermute(gathered, "col", swap)
    keys = jnp.where(col == 0, gathered, gathered_other)
    values = jnp.where(col == 0, gathered_other, gathered)

    attended = pl.pallas_call(
        attend_kernel,
        out_shape=shape((heads, tokens, DV), BF16),
        in_specs=vspec(3),
        out_specs=pl.BlockSpec(memory_space=VMEM),
        compiler_params=params(48),
        cost_estimate=cost(2 * tokens * heads * count * tokens * (DK + DV), 4 * count * tokens * DV),
        name="attend",
    )(queries, keys, values)

    own_rows = tokens // cols
    mine, theirs = pl.pallas_call(
        functools.partial(output_kernel, pieces),
        out_shape=(shape((pieces, own_rows, block), F32), shape((pieces, own_rows, block), BF16)),
        in_specs=vspec(1 + pieces),
        out_specs=vspec(2),
        scratch_shapes=[pltpu.VMEM((pieces, tokens, block), F32)],
        compiler_params=params(32),
        cost_estimate=cost(2 * tokens * heads * DV * width, 2 * heads * DV * width),
        name="output",
    )(attended, *output_blocks)
    theirs = lax.ppermute(theirs, "col", swap)

    out_width = rowcol_weight.shape[1]
    each = own_rows // PAIR_POOL
    out_tokens, projected = pl.pallas_call(
        token_kernel,
        out_shape=(shape((own_rows, width), BF16), shape((count * cols, each, out_width), BF16)),
        in_specs=vspec(5),
        out_specs=vspec(2),
        compiler_params=params(16),
        cost_estimate=cost(2 * each * width * out_width, 2 * width * out_width),
        name="tokens",
    )(part, other_part, mine, theirs, rowcol_weight)
    all_projected = lax.all_to_all(projected, ("seq", "col"), 0, 0)

    pair_rows, span = each * cols, each * count
    pair_features = pair_weight.shape[0]
    pair_out = pl.pallas_call(
        pair_kernel,
        out_shape=shape((pair_rows, span, pair_features), BF16),
        in_specs=vspec(2),
        out_specs=pl.BlockSpec(memory_space=VMEM),
        scratch_shapes=[pltpu.VMEM((pair_rows, pair_features), F32), pltpu.VMEM((span, pair_features), F32)],
        compiler_params=params(16),
        cost_estimate=cost(2 * pair_rows * span * pair_features**2, 2 * pair_rows * span * pair_features),
        name="pair",
    )(all_projected, pair_weight)
    return out_tokens, pair_out


def solution(mesh):
    placed = (
        P(("grp", "seq"), "col"),
        P(None, None, "col"),
        P(),
        P("col", "seq"),
        P(),
        P("seq", None),
        P("seq", None),
        P(None, "seq"),
        P(),
        P(),
    )
    return jax.shard_map(
        on_device,
        mesh=mesh,
        in_specs=placed,
        out_specs=(P(("grp", "seq", "col"), None), P(("grp", "seq"), "col", None)),
        check_vma=False,
    )
```

```python
import functools
import math

import jax
import jax.numpy as jnp
import numpy as np
from jax import lax
from jax.experimental import pallas as pl
from jax.experimental.pallas import tpu as pltpu
from jax.sharding import PartitionSpec as P

DK = 128
DV = 192
POOL = 4
PAIR_POOL = 16
EPS = 1e-06
VMEM = pltpu.VMEM
F32 = jnp.float32
BF16 = jnp.bfloat16


def gelu(x):
    return 0.5 * x * (1.0 + jnp.tanh(math.sqrt(2.0 / math.pi) * (x + 0.044715 * (x * x * x))))


def dot_nt(a, b):
    return lax.dot_general(a, b, (((1,), (1,)), ((), ())), preferred_element_type=F32)


def dot_nn(a, b):
    return lax.dot_general(a, b, (((1,), (0,)), ((), ())), preferred_element_type=F32)


def params(mib, **kw):
    return pltpu.CompilerParams(vmem_limit_bytes=mib << 20, **kw)


def vspec(n):
    return [pl.BlockSpec(memory_space=VMEM)] * n


RING = (0, 1, 3, 2)


def planned(count, groups):
    return count == 2 * len(RING) and groups == 2


def pick(index, table):
    value = jnp.int32(table[0])
    for i, entry in enumerate(table[1:], 1):
        value = jnp.where(index == i, jnp.int32(entry), value)
    return value


def owners(count, groups):
    if not planned(count, groups):
        return [jnp.int32(0)]
    group, me = lax.axis_index("grp"), lax.axis_index("seq")
    side, place = me % 2, pick(me // 2, [RING.index(i) for i in range(4)])
    result = []
    for step in (0, 3 + 2 * group, 1 + 2 * group, 2):
        row = pick(lax.rem(place + step, 4), RING)
        result += [2 * row + side, 2 * row + 1 - side]
    return result


class Blocks:
    def __init__(self, own, count):
        self.count = count
        self.at = {"own": own}

    def along(self, source, target):
        pairs = []
        for group in range(2):
            for k in range(4):
                a, b = RING[k], RING[(k + 1) % 4]
                if group:
                    a, b = b, a
                pairs += [(group * self.count + 2 * a + i, group * self.count + 2 * b + i) for i in range(2)]
        self.at[target] = lax.ppermute(self.at[source], ("grp", "seq"), pairs)

    def across(self, source, target):
        self.at[target] = lax.ppermute(self.at[source], "seq", [(i, i ^ 1) for i in range(self.count)])

    def between(self, source, target):
        self.at[target] = lax.ppermute(self.at[source], "grp", [(0, 1), (1, 0)])

    def pieces(self):
        names = ("own", "own2", "step", "step2", "cross", "cross2", "far", "far2")
        return [self.at[name] for name in names]


def after(values, *done):
    return lax.optimization_barrier((values, done))[0]


def conv_kernel(own_ref, other_ref, halo_ref, gaincol_ref, gainrow_ref, pool_ref, poolhalo_ref, weight_hbm,
                out_ref, act, slabs, weights, sems):
    taps, width, channels = weights.shape
    copies = [pltpu.make_async_copy(weight_hbm.at[t], weights.at[t], sems.at[t]) for t in range(taps)]
    for c in copies:
        c.start()
    col = lax.axis_index("col")
    half, positions = own_ref.shape
    tokens = out_ref.shape[1]
    step = 64
    halves = ((own_ref, col), (other_ref, 1 - col))
    squares = jnp.zeros((8, positions), F32)
    for ref, _ in halves:
        for j in range(half // step):
            x = ref[j * step:(j + 1) * step, :].astype(F32)
            x = x * x
            for i in range(step // 8):
                squares = squares + x[i * 8:(i + 1) * 8]
    scale = lax.rsqrt(jnp.sum(squares, axis=0, keepdims=True) / channels + EPS)
    for ref, index in halves:
        for j in range(half // step):
            start = pl.multiple_of(index * half + j * step, step)
            x = ref[j * step:(j + 1) * step, :].astype(F32)
            x = x * scale * gaincol_ref[pl.ds(start, step), :]
            act[pl.ds(start, step), :] = gelu(x).astype(BF16)
    h = halo_ref[...].astype(F32)
    h = h * lax.rsqrt(jnp.sum(h * h, axis=1, keepdims=True) / channels + EPS) * gainrow_ref[...]
    h = gelu(h)
    edges = lax.dot_general(h.astype(BF16), poolhalo_ref[...], (((0,), (0,)), ((), ())), preferred_element_type=F32)
    slabs[...] = (dot_nn(act[...], pool_ref[...]) + edges).astype(BF16)
    middle = (taps // 2) * tokens
    total = dot_nn(own_ref[...], pool_ref[:, middle:middle + tokens])
    for t in range(taps):
        copies[t].wait()
        total = total + dot_nn(weights[t], slabs[:, t * tokens:(t + 1) * tokens])
    out_ref[...] = total.astype(BF16)


def block_owners():
    return owners(lax.axis_size("seq"), lax.axis_size("grp"))


def embed_kernel(pieces, pooled_ref, *refs):
    blocks, out_ref = refs[:pieces], refs[pieces]
    for ref, owner in zip(blocks, block_owners()):
        out_ref[owner] = dot_nn(ref[...], pooled_ref[...]).astype(BF16)


def query_kernel(pieces, features, part_ref, other_ref, gain_ref, *refs):
    blocks, (query_ref, kv_ref, embedded_ref, normed) = refs[:pieces], refs[pieces:]
    count, width, _ = part_ref.shape
    squares = 0.0
    for s in range(count):
        e = (part_ref[s].astype(F32) + other_ref[s].astype(F32)).astype(BF16)
        e = e.astype(F32)
        squares = squares + jnp.sum(e * e, axis=0, keepdims=True)
    scale = lax.rsqrt(squares / (count * width) + EPS)
    for s in range(count):
        e = (part_ref[s].astype(F32) + other_ref[s].astype(F32)).astype(BF16).astype(F32)
        embedded_ref[s] = e.T.astype(BF16)
        normed[s] = ((e * scale).T * gain_ref[s]).astype(BF16)
    total = None
    for ref, owner in zip(blocks, block_owners()):
        part = dot_nn(normed[owner], ref[...])
        total = part if total is None else total + part
    query_ref[...] = (total[:, :features] * DK ** (-0.5)).astype(BF16)
    kv = total[:, features:].astype(BF16)
    for i in range(kv_ref.shape[0]):
        kv_ref[i] = kv


def attend_kernel(query_ref, own_ref, other_ref, out_ref):
    tokens, features = query_ref.shape
    first = lax.axis_index("col") == 0
    keys = jnp.where(first, own_ref[:, :DK], other_ref[:, :DK])
    values = jnp.where(first, other_ref[...], own_ref[...])
    for h in range(features // DK):
        scores = dot_nt(query_ref[:, h * DK:(h + 1) * DK], keys)
        weights = jnp.exp(scores - jnp.max(scores, axis=1, keepdims=True))
        total = jnp.sum(weights, axis=1, keepdims=True)
        out_ref[h] = (dot_nn(weights.astype(BF16), values) / total).astype(BF16)


def output_kernel(pieces, attended_ref, *refs):
    blocks, out_ref = refs[:pieces], refs[pieces]
    heads = attended_ref.shape[0]
    flat = jnp.concatenate([attended_ref[h] for h in range(heads)], axis=1)
    for ref, owner in zip(blocks, block_owners()):
        out_ref[owner] = dot_nt(flat, ref[...]).astype(BF16)


def token_kernel(embedded_ref, part_ref, other_ref, weight_ref, token_ref, send_ref, whole):
    col = lax.axis_index("col")
    count, rows, width = part_ref.shape
    projected = None
    for s in range(count):
        tokens = (embedded_ref[s].astype(F32) + (part_ref[s].astype(F32) + other_ref[s].astype(F32))).astype(BF16)
        whole[s] = tokens
        pooled = jnp.mean(tokens.astype(F32).reshape(rows // PAIR_POOL, PAIR_POOL, width), axis=1).astype(BF16)
        part = dot_nn(pooled, weight_ref[s * width:(s + 1) * width])
        projected = part if projected is None else projected + part
    own = token_ref.shape[0]
    mine = pl.ds(pl.multiple_of(col * own, own), own)
    token_ref[...] = jnp.concatenate([whole[s, mine] for s in range(count)], axis=1)
    projected = projected.astype(BF16)
    for i in range(send_ref.shape[0]):
        send_ref[i] = projected


def pair_kernel(all_ref, weight_ref, out_ref, columns_here):
    seq, col = lax.axis_index("seq"), lax.axis_index("col")
    blocks, each, _ = all_ref.shape
    features = weight_ref.shape[0]
    span = blocks // lax.axis_size("col")
    rows_here = all_ref[seq].astype(F32)[:, :features]
    for j in range(span):
        columns_here[j * each:(j + 1) * each] = all_ref[col * span + j].astype(F32)[:, features:]
    hidden = gelu(rows_here[:, None, :] + columns_here[...][None, :, :])
    r, c, f = hidden.shape
    out_ref[...] = dot_nn(hidden.reshape(r * c, f).astype(BF16), weight_ref[...]).reshape(r, c, f).astype(BF16)


def pooling_matrices(positions, taps):
    tokens, reach = positions // POOL, taps // 2
    main = np.zeros((positions, taps, tokens), np.float32)
    halo = np.zeros((16, taps, tokens), np.float32)
    for t in range(taps):
        for i in range(tokens):
            for j in range(POOL):
                p = POOL * i + j + t - reach
                if p < 0:
                    halo[p + reach, t, i] += 1.0 / POOL
                elif p >= positions:
                    halo[reach + p - positions, t, i] += 1.0 / POOL
                else:
                    main[p, t, i] += 1.0 / POOL
    flat = lambda a: jnp.asarray(a.reshape(a.shape[0], taps * tokens), BF16)
    return flat(main), flat(halo)


def cost(flops, size):
    return pl.CostEstimate(flops=int(flops), bytes_accessed=int(size), transcendentals=0)


def on_device(signal, conv_weight, conv_gain, embed_weight, attn_gain, query_weight, keyvalue_weight,
              output_weight, rowcol_weight, pair_weight):
    col = lax.axis_index("col")
    count, cols = lax.axis_size("seq"), lax.axis_size("col")
    positions, half = signal.shape
    taps, channels, _ = conv_weight.shape
    reach = taps // 2
    tokens = positions // POOL
    width = embed_weight.shape[1] * count
    features = query_weight.shape[1] // cols
    heads = features // DK
    swap = [(i, (i + 1) % cols) for i in range(cols)]
    shape = jax.ShapeDtypeStruct

    signal_t = signal.T
    other_t = lax.ppermute(signal_t, "col", swap)
    first, last = signal[:reach], signal[positions - reach:]

    def shifted(rows, by, across):
        pairs = [
            (s * cols + c, (s + by) * cols + ((c + 1) % cols if across else c))
            for s in range(count) for c in range(cols) if 0 <= s + by < count
        ]
        return lax.ppermute(rows, ("seq", "col"), pairs)

    own_halo = jnp.concatenate([shifted(last, 1, False), shifted(first, -1, False)], axis=0)
    other_halo = jnp.concatenate([shifted(last, 1, True), shifted(first, -1, True)], axis=0)
    halo = jnp.where(
        col == 0, jnp.concatenate([own_halo, other_halo], axis=1), jnp.concatenate([other_halo, own_halo], axis=1)
    )
    halo = jnp.pad(halo, ((0, 16 - 2 * reach), (0, 0)))

    query_own = jnp.concatenate(
        [
            lax.dynamic_slice_in_dim(query_weight, col * features, features, 1),
            lax.dynamic_slice_in_dim(keyvalue_weight, col * DK, DV, 1),
        ],
        axis=1,
    )
    output_own = lax.dynamic_slice_in_dim(output_weight.T, col * heads * DV, heads * DV, 1)
    ring = planned(count, lax.axis_size("grp"))
    e, q, o = (Blocks(x, count) for x in (embed_weight.T, query_own, output_own))
    if ring:
        e.along("own", "step")
        e.across("own", "own2")
        e.along("step", "far")
        e.across("step", "step2")
        e.between("step", "cross")
        q.at["own"] = after(q.at["own"], e.at["far"])
        e.across("far", "far2")
        e.between("step2", "cross2")
        q.along("own", "step")
        q.along("step", "far")
        q.across("step", "step2")
        q.between("step", "cross")
        q.along("step2", "far2")
        q.between("step2", "cross2")
        q.across("own", "own2")
        o.at["own"] = after(o.at["own"], q.at["step2"])
        o.along("own", "step")
        o.across("own", "own2")
        o.along("step", "far")
        o.across("step", "step2")
        o.between("step", "cross")
        o.across("far", "far2")
        o.between("step2", "cross2")
        embed_blocks, query_blocks, output_blocks = e.pieces(), q.pieces(), o.pieces()
    else:
        embed_blocks, query_blocks, output_blocks = (
            [lax.all_gather(x.at["own"], "seq", axis=0, tiled=True)] for x in (e, q, o)
        )
    pieces = len(embed_blocks)
    block = width // pieces

    pool_main, pool_halo = pooling_matrices(positions, taps)
    pooled = pl.pallas_call(
        conv_kernel,
        out_shape=shape((half, tokens), BF16),
        in_specs=vspec(7) + [pl.BlockSpec(memory_space=pl.ANY)],
        out_specs=pl.BlockSpec(memory_space=VMEM),
        scratch_shapes=[
            pltpu.VMEM((channels, positions), BF16),
            pltpu.VMEM((channels, taps * tokens), BF16),
            pltpu.VMEM((taps, half, channels), BF16),
            pltpu.SemaphoreType.DMA((taps,)),
        ],
        compiler_params=params(32),
        cost_estimate=cost(2 * taps * tokens * channels * (half + positions), 2 * taps * channels * half * 2),
        name="conv",
    )(
        signal_t, other_t, halo, conv_gain.reshape(channels, 1), conv_gain.reshape(1, channels),
        pool_main, pool_halo, conv_weight.transpose(0, 2, 1),
    )

    part = pl.pallas_call(
        functools.partial(embed_kernel, pieces),
        out_shape=shape((pieces, block, tokens), BF16),
        in_specs=vspec(1 + pieces),
        out_specs=pl.BlockSpec(memory_space=VMEM),
        compiler_params=params(16),
        cost_estimate=cost(2 * tokens * half * width, 2 * half * width),
        name="embed",
    )(pooled, *embed_blocks)
    other_part = lax.ppermute(part, "col", swap)

    queries, keyvalue, embedded = pl.pallas_call(
        functools.partial(query_kernel, pieces, features),
        out_shape=(
            shape((tokens, features), BF16), shape((count, tokens, DV), BF16), shape((pieces, tokens, block), BF16)
        ),
        in_specs=vspec(3 + pieces),
        out_specs=vspec(3),
        scratch_shapes=[pltpu.VMEM((pieces, tokens, block), BF16)],
        compiler_params=params(24),
        cost_estimate=cost(2 * tokens * width * (features + DV), 2 * width * (features + DV)),
        name="query",
    )(part, other_part, attn_gain.reshape(pieces, 1, block), *query_blocks)

    gathered = lax.all_to_all(keyvalue, "seq", 0, 0).reshape(count * tokens, DV)
    gathered_other = lax.ppermute(gathered, "col", swap)

    attended = pl.pallas_call(
        attend_kernel,
        out_shape=shape((heads, tokens, DV), BF16),
        in_specs=vspec(3),
        out_specs=pl.BlockSpec(memory_space=VMEM),
        compiler_params=params(40),
        cost_estimate=cost(2 * tokens * heads * count * tokens * (DK + DV), 4 * count * tokens * DV),
        name="attend",
    )(queries, gathered, gathered_other)

    part_out = pl.pallas_call(
        functools.partial(output_kernel, pieces),
        out_shape=shape((pieces, tokens, block), BF16),
        in_specs=vspec(1 + pieces),
        out_specs=pl.BlockSpec(memory_space=VMEM),
        compiler_params=params(24),
        cost_estimate=cost(2 * tokens * heads * DV * width, 2 * heads * DV * width),
        name="output",
    )(attended, *output_blocks)
    other_out = lax.ppermute(part_out, "col", swap)

    out_width = rowcol_weight.shape[1]
    own_rows, pair_rows = tokens // cols, tokens // PAIR_POOL
    out_tokens, projected = pl.pallas_call(
        token_kernel,
        out_shape=(shape((own_rows, width), BF16), shape((count, pair_rows, out_width), BF16)),
        in_specs=vspec(4),
        out_specs=vspec(2),
        scratch_shapes=[pltpu.VMEM((pieces, tokens, block), BF16)],
        compiler_params=params(16),
        cost_estimate=cost(2 * pair_rows * width * out_width, 2 * width * out_width),
        name="tokens",
    )(embedded, part_out, other_out, rowcol_weight)
    all_projected = lax.all_to_all(projected, "seq", 0, 0)

    span = pair_rows * count // cols
    pair_features = pair_weight.shape[0]
    pair_out = pl.pallas_call(
        pair_kernel,
        out_shape=shape((pair_rows, span, pair_features), BF16),
        in_specs=vspec(2),
        out_specs=pl.BlockSpec(memory_space=VMEM),
        scratch_shapes=[pltpu.VMEM((span, pair_features), F32)],
        compiler_params=params(16),
        cost_estimate=cost(2 * pair_rows * span * pair_features**2, 2 * pair_rows * span * pair_features),
        name="pair",
    )(all_projected, pair_weight)
    return out_tokens, pair_out


def solution(mesh):
    placed = (
        P(("grp", "seq"), "col"),
        P(None, None, "col"),
        P(),
        P("col", "seq"),
        P(),
        P("seq", None),
        P("seq", None),
        P(None, "seq"),
        P(),
        P(),
    )
    return jax.shard_map(
        on_device,
        mesh=mesh,
        in_specs=placed,
        out_specs=(P(("grp", "seq", "col"), None), P(("grp", "seq"), "col", None)),
        check_vma=False,
    )
```

```python
import functools
import math

import jax
import jax.numpy as jnp
import numpy as np
from jax import lax
from jax.experimental import pallas as pl
from jax.experimental.pallas import tpu as pltpu
from jax.sharding import PartitionSpec as P

DK = 128
DV = 192
POOL = 4
PAIR_POOL = 16
EPS = 1e-06
VMEM = pltpu.VMEM
F32 = jnp.float32
BF16 = jnp.bfloat16


def gelu(x):
    c = math.sqrt(2.0 / math.pi)
    half = 0.5 * x
    return half + half * jnp.tanh(x * (c + (0.044715 * c) * (x * x)))


def dot_nt(a, b):
    return lax.dot_general(a, b, (((1,), (1,)), ((), ())), preferred_element_type=F32)


def dot_nn(a, b):
    return lax.dot_general(a, b, (((1,), (0,)), ((), ())), preferred_element_type=F32)


def params(mib, **kw):
    return pltpu.CompilerParams(vmem_limit_bytes=mib << 20, **kw)


def vspec(n):
    return [pl.BlockSpec(memory_space=VMEM)] * n


def hspec(n):
    return [pl.BlockSpec(memory_space=pltpu.HBM)] * n


def fetch(sources, held, sems):
    copies = [pltpu.make_async_copy(ref, held.at[i], sems.at[i]) for i, ref in enumerate(sources)]
    for c in copies:
        c.start()
    return copies


def slots(pieces, rows, columns):
    return [pltpu.VMEM((pieces, rows, columns), BF16), pltpu.SemaphoreType.DMA((pieces,))]


RING = (0, 1, 3, 2)


def planned(count, groups):
    return count == 2 * len(RING) and groups == 2


def pick(index, table):
    value = jnp.int32(table[0])
    for i, entry in enumerate(table[1:], 1):
        value = jnp.where(index == i, jnp.int32(entry), value)
    return value


def owners(count, groups):
    if not planned(count, groups):
        return [jnp.int32(0)]
    group, me = lax.axis_index("grp"), lax.axis_index("seq")
    side, place = me % 2, pick(me // 2, [RING.index(i) for i in range(4)])
    result = []
    for step in (0, 3 + 2 * group, 1 + 2 * group, 2):
        row = pick(lax.rem(place + step, 4), RING)
        result += [2 * row + side, 2 * row + 1 - side]
    return result


class Blocks:
    def __init__(self, own, count):
        self.count = count
        self.at = {"own": own}

    def along(self, source, target):
        pairs = []
        for group in range(2):
            for k in range(4):
                a, b = RING[k], RING[(k + 1) % 4]
                if group:
                    a, b = b, a
                pairs += [(group * self.count + 2 * a + i, group * self.count + 2 * b + i) for i in range(2)]
        self.at[target] = lax.ppermute(self.at[source], ("grp", "seq"), pairs)

    def across(self, source, target):
        self.at[target] = lax.ppermute(self.at[source], "seq", [(i, i ^ 1) for i in range(self.count)])

    def between(self, source, target):
        self.at[target] = lax.ppermute(self.at[source], "grp", [(0, 1), (1, 0)])

    def pieces(self):
        names = ("own", "own2", "step", "step2", "cross", "cross2", "far", "far2")
        return [self.at[name] for name in names]


def after(values, *done):
    return lax.optimization_barrier((values, done))[0]


def conv_kernel(own_ref, other_ref, halo_ref, gaincol_ref, gainrow_ref, pool_ref, poolhalo_ref, weight_hbm,
                out_ref, act, slabs, weights, sems):
    taps, width, channels = weights.shape
    copies = [pltpu.make_async_copy(weight_hbm.at[t], weights.at[t], sems.at[t]) for t in range(taps)]
    for c in copies:
        c.start()
    col = lax.axis_index("col")
    half, positions = own_ref.shape
    tokens = out_ref.shape[1]
    step, group = 16, 4
    halves = ((own_ref, col), (other_ref, 1 - col))
    squares = jnp.zeros((8, positions), F32)
    for ref, _ in halves:

        def add(j, squares, ref=ref):
            for i in range(group):
                x = ref[pl.ds(pl.multiple_of((j * group + i) * step, step), step), :].astype(F32)
                x = x * x
                squares = squares + (x[:8] + x[8:])
            return squares

        squares = lax.fori_loop(0, half // (step * group), add, squares)
    scale = lax.rsqrt(jnp.sum(squares, axis=0, keepdims=True) / channels + EPS)
    for ref, index in halves:

        def activate(j, carry, ref=ref, index=index):
            for i in range(group):
                at = pl.multiple_of((j * group + i) * step, step)
                x = ref[pl.ds(at, step), :].astype(F32) * scale
                at = pl.multiple_of(index * half + at, step)
                act[pl.ds(at, step), :] = gelu(x * gaincol_ref[pl.ds(at, step), :]).astype(BF16)
            return carry

        lax.fori_loop(0, half // (step * group), activate, 0)
    h = halo_ref[...].astype(F32)
    h = h * lax.rsqrt(jnp.sum(h * h, axis=1, keepdims=True) / channels + EPS) * gainrow_ref[...]
    h = gelu(h)
    edges = lax.dot_general(h.astype(BF16), poolhalo_ref[...], (((0,), (0,)), ((), ())), preferred_element_type=F32)
    slabs[...] = (dot_nn(act[...], pool_ref[...]) + edges).astype(BF16)
    middle = (taps // 2) * tokens
    total = dot_nn(own_ref[...], pool_ref[:, middle:middle + tokens])
    for t in range(taps):
        copies[t].wait()
        total = total + dot_nn(weights[t], slabs[:, t * tokens:(t + 1) * tokens])
    out_ref[...] = total.astype(BF16)


def block_owners():
    return owners(lax.axis_size("seq"), lax.axis_size("grp"))


def embed_kernel(pieces, pooled_ref, *refs):
    blocks, (out_ref, held, sems) = refs[:pieces], refs[pieces:]
    half, lanes = pooled_ref.shape[0], held.shape[2]
    copies = fetch([ref.at[:, pl.ds(0, lanes)] for ref in blocks], held, sems)
    for i, owner in enumerate(block_owners()):
        copies[i].wait()
        out_ref[owner] = dot_nn(held[i][:, :half], pooled_ref[...]).astype(BF16)


def keyvalue_kernel(pieces, half, part_ref, other_ref, gain_ref, *refs):
    blocks, (kv_ref, normed_ref, embedded_ref, held, sems) = refs[:pieces], refs[pieces:]
    lanes = held.shape[2]
    start = blocks[0].shape[1] - lanes
    copies = fetch([ref.at[:, pl.ds(start, lanes)] for ref in blocks], held, sems)
    count, width, _ = part_ref.shape
    squares = 0.0
    for s in range(count):
        e = (part_ref[s].astype(F32) + other_ref[s].astype(F32)).astype(BF16).astype(F32)
        squares = squares + jnp.sum(e * e, axis=0, keepdims=True)
    scale = lax.rsqrt(squares / (count * width) + EPS)
    for s in range(count):
        e = (part_ref[s].astype(F32) + other_ref[s].astype(F32)).astype(BF16).astype(F32)
        embedded_ref[s] = e.T.astype(BF16)
        normed_ref[s] = ((e * scale).T * gain_ref[s]).astype(BF16)
    total = 0.0
    for i, owner in enumerate(block_owners()):
        copies[i].wait()
        total = total + dot_nn(normed_ref[owner], held[i][:, half - start:])
    kv_ref[...] = total.T.astype(BF16)


def query_kernel(pieces, normed_ref, *refs):
    blocks, (query_ref, held, sems) = refs[:pieces], refs[pieces:]
    copies = fetch(blocks, held, sems)
    total = 0.0
    for i, owner in enumerate(block_owners()):
        copies[i].wait()
        total = total + dot_nn(normed_ref[owner], held[i])
    query_ref[...] = (total * DK ** (-0.5)).astype(BF16)


def attend_kernel(query_ref, own_ref, other_ref, out_ref, keys, values):
    tokens, features = query_ref.shape
    blocks, _, each = own_ref.shape
    first = lax.axis_index("col") == 0
    for i in range(blocks):
        keys[:, i * each:(i + 1) * each] = jnp.where(first, own_ref[i][:DK], other_ref[i][:DK])
        values[:, i * each:(i + 1) * each] = jnp.where(first, other_ref[i], own_ref[i])
    for h in range(features // DK):
        scores = dot_nn(query_ref[:, h * DK:(h + 1) * DK], keys[...])
        weights = jnp.exp(scores - jnp.max(scores, axis=1, keepdims=True))
        total = jnp.sum(weights, axis=1, keepdims=True)
        out_ref[h] = (dot_nt(weights.astype(BF16), values[...]) / total).astype(BF16)


def output_kernel(pieces, attended_ref, *refs):
    blocks, (out_ref, held, sems) = refs[:pieces], refs[pieces:]
    copies = fetch(blocks, held, sems)
    heads = attended_ref.shape[0]
    flat = jnp.concatenate([attended_ref[h] for h in range(heads)], axis=1)
    for i, owner in enumerate(block_owners()):
        copies[i].wait()
        out_ref[owner] = dot_nt(flat, held[i]).astype(BF16)


def token_kernel(embedded_ref, part_ref, other_ref, weight_ref, token_ref, send_ref, whole):
    col = lax.axis_index("col")
    count, rows, width = part_ref.shape
    projected = None
    for s in range(count):
        tokens = (embedded_ref[s].astype(F32) + (part_ref[s].astype(F32) + other_ref[s].astype(F32))).astype(BF16)
        whole[s] = tokens
        pooled = jnp.mean(tokens.astype(F32).reshape(rows // PAIR_POOL, PAIR_POOL, width), axis=1).astype(BF16)
        part = dot_nn(pooled, weight_ref[s * width:(s + 1) * width])
        projected = part if projected is None else projected + part
    own = token_ref.shape[0]
    mine = pl.ds(pl.multiple_of(col * own, own), own)
    token_ref[...] = jnp.concatenate([whole[s, mine] for s in range(count)], axis=1)
    send_ref[...] = projected.astype(BF16)


def pair_kernel(own_ref, weight_ref, *refs):
    arrived, (out_ref, columns_here) = refs[:-2], refs[-2:]
    seq, col = lax.axis_index("seq"), lax.axis_index("col")
    features, each = weight_ref.shape[0], own_ref.shape[0]
    span = columns_here.shape[0] // each
    for j in range(span):
        if len(arrived) == 1:
            rows, at = arrived[0][col * span + j], j
        else:
            rows, at = arrived[j][...], j ^ (seq % span)
        columns_here[pl.ds(pl.multiple_of(at * each, each), each)] = rows.astype(F32)[:, features:]
    rows_here = own_ref[...].astype(F32)[:, :features]
    hidden = gelu(rows_here[:, None, :] + columns_here[...][None, :, :])
    r, c, f = hidden.shape
    out_ref[...] = dot_nn(hidden.reshape(r * c, f).astype(BF16), weight_ref[...]).reshape(r, c, f).astype(BF16)


def pooling_matrices(positions, taps):
    tokens, reach = positions // POOL, taps // 2
    main = np.zeros((positions, taps, tokens), np.float32)
    halo = np.zeros((16, taps, tokens), np.float32)
    for t in range(taps):
        for i in range(tokens):
            for j in range(POOL):
                p = POOL * i + j + t - reach
                if p < 0:
                    halo[p + reach, t, i] += 1.0 / POOL
                elif p >= positions:
                    halo[reach + p - positions, t, i] += 1.0 / POOL
                else:
                    main[p, t, i] += 1.0 / POOL
    flat = lambda a: jnp.asarray(a.reshape(a.shape[0], taps * tokens), BF16)
    return flat(main), flat(halo)


def cost(flops, size):
    return pl.CostEstimate(flops=int(flops), bytes_accessed=int(size), transcendentals=0)


def on_device(signal, conv_weight, conv_gain, embed_weight, attn_gain, query_weight, keyvalue_weight,
              output_weight, rowcol_weight, pair_weight):
    col = lax.axis_index("col")
    count, cols = lax.axis_size("seq"), lax.axis_size("col")
    positions, half = signal.shape
    taps, channels, _ = conv_weight.shape
    reach = taps // 2
    tokens = positions // POOL
    width = embed_weight.shape[1] * count
    features = query_weight.shape[1] // cols
    heads = features // DK
    swap = [(i, (i + 1) % cols) for i in range(cols)]
    shape = jax.ShapeDtypeStruct

    signal_t = signal.T
    up = [(i, i + 1) for i in range(count - 1)]
    before = lax.ppermute(signal[positions - reach:], "seq", up)
    behind = lax.ppermute(signal[:reach], "seq", [(j, i) for i, j in up])
    other_t = lax.ppermute(signal_t, "col", swap)
    own_halo = jnp.pad(jnp.concatenate([before, behind], axis=0), ((0, 16 - 2 * reach), (0, 0)))
    other_halo = lax.ppermute(own_halo, "col", swap)
    halo = jnp.where(
        col == 0, jnp.concatenate([own_halo, other_halo], axis=1), jnp.concatenate([other_halo, own_halo], axis=1)
    )

    embed_own = jnp.concatenate(
        [embed_weight.T, lax.dynamic_slice_in_dim(keyvalue_weight, col * DK, DV, 1)], axis=1
    )
    query_own = lax.dynamic_slice_in_dim(query_weight, col * features, features, 1)
    output_own = lax.dynamic_slice_in_dim(output_weight.T, col * heads * DV, heads * DV, 1)
    ring = planned(count, lax.axis_size("grp")) and cols == 2
    e, q, o = (Blocks(x, count) for x in (embed_own, query_own, output_own))
    if ring:
        e.at["own"] = after(e.at["own"], before, behind)
        e.along("own", "step")
        e.across("own", "own2")
        e.at["step"] = after(e.at["step"], e.at["own2"])
        e.along("step", "far")
        e.across("step", "step2")
        e.between("step", "cross")
        q.at["own"] = after(q.at["own"], e.at["far"])
        e.across("far", "far2")
        e.between("step2", "cross2")
        q.along("own", "step")
        q.along("step", "far")
        q.at["step"] = after(q.at["step"], e.at["far2"])
        q.across("step", "step2")
        q.between("step", "cross")
        q.along("step2", "far2")
        q.between("step2", "cross2")
        q.at["own"] = after(q.at["own"], q.at["step2"])
        q.across("own", "own2")
        o.at["own"] = after(o.at["own"], q.at["step2"], q.at["far"])
        o.along("own", "step")
        o.across("own", "own2")
        o.along("step", "far")
        o.across("step", "step2")
        o.between("step", "cross")
        o.across("far", "far2")
        o.between("step2", "cross2")
        embed_blocks, query_blocks, output_blocks = e.pieces(), q.pieces(), o.pieces()
    else:
        embed_blocks, query_blocks, output_blocks = (
            [lax.all_gather(x.at["own"], "seq", axis=0, tiled=True)] for x in (e, q, o)
        )
    pieces = len(embed_blocks)
    block = width // pieces

    pool_main, pool_halo = pooling_matrices(positions, taps)
    pooled = pl.pallas_call(
        conv_kernel,
        out_shape=shape((half, tokens), BF16),
        in_specs=vspec(7) + hspec(1),
        out_specs=pl.BlockSpec(memory_space=VMEM),
        scratch_shapes=[
            pltpu.VMEM((channels, positions), BF16),
            pltpu.VMEM((channels, taps * tokens), BF16),
            pltpu.VMEM((taps, half, channels), BF16),
            pltpu.SemaphoreType.DMA((taps,)),
        ],
        compiler_params=params(28),
        cost_estimate=cost(2 * taps * tokens * channels * (half + positions), 2 * taps * channels * half * 2),
        name="conv",
    )(
        signal_t, other_t, halo, conv_gain.reshape(channels, 1), conv_gain.reshape(1, channels),
        pool_main, pool_halo, conv_weight.transpose(0, 2, 1),
    )

    upper = -(-half // 128) * 128
    lower = half // 128 * 128
    part = pl.pallas_call(
        functools.partial(embed_kernel, pieces),
        out_shape=shape((pieces, block, tokens), BF16),
        in_specs=vspec(1) + hspec(pieces),
        out_specs=pl.BlockSpec(memory_space=VMEM),
        scratch_shapes=slots(pieces, block, min(upper, half + DV)),
        compiler_params=params(12),
        cost_estimate=cost(2 * tokens * half * width, 2 * half * width),
        name="embed",
    )(pooled, *embed_blocks)
    other_part = lax.ppermute(part, "col", swap)

    keyvalue, normed, embedded = pl.pallas_call(
        functools.partial(keyvalue_kernel, pieces, half),
        out_shape=(
            shape((DV, tokens), BF16), shape((pieces, tokens, block), BF16), shape((pieces, tokens, block), BF16)
        ),
        in_specs=vspec(3) + hspec(pieces),
        out_specs=vspec(3),
        scratch_shapes=slots(pieces, block, half + DV - lower),
        compiler_params=params(12),
        cost_estimate=cost(2 * tokens * width * DV, 2 * width * DV),
        name="keyvalue",
    )(part, other_part, attn_gain.reshape(pieces, 1, block), *embed_blocks)

    if ring:
        arrived = [keyvalue]
        for k in range(1, count // 2):
            arrived.append(lax.ppermute(keyvalue, "seq", [(i, i ^ (2 * k)) for i in range(count)]))
        arrived += [lax.ppermute(x, "seq", [(i, i ^ 1) for i in range(count)]) for x in arrived]
        gathered = jnp.stack(arrived)
    else:
        gathered = lax.all_gather(keyvalue, "seq", axis=0)
    gathered_other = lax.ppermute(gathered, "col", swap)

    queries = pl.pallas_call(
        functools.partial(query_kernel, pieces),
        out_shape=shape((tokens, features), BF16),
        in_specs=vspec(1) + hspec(pieces),
        out_specs=pl.BlockSpec(memory_space=VMEM),
        scratch_shapes=slots(pieces, block, features),
        compiler_params=params(12),
        cost_estimate=cost(2 * tokens * width * features, 2 * width * features),
        name="query",
    )(normed, *query_blocks)
    if ring:
        queries = after(queries, o.at["step"], o.at["own2"])

    attended = pl.pallas_call(
        attend_kernel,
        out_shape=shape((heads, tokens, DV), BF16),
        in_specs=vspec(3),
        out_specs=pl.BlockSpec(memory_space=VMEM),
        scratch_shapes=[pltpu.VMEM((DK, count * tokens), BF16), pltpu.VMEM((DV, count * tokens), BF16)],
        compiler_params=params(40),
        cost_estimate=cost(2 * tokens * heads * count * tokens * (DK + DV), 4 * count * tokens * DV),
        name="attend",
    )(queries, gathered, gathered_other)

    part_out = pl.pallas_call(
        functools.partial(output_kernel, pieces),
        out_shape=shape((pieces, tokens, block), BF16),
        in_specs=vspec(1) + hspec(pieces),
        out_specs=pl.BlockSpec(memory_space=VMEM),
        scratch_shapes=slots(pieces, block, heads * DV),
        compiler_params=params(16),
        cost_estimate=cost(2 * tokens * heads * DV * width, 2 * heads * DV * width),
        name="output",
    )(attended, *output_blocks)
    other_out = lax.ppermute(part_out, "col", swap)

    out_width = rowcol_weight.shape[1]
    own_rows, pair_rows = tokens // cols, tokens // PAIR_POOL
    out_tokens, projected = pl.pallas_call(
        token_kernel,
        out_shape=(shape((own_rows, width), BF16), shape((pair_rows, out_width), BF16)),
        in_specs=vspec(4),
        out_specs=vspec(2),
        scratch_shapes=[pltpu.VMEM((pieces, tokens, block), BF16)],
        compiler_params=params(12),
        cost_estimate=cost(2 * pair_rows * width * out_width, 2 * width * out_width),
        name="tokens",
    )(embedded, part_out, other_out, rowcol_weight)

    if ring:
        columns = []
        for turn in range(count // 2):
            pairs = []
            for source in range(count):
                need, i = source // (count // 2), source % (count // 2)
                for c in range(2):
                    pairs.append((source * 2 + c, ((i ^ turn) + c * (count // 2)) * 2 + need))
            columns.append(lax.ppermute(projected, ("seq", "col"), pairs))
    else:
        columns = [lax.all_gather(projected, "seq", axis=0)]

    span = pair_rows * count // cols
    pair_features = pair_weight.shape[0]
    pair_out = pl.pallas_call(
        pair_kernel,
        out_shape=shape((pair_rows, span, pair_features), BF16),
        in_specs=vspec(2 + len(columns)),
        out_specs=pl.BlockSpec(memory_space=VMEM),
        scratch_shapes=[pltpu.VMEM((span, pair_features), F32)],
        compiler_params=params(16),
        cost_estimate=cost(2 * pair_rows * span * pair_features**2, 2 * pair_rows * span * pair_features),
        name="pair",
    )(projected, pair_weight, *columns)
    return out_tokens, pair_out


def solution(mesh):
    placed = (
        P(("grp", "seq"), "col"),
        P(None, None, "col"),
        P(),
        P("col", "seq"),
        P(),
        P("seq", None),
        P("seq", None),
        P(None, "seq"),
        P(),
        P(),
    )
    return jax.shard_map(
        on_device,
        mesh=mesh,
        in_specs=placed,
        out_specs=(P(("grp", "seq", "col"), None), P(("grp", "seq"), "col", None)),
        check_vma=False,
    )
```

```python
import functools
import math

import jax
import jax.numpy as jnp
import numpy as np
from jax import lax
from jax.experimental import pallas as pl
from jax.experimental.pallas import tpu as pltpu
from jax.sharding import PartitionSpec as P

DK = 128
DV = 192
POOL = 4
PAIR_POOL = 16
EPS = 1e-06
VMEM = pltpu.VMEM
F32 = jnp.float32
BF16 = jnp.bfloat16


def gelu(x):
    c = math.sqrt(2.0 / math.pi)
    half = 0.5 * x
    return half + half * jnp.tanh(x * (c + (0.044715 * c) * (x * x)))


def dot_nt(a, b):
    return lax.dot_general(a, b, (((1,), (1,)), ((), ())), preferred_element_type=F32)


def dot_nn(a, b):
    return lax.dot_general(a, b, (((1,), (0,)), ((), ())), preferred_element_type=F32)


def params(mib, **kw):
    return pltpu.CompilerParams(vmem_limit_bytes=mib << 20, **kw)


def vspec(n):
    return [pl.BlockSpec(memory_space=VMEM)] * n


def hspec(n):
    return [pl.BlockSpec(memory_space=pltpu.HBM)] * n


RING = (0, 1, 3, 2)


def planned(count, groups):
    return count == 2 * len(RING) and groups == 2


def pick(index, table):
    value = jnp.int32(table[0])
    for i, entry in enumerate(table[1:], 1):
        value = jnp.where(index == i, jnp.int32(entry), value)
    return value


def owners(count, groups):
    if not planned(count, groups):
        return [jnp.int32(0)]
    group, me = lax.axis_index("grp"), lax.axis_index("seq")
    side, place = me % 2, pick(me // 2, [RING.index(i) for i in range(4)])
    result = []
    for step in (0, 3 + 2 * group, 1 + 2 * group, 2):
        row = pick(lax.rem(place + step, 4), RING)
        result += [2 * row + side, 2 * row + 1 - side]
    return result


class Blocks:
    def __init__(self, own, count):
        self.count = count
        self.at = {"own": own}

    def along(self, source, target):
        pairs = []
        for group in range(2):
            for k in range(4):
                a, b = RING[k], RING[(k + 1) % 4]
                if group:
                    a, b = b, a
                pairs += [(group * self.count + 2 * a + i, group * self.count + 2 * b + i) for i in range(2)]
        self.at[target] = lax.ppermute(self.at[source], ("grp", "seq"), pairs)

    def across(self, source, target):
        self.at[target] = lax.ppermute(self.at[source], "seq", [(i, i ^ 1) for i in range(self.count)])

    def between(self, source, target):
        self.at[target] = lax.ppermute(self.at[source], "grp", [(0, 1), (1, 0)])

    def pieces(self):
        names = ("own", "own2", "step", "step2", "cross", "cross2", "far", "far2")
        return [self.at[name] for name in names]


def after(values, *done):
    return lax.optimization_barrier((values, done))[0]


def act_kernel(own_ref, other_ref, halo_ref, gaincol_ref, gainrow_ref, pool_ref, poolhalo_ref, out_ref, act):
    channels, positions = act.shape
    half = own_ref.shape[0]
    col = lax.axis_index("col")
    step = 64
    halves = ((own_ref, col), (other_ref, 1 - col))
    squares = jnp.zeros((8, positions), F32)
    for ref, _ in halves:
        for j in range(half // step):
            x = ref[j * step:(j + 1) * step, :].astype(F32)
            x = x * x
            for i in range(step // 8):
                squares = squares + x[i * 8:(i + 1) * 8]
    scale = lax.rsqrt(jnp.sum(squares, axis=0, keepdims=True) / channels + EPS)
    for ref, index in halves:
        for j in range(half // step):
            at = pl.multiple_of(index * half + j * step, step)
            x = ref[j * step:(j + 1) * step, :].astype(F32) * scale
            act[pl.ds(at, step), :] = gelu(x * gaincol_ref[pl.ds(at, step), :]).astype(BF16)
    h = halo_ref[...].astype(F32)
    h = h * lax.rsqrt(jnp.sum(h * h, axis=1, keepdims=True) / channels + EPS) * gainrow_ref[...]
    h = gelu(h).astype(BF16)
    out_ref[...] = (dot_nt(pool_ref[...], act[...]) + dot_nn(poolhalo_ref[...], h)).astype(BF16)


def conv_kernel(windows_ref, own_ref, pool_ref, weight_hbm, out_ref, weights, sems):
    taps = weights.shape[0]
    copies = [pltpu.make_async_copy(weight_hbm.at[t], weights.at[t], sems.at[t]) for t in range(taps)]
    for c in copies:
        c.start()
    tokens = out_ref.shape[0]
    middle = (taps // 2) * tokens
    total = dot_nt(pool_ref[middle:middle + tokens], own_ref[...])
    for t in range(taps):
        copies[t].wait()
        total = total + dot_nt(windows_ref[t * tokens:(t + 1) * tokens], weights[t])
    out_ref[...] = total.astype(BF16)


def block_owners():
    return owners(lax.axis_size("seq"), lax.axis_size("grp"))


def embed_kernel(pieces, pooled_ref, *refs):
    blocks, out_ref = refs[:pieces], refs[pieces]
    half = pooled_ref.shape[1]
    for ref, owner in zip(blocks, block_owners()):
        out_ref[owner] = dot_nt(pooled_ref[...], ref[:, :half]).astype(BF16)


def keyvalue_kernel(pieces, half, part_ref, other_ref, gain_ref, *refs):
    blocks, (kv_ref, normed_ref, embedded_ref) = refs[:pieces], refs[pieces:]
    count, _, width = part_ref.shape
    e = (part_ref[...].astype(F32) + other_ref[...].astype(F32)).astype(BF16)
    embedded_ref[...] = e
    e = e.astype(F32)
    squares = jnp.sum(jnp.sum(e * e, axis=0), axis=1, keepdims=True)
    scale = lax.rsqrt(squares / (count * width) + EPS)
    normed_ref[...] = (e * scale[None] * gain_ref[...]).astype(BF16)
    total = 0.0
    for ref, owner in zip(blocks, block_owners()):
        total = total + dot_nn(normed_ref[owner], ref[:, half:])
    kv = total.T.astype(BF16)
    for i in range(kv_ref.shape[0]):
        kv_ref[i] = kv


def query_kernel(pieces, normed_ref, *refs):
    blocks, query_ref = refs[:pieces], refs[pieces]
    total = 0.0
    for ref, owner in zip(blocks, block_owners()):
        total = total + dot_nn(normed_ref[owner], ref[...])
    query_ref[...] = (total * DK ** (-0.5)).astype(BF16)


def attend_kernel(query_ref, own_ref, other_ref, out_ref, keys, values):
    tokens, features = query_ref.shape
    blocks, _, each = own_ref.shape
    first = lax.axis_index("col") == 0
    for i in range(blocks):
        keys[:, i * each:(i + 1) * each] = jnp.where(first, own_ref[i][:DK], other_ref[i][:DK])
        values[:, i * each:(i + 1) * each] = jnp.where(first, other_ref[i], own_ref[i])
    for h in range(features // DK):
        scores = dot_nn(query_ref[:, h * DK:(h + 1) * DK], keys[...])
        weights = jnp.exp(scores - jnp.max(scores, axis=1, keepdims=True))
        total = jnp.sum(weights, axis=1, keepdims=True)
        out_ref[h] = (dot_nt(weights.astype(BF16), values[...]) / total).astype(BF16)


def output_kernel(pieces, attended_ref, *refs):
    blocks, out_ref = refs[:pieces], refs[pieces]
    heads = attended_ref.shape[0]
    flat = jnp.concatenate([attended_ref[h] for h in range(heads)], axis=1)
    for ref, owner in zip(blocks, block_owners()):
        out_ref[owner] = dot_nt(flat, ref[...]).astype(BF16)


def token_kernel(embedded_ref, part_ref, other_ref, weight_ref, token_ref, send_ref, whole):
    col = lax.axis_index("col")
    count, rows, width = part_ref.shape
    projected = None
    for s in range(count):
        tokens = (embedded_ref[s].astype(F32) + (part_ref[s].astype(F32) + other_ref[s].astype(F32))).astype(BF16)
        whole[s] = tokens
        pooled = jnp.mean(tokens.astype(F32).reshape(rows // PAIR_POOL, PAIR_POOL, width), axis=1).astype(BF16)
        part = dot_nn(pooled, weight_ref[s * width:(s + 1) * width])
        projected = part if projected is None else projected + part
    own = token_ref.shape[0]
    mine = pl.ds(pl.multiple_of(col * own, own), own)
    token_ref[...] = jnp.concatenate([whole[s, mine] for s in range(count)], axis=1)
    send_ref[...] = projected.astype(BF16)


def pair_kernel(own_ref, weight_ref, *refs):
    arrived, (out_ref, columns_here) = refs[:-2], refs[-2:]
    seq, col = lax.axis_index("seq"), lax.axis_index("col")
    features, each = weight_ref.shape[0], own_ref.shape[0]
    span = columns_here.shape[0] // each
    for j in range(span):
        if len(arrived) == 1:
            rows, at = arrived[0][col * span + j], j
        else:
            rows, at = arrived[j][...], j ^ (seq % span)
        columns_here[pl.ds(pl.multiple_of(at * each, each), each)] = rows.astype(F32)[:, features:]
    rows_here = own_ref[...].astype(F32)[:, :features]
    hidden = gelu(rows_here[:, None, :] + columns_here[...][None, :, :])
    r, c, f = hidden.shape
    out_ref[...] = dot_nn(hidden.reshape(r * c, f).astype(BF16), weight_ref[...]).reshape(r, c, f).astype(BF16)


def pooling_matrices(positions, taps):
    tokens, reach = positions // POOL, taps // 2
    main = np.zeros((taps, tokens, positions), np.float32)
    halo = np.zeros((taps, tokens, 16), np.float32)
    for t in range(taps):
        for i in range(tokens):
            for j in range(POOL):
                p = POOL * i + j + t - reach
                if p < 0:
                    halo[t, i, p + reach] += 1.0 / POOL
                elif p >= positions:
                    halo[t, i, reach + p - positions] += 1.0 / POOL
                else:
                    main[t, i, p] += 1.0 / POOL
    flat = lambda a: jnp.asarray(a.reshape(taps * tokens, -1), BF16)
    return flat(main), flat(halo)


def cost(flops, size):
    return pl.CostEstimate(flops=int(flops), bytes_accessed=int(size), transcendentals=0)


def on_device(signal, conv_weight, conv_gain, embed_weight, attn_gain, query_weight, keyvalue_weight,
              output_weight, rowcol_weight, pair_weight):
    col = lax.axis_index("col")
    count, cols = lax.axis_size("seq"), lax.axis_size("col")
    positions, half = signal.shape
    taps, channels, _ = conv_weight.shape
    reach = taps // 2
    tokens = positions // POOL
    width = embed_weight.shape[1] * count
    features = query_weight.shape[1] // cols
    heads = features // DK
    swap = [(i, (i + 1) % cols) for i in range(cols)]
    shape = jax.ShapeDtypeStruct

    signal_t = signal.T
    up = [(i, i + 1) for i in range(count - 1)]
    before = lax.ppermute(signal[positions - reach:], "seq", up)
    behind = lax.ppermute(signal[:reach], "seq", [(j, i) for i, j in up])
    other_t = lax.ppermute(signal_t, "col", swap)
    own_halo = jnp.pad(jnp.concatenate([before, behind], axis=0), ((0, 16 - 2 * reach), (0, 0)))
    other_halo = lax.ppermute(own_halo, "col", swap)
    halo = jnp.where(
        col == 0, jnp.concatenate([own_halo, other_halo], axis=1), jnp.concatenate([other_halo, own_halo], axis=1)
    )

    embed_own = jnp.concatenate(
        [embed_weight.T, lax.dynamic_slice_in_dim(keyvalue_weight, col * DK, DV, 1)], axis=1
    )
    query_own = lax.dynamic_slice_in_dim(query_weight, col * features, features, 1)
    output_own = lax.dynamic_slice_in_dim(output_weight.T, col * heads * DV, heads * DV, 1)
    ring = planned(count, lax.axis_size("grp")) and cols == 2
    e, q, o = (Blocks(x, count) for x in (embed_own, query_own, output_own))
    pool_main, pool_halo = pooling_matrices(positions, taps)
    if ring:
        e.at["own"] = after(e.at["own"], before, behind)
        e.along("own", "step")
        e.across("own", "own2")
    windows = pl.pallas_call(
        act_kernel,
        out_shape=shape((taps * tokens, channels), BF16),
        in_specs=vspec(7),
        out_specs=pl.BlockSpec(memory_space=VMEM),
        scratch_shapes=[pltpu.VMEM((channels, positions), BF16)],
        compiler_params=params(24),
        cost_estimate=cost(2 * taps * tokens * channels * positions, 4 * channels * positions),
        name="act",
    )(
        signal_t, other_t, halo, conv_gain.reshape(channels, 1), conv_gain.reshape(1, channels), pool_main, pool_halo
    )
    if ring:
        e.at["step"] = after(e.at["step"], e.at["own2"], windows)
        e.along("step", "far")
        e.across("step", "step2")
        e.between("step", "cross")
    pooled = pl.pallas_call(
        conv_kernel,
        out_shape=shape((tokens, half), BF16),
        in_specs=vspec(3) + hspec(1),
        out_specs=pl.BlockSpec(memory_space=VMEM),
        scratch_shapes=[pltpu.VMEM((taps, half, channels), BF16), pltpu.SemaphoreType.DMA((taps,))],
        compiler_params=params(56),
        cost_estimate=cost(2 * taps * tokens * channels * half, 2 * taps * channels * half),
        name="conv",
    )(windows, signal_t, pool_main, conv_weight.transpose(0, 2, 1))
    if ring:
        e.at["far"] = after(e.at["far"], pooled)
        e.at["step2"] = after(e.at["step2"], pooled)
        e.across("far", "far2")
        e.between("step2", "cross2")
        q.at["own"] = after(q.at["own"], pooled, e.at["far"])
        q.along("own", "step")
        q.at["step"] = after(q.at["step"], e.at["far2"], e.at["cross2"])
        q.along("step", "far")
        q.across("step", "step2")
        q.between("step", "cross")
        q.at["own"] = after(q.at["own"], q.at["step2"])
        q.along("step2", "far2")
        q.across("own", "own2")
        q.between("step2", "cross2")
        o.at["own"] = after(o.at["own"], q.at["step2"], q.at["far"])
        o.along("own", "step")
        o.across("own", "own2")
        o.along("step", "far")
        o.across("step", "step2")
        o.between("step", "cross")
        o.across("far", "far2")
        o.between("step2", "cross2")
        embed_blocks, query_blocks, output_blocks = e.pieces(), q.pieces(), o.pieces()
    else:
        embed_blocks, query_blocks, output_blocks = (
            [lax.all_gather(x.at["own"], "seq", axis=0, tiled=True)] for x in (e, q, o)
        )
    pieces = len(embed_blocks)
    block = width // pieces

    part = pl.pallas_call(
        functools.partial(embed_kernel, pieces),
        out_shape=shape((pieces, tokens, block), BF16),
        in_specs=vspec(1 + pieces),
        out_specs=pl.BlockSpec(memory_space=VMEM),
        compiler_params=params(12),
        cost_estimate=cost(2 * tokens * half * width, 2 * half * width),
        name="embed",
    )(pooled, *embed_blocks)
    other_part = lax.ppermute(part, "col", swap)
    if ring:
        other_part = after(other_part, q.at["step2"], q.at["far"])

    keyvalue, normed, embedded = pl.pallas_call(
        functools.partial(keyvalue_kernel, pieces, half),
        out_shape=(
            shape((count, DV, tokens), BF16),
            shape((pieces, tokens, block), BF16),
            shape((pieces, tokens, block), BF16),
        ),
        in_specs=vspec(3 + pieces),
        out_specs=vspec(3),
        compiler_params=params(16),
        cost_estimate=cost(2 * tokens * width * DV, 2 * width * DV),
        name="keyvalue",
    )(part, other_part, attn_gain.reshape(pieces, 1, block), *embed_blocks)
    gathered = lax.all_to_all(keyvalue, "seq", 0, 0)
    gathered_other = lax.ppermute(gathered, "col", swap)

    queries = pl.pallas_call(
        functools.partial(query_kernel, pieces),
        out_shape=shape((tokens, features), BF16),
        in_specs=vspec(1 + pieces),
        out_specs=pl.BlockSpec(memory_space=VMEM),
        compiler_params=params(12),
        cost_estimate=cost(2 * tokens * width * features, 2 * width * features),
        name="query",
    )(normed, *query_blocks)
    if ring:
        queries = after(queries, o.at["step"], o.at["own2"])

    attended = pl.pallas_call(
        attend_kernel,
        out_shape=shape((heads, tokens, DV), BF16),
        in_specs=vspec(3),
        out_specs=pl.BlockSpec(memory_space=VMEM),
        scratch_shapes=[pltpu.VMEM((DK, count * tokens), BF16), pltpu.VMEM((DV, count * tokens), BF16)],
        compiler_params=params(40),
        cost_estimate=cost(2 * tokens * heads * count * tokens * (DK + DV), 4 * count * tokens * DV),
        name="attend",
    )(queries, gathered, gathered_other)

    part_out = pl.pallas_call(
        functools.partial(output_kernel, pieces),
        out_shape=shape((pieces, tokens, block), BF16),
        in_specs=vspec(1 + pieces),
        out_specs=pl.BlockSpec(memory_space=VMEM),
        compiler_params=params(16),
        cost_estimate=cost(2 * tokens * heads * DV * width, 2 * heads * DV * width),
        name="output",
    )(attended, *output_blocks)
    other_out = lax.ppermute(part_out, "col", swap)

    out_width = rowcol_weight.shape[1]
    own_rows, pair_rows = tokens // cols, tokens // PAIR_POOL
    out_tokens, projected = pl.pallas_call(
        token_kernel,
        out_shape=(shape((own_rows, width), BF16), shape((pair_rows, out_width), BF16)),
        in_specs=vspec(4),
        out_specs=vspec(2),
        scratch_shapes=[pltpu.VMEM((pieces, tokens, block), BF16)],
        compiler_params=params(12),
        cost_estimate=cost(2 * pair_rows * width * out_width, 2 * width * out_width),
        name="tokens",
    )(embedded, part_out, other_out, rowcol_weight)

    if ring:
        columns = []
        for turn in range(count // 2):
            pairs = []
            for source in range(count):
                need, i = source // (count // 2), source % (count // 2)
                for c in range(2):
                    pairs.append((source * 2 + c, ((i ^ turn) + c * (count // 2)) * 2 + need))
            columns.append(lax.ppermute(projected, ("seq", "col"), pairs))
    else:
        columns = [lax.all_gather(projected, "seq", axis=0)]

    span = pair_rows * count // cols
    pair_features = pair_weight.shape[0]
    pair_out = pl.pallas_call(
        pair_kernel,
        out_shape=shape((pair_rows, span, pair_features), BF16),
        in_specs=vspec(2 + len(columns)),
        out_specs=pl.BlockSpec(memory_space=VMEM),
        scratch_shapes=[pltpu.VMEM((span, pair_features), F32)],
        compiler_params=params(16),
        cost_estimate=cost(2 * pair_rows * span * pair_features**2, 2 * pair_rows * span * pair_features),
        name="pair",
    )(projected, pair_weight, *columns)
    return out_tokens, pair_out


def solution(mesh):
    placed = (
        P(("grp", "seq"), "col"),
        P(None, None, "col"),
        P(),
        P("col", "seq"),
        P(),
        P("seq", None),
        P("seq", None),
        P(None, "seq"),
        P(),
        P(),
    )
    return jax.shard_map(
        on_device,
        mesh=mesh,
        in_specs=placed,
        out_specs=(P(("grp", "seq", "col"), None), P(("grp", "seq"), "col", None)),
        check_vma=False,
    )
```

```python
import functools
import math

import jax
import jax.numpy as jnp
from jax import lax
from jax.experimental import pallas as pl
from jax.experimental.pallas import tpu as pltpu
from jax.sharding import PartitionSpec as P

DK = 128
DV = 192
POOL = 4
PAIR_POOL = 16
EPS = 1e-06
VMEM = pltpu.VMEM
F32 = jnp.float32
BF16 = jnp.bfloat16


def gelu(x):
    c = math.sqrt(2.0 / math.pi)
    half = 0.5 * x
    return half + half * jnp.tanh(x * (c + (0.044715 * c) * (x * x)))


def dot_nt(a, b):
    return lax.dot_general(a, b, (((1,), (1,)), ((), ())), preferred_element_type=F32)


def dot_nn(a, b):
    return lax.dot_general(a, b, (((1,), (0,)), ((), ())), preferred_element_type=F32)


def params(mib, **kw):
    return pltpu.CompilerParams(vmem_limit_bytes=mib << 20, **kw)


def vspec(n):
    return [pl.BlockSpec(memory_space=VMEM)] * n


def hspec(n):
    return [pl.BlockSpec(memory_space=pltpu.HBM)] * n


RING = (0, 1, 3, 2)


def planned(count, groups):
    return count == 2 * len(RING) and groups == 2


def pick(index, table):
    value = jnp.int32(table[0])
    for i, entry in enumerate(table[1:], 1):
        value = jnp.where(index == i, jnp.int32(entry), value)
    return value


def owners(count, groups):
    if not planned(count, groups):
        return [jnp.int32(0)]
    group, me = lax.axis_index("grp"), lax.axis_index("seq")
    side, place = me % 2, pick(me // 2, [RING.index(i) for i in range(4)])
    result = []
    for step in (0, 3 + 2 * group, 1 + 2 * group, 2):
        row = pick(lax.rem(place + step, 4), RING)
        result += [2 * row + side, 2 * row + 1 - side]
    return result


class Blocks:
    def __init__(self, own, count):
        self.count = count
        self.at = {"own": own}

    def along(self, source, target):
        pairs = []
        for group in range(2):
            for k in range(4):
                a, b = RING[k], RING[(k + 1) % 4]
                if group:
                    a, b = b, a
                pairs += [(group * self.count + 2 * a + i, group * self.count + 2 * b + i) for i in range(2)]
        self.at[target] = lax.ppermute(self.at[source], ("grp", "seq"), pairs)

    def across(self, source, target):
        self.at[target] = lax.ppermute(self.at[source], "seq", [(i, i ^ 1) for i in range(self.count)])

    def between(self, source, target):
        self.at[target] = lax.ppermute(self.at[source], "grp", [(0, 1), (1, 0)])

    def pieces(self):
        names = ("own", "own2", "step", "step2", "cross", "cross2", "far", "far2")
        return [self.at[name] for name in names]


def after(values, *done):
    return lax.optimization_barrier((values, done))[0]


def window_means(first_row, rows, tokens, taps, positions, columns):
    r = lax.broadcasted_iota(jnp.int32, (rows, columns), 0) + first_row
    k = lax.broadcasted_iota(jnp.int32, (rows, columns), 1)
    reach = taps // 2
    if columns != positions:
        k = jnp.where(k < 2 * reach, jnp.where(k < reach, k - reach, k - reach + positions), -positions)
    tap = r // tokens
    gap = k - (POOL * (r - tap * tokens) + tap - reach)
    return jnp.where((gap >= 0) & (gap < POOL), 1.0 / POOL, 0.0).astype(BF16)


def act_kernel(taps, own_ref, other_ref, halo_ref, gain_ref, out_ref, act, gaincol):
    channels, positions = act.shape
    half = own_ref.shape[0]
    col = lax.axis_index("col")
    gaincol[...] = jnp.broadcast_to(gain_ref[...], (8, channels)).T
    step = 64
    halves = ((own_ref, col), (other_ref, 1 - col))
    squares = jnp.zeros((8, positions), F32)
    for ref, _ in halves:
        for j in range(half // step):
            x = ref[j * step:(j + 1) * step, :].astype(F32)
            x = x * x
            for i in range(step // 8):
                squares = squares + x[i * 8:(i + 1) * 8]
    scale = lax.rsqrt(jnp.sum(squares, axis=0, keepdims=True) / channels + EPS)
    for ref, index in halves:
        for j in range(half // step):
            at = pl.multiple_of(index * half + j * step, step)
            x = ref[j * step:(j + 1) * step, :].astype(F32) * scale
            act[pl.ds(at, step), :] = gelu(x * gaincol[pl.ds(at, step), :1]).astype(BF16)
    h = halo_ref[...].astype(F32)
    h = h * lax.rsqrt(jnp.sum(h * h, axis=1, keepdims=True) / channels + EPS) * gain_ref[...]
    h = gelu(h).astype(BF16)
    rows = out_ref.shape[0]
    shape = (0, rows, rows // taps, taps, positions)
    out_ref[...] = (
        dot_nt(window_means(*shape, positions), act[...]) + dot_nn(window_means(*shape, h.shape[0]), h)
    ).astype(BF16)


def conv_kernel(windows_ref, own_ref, weight_hbm, out_ref, weights, sems):
    taps = weights.shape[0]
    copies = [pltpu.make_async_copy(weight_hbm.at[t], weights.at[t], sems.at[t]) for t in range(taps)]
    ahead = 2
    for c in copies[:ahead]:
        c.start()
    tokens, positions = out_ref.shape[0], own_ref.shape[1]
    total = dot_nt(window_means((taps // 2) * tokens, tokens, tokens, taps, positions, positions), own_ref[...])
    for t in range(taps):
        copies[t].wait()
        if t + ahead < taps:
            copies[t + ahead].start()
        total = total + dot_nt(windows_ref[t * tokens:(t + 1) * tokens], weights[t])
    out_ref[...] = total.astype(BF16)


def block_owners():
    return owners(lax.axis_size("seq"), lax.axis_size("grp"))


def embed_kernel(pieces, pooled_ref, *refs):
    blocks, out_ref = refs[:pieces], refs[pieces]
    half = pooled_ref.shape[1]
    for ref, owner in zip(blocks, block_owners()):
        out_ref[owner] = dot_nt(pooled_ref[...], ref[:, :half]).astype(BF16)


def keyvalue_kernel(pieces, half, part_ref, other_ref, gain_ref, *refs):
    blocks, (kv_ref, normed_ref, embedded_ref) = refs[:pieces], refs[pieces:]
    count, _, width = part_ref.shape
    e = (part_ref[...].astype(F32) + other_ref[...].astype(F32)).astype(BF16)
    embedded_ref[...] = e
    e = e.astype(F32)
    squares = jnp.sum(jnp.sum(e * e, axis=0), axis=1, keepdims=True)
    scale = lax.rsqrt(squares / (count * width) + EPS)
    normed_ref[...] = (e * scale[None] * gain_ref[...]).astype(BF16)
    total = 0.0
    for ref, owner in zip(blocks, block_owners()):
        total = total + dot_nn(normed_ref[owner], ref[:, half:])
    kv = total.T.astype(BF16)
    for i in range(kv_ref.shape[0]):
        kv_ref[i] = kv


def query_kernel(pieces, normed_ref, *refs):
    blocks, query_ref = refs[:pieces], refs[pieces]
    total = 0.0
    for ref, owner in zip(blocks, block_owners()):
        total = total + dot_nn(normed_ref[owner], ref[...])
    query_ref[...] = (total * DK ** (-0.5)).astype(BF16)


def attend_kernel(query_ref, own_ref, other_ref, out_ref, keys, values):
    tokens, features = query_ref.shape
    blocks, _, each = own_ref.shape
    first = lax.axis_index("col") == 0
    for i in range(blocks):
        keys[:, i * each:(i + 1) * each] = jnp.where(first, own_ref[i][:DK], other_ref[i][:DK])
        values[:, i * each:(i + 1) * each] = jnp.where(first, other_ref[i], own_ref[i])
    for h in range(features // DK):
        scores = dot_nn(query_ref[:, h * DK:(h + 1) * DK], keys[...])
        weights = jnp.exp(scores - jnp.max(scores, axis=1, keepdims=True))
        total = jnp.sum(weights, axis=1, keepdims=True)
        out_ref[h] = (dot_nt(weights.astype(BF16), values[...]) / total).astype(BF16)


def output_kernel(attended_ref, weight_ref, out_ref):
    heads = attended_ref.shape[0]
    flat = jnp.concatenate([attended_ref[h] for h in range(heads)], axis=1)
    count, _, block = out_ref.shape
    for s in range(count):
        out_ref[s] = dot_nt(flat, weight_ref[s * block:(s + 1) * block]).astype(BF16)


def token_kernel(embedded_ref, part_ref, other_ref, weight_ref, token_ref, send_ref, whole):
    col = lax.axis_index("col")
    count, rows, width = part_ref.shape
    projected = None
    for s in range(count):
        tokens = (embedded_ref[s].astype(F32) + (part_ref[s].astype(F32) + other_ref[s].astype(F32))).astype(BF16)
        whole[s] = tokens
        pooled = jnp.mean(tokens.astype(F32).reshape(rows // PAIR_POOL, PAIR_POOL, width), axis=1).astype(BF16)
        part = dot_nn(pooled, weight_ref[s * width:(s + 1) * width])
        projected = part if projected is None else projected + part
    own = token_ref.shape[0]
    mine = pl.ds(pl.multiple_of(col * own, own), own)
    token_ref[...] = jnp.concatenate([whole[s, mine] for s in range(count)], axis=1)
    send_ref[...] = projected.astype(BF16)


def pair_kernel(own_ref, all_ref, weight_ref, out_ref, columns_here):
    seq, col = lax.axis_index("seq"), lax.axis_index("col")
    features, each = weight_ref.shape[0], own_ref.shape[0]
    span = columns_here.shape[0] // each
    rows = all_ref[...].astype(F32)[:, features:]
    if rows.shape[0] == columns_here.shape[0]:
        for j in range(span):
            at = pl.multiple_of((j ^ (seq % span)) * each, each)
            columns_here[pl.ds(at, each)] = rows[j * each:(j + 1) * each]
    else:
        half = columns_here.shape[0]
        columns_here[...] = jnp.where(col == 0, rows[:half], rows[half:])
    rows_here = own_ref[...].astype(F32)[:, :features]
    hidden = gelu(rows_here[:, None, :] + columns_here[...][None, :, :])
    r, c, f = hidden.shape
    out_ref[...] = dot_nn(hidden.reshape(r * c, f).astype(BF16), weight_ref[...]).reshape(r, c, f).astype(BF16)


def cost(flops, size):
    return pl.CostEstimate(flops=int(flops), bytes_accessed=int(size), transcendentals=0)


def on_device(signal, conv_weight, conv_gain, embed_weight, attn_gain, query_weight, keyvalue_weight,
              output_weight, rowcol_weight, pair_weight):
    col = lax.axis_index("col")
    count, cols = lax.axis_size("seq"), lax.axis_size("col")
    positions, half = signal.shape
    taps, channels, _ = conv_weight.shape
    reach = taps // 2
    tokens = positions // POOL
    width = embed_weight.shape[1] * count
    features = query_weight.shape[1] // cols
    heads = features // DK
    swap = [(i, (i + 1) % cols) for i in range(cols)]
    shape = jax.ShapeDtypeStruct

    signal_t = signal.T
    up = [(i, i + 1) for i in range(count - 1)]
    before = lax.ppermute(signal[positions - reach:], "seq", up)
    behind = lax.ppermute(signal[:reach], "seq", [(j, i) for i, j in up])
    other_t = lax.ppermute(signal_t, "col", swap)
    own_halo = jnp.pad(jnp.concatenate([before, behind], axis=0), ((0, 16 - 2 * reach), (0, 0)))
    other_halo = lax.ppermute(own_halo, "col", swap)
    halo = jnp.where(
        col == 0, jnp.concatenate([own_halo, other_halo], axis=1), jnp.concatenate([other_halo, own_halo], axis=1)
    )

    embed_own = jnp.concatenate(
        [embed_weight.T, lax.dynamic_slice_in_dim(keyvalue_weight, col * DK, DV, 1)], axis=1
    )
    query_own = lax.dynamic_slice_in_dim(query_weight, col * features, features, 1)
    output_own = lax.dynamic_slice_in_dim(output_weight.T, col * heads * DV, heads * DV, 1)
    ring = planned(count, lax.axis_size("grp")) and cols == 2
    e, q = (Blocks(x, count) for x in (embed_own, query_own))
    output_all = lax.all_gather(output_own, "seq", axis=0, tiled=True)
    if ring:
        e.at["own"] = after(e.at["own"], before, behind)
        e.along("own", "step")
        e.across("own", "own2")
    windows = pl.pallas_call(
        functools.partial(act_kernel, taps),
        out_shape=shape((taps * tokens, channels), BF16),
        in_specs=vspec(4),
        out_specs=pl.BlockSpec(memory_space=VMEM),
        scratch_shapes=[pltpu.VMEM((channels, positions), BF16), pltpu.VMEM((channels, 8), F32)],
        compiler_params=params(20),
        cost_estimate=cost(2 * taps * tokens * channels * positions, 4 * channels * positions),
        name="act",
    )(signal_t, other_t, halo, conv_gain.reshape(1, channels))
    if ring:
        e.at["step"] = after(e.at["step"], e.at["own2"], windows)
        e.along("step", "far")
        e.across("step", "step2")
        e.between("step", "cross")
    pooled = pl.pallas_call(
        conv_kernel,
        out_shape=shape((tokens, half), BF16),
        in_specs=vspec(2) + hspec(1),
        out_specs=pl.BlockSpec(memory_space=VMEM),
        scratch_shapes=[pltpu.VMEM((taps, half, channels), BF16), pltpu.SemaphoreType.DMA((taps,))],
        compiler_params=params(52),
        cost_estimate=cost(2 * taps * tokens * channels * half, 2 * taps * channels * half),
        name="conv",
    )(windows, signal_t, conv_weight.transpose(0, 2, 1))
    if ring:
        e.at["far"] = after(e.at["far"], pooled)
        e.at["step2"] = after(e.at["step2"], pooled)
        e.across("far", "far2")
        e.between("step2", "cross2")
        q.at["own"] = after(q.at["own"], pooled, e.at["far"])
        q.along("own", "step")
        q.at["step"] = after(q.at["step"], e.at["far2"], e.at["cross2"])
        q.along("step", "far")
        q.across("step", "step2")
        q.between("step", "cross")
        q.at["own"] = after(q.at["own"], q.at["step2"])
        q.along("step2", "far2")
        q.across("own", "own2")
        q.between("step2", "cross2")
        embed_blocks, query_blocks = e.pieces(), q.pieces()
    else:
        embed_blocks, query_blocks = ([lax.all_gather(x.at["own"], "seq", axis=0, tiled=True)] for x in (e, q))
    pieces = len(embed_blocks)
    block = width // pieces

    part = pl.pallas_call(
        functools.partial(embed_kernel, pieces),
        out_shape=shape((pieces, tokens, block), BF16),
        in_specs=vspec(1 + pieces),
        out_specs=pl.BlockSpec(memory_space=VMEM),
        compiler_params=params(12),
        cost_estimate=cost(2 * tokens * half * width, 2 * half * width),
        name="embed",
    )(pooled, *embed_blocks)
    other_part = lax.ppermute(part, "col", swap)

    keyvalue, normed, embedded = pl.pallas_call(
        functools.partial(keyvalue_kernel, pieces, half),
        out_shape=(
            shape((count, DV, tokens), BF16),
            shape((pieces, tokens, block), BF16),
            shape((pieces, tokens, block), BF16),
        ),
        in_specs=vspec(3 + pieces),
        out_specs=vspec(3),
        compiler_params=params(16),
        cost_estimate=cost(2 * tokens * width * DV, 2 * width * DV),
        name="keyvalue",
    )(part, other_part, attn_gain.reshape(pieces, 1, block), *embed_blocks)
    gathered = lax.all_to_all(keyvalue, "seq", 0, 0)
    gathered_other = lax.ppermute(gathered, "col", swap)

    queries = pl.pallas_call(
        functools.partial(query_kernel, pieces),
        out_shape=shape((tokens, features), BF16),
        in_specs=vspec(1 + pieces),
        out_specs=pl.BlockSpec(memory_space=VMEM),
        compiler_params=params(12),
        cost_estimate=cost(2 * tokens * width * features, 2 * width * features),
        name="query",
    )(normed, *query_blocks)

    attended = pl.pallas_call(
        attend_kernel,
        out_shape=shape((heads, tokens, DV), BF16),
        in_specs=vspec(3),
        out_specs=pl.BlockSpec(memory_space=VMEM),
        scratch_shapes=[pltpu.VMEM((DK, count * tokens), BF16), pltpu.VMEM((DV, count * tokens), BF16)],
        compiler_params=params(24),
        cost_estimate=cost(2 * tokens * heads * count * tokens * (DK + DV), 4 * count * tokens * DV),
        name="attend",
    )(queries, gathered, gathered_other)

    part_out = pl.pallas_call(
        output_kernel,
        out_shape=shape((pieces, tokens, block), BF16),
        in_specs=vspec(2),
        out_specs=pl.BlockSpec(memory_space=VMEM),
        compiler_params=params(16),
        cost_estimate=cost(2 * tokens * heads * DV * width, 2 * heads * DV * width),
        name="output",
    )(attended, output_all)
    other_out = lax.ppermute(part_out, "col", swap)

    out_width = rowcol_weight.shape[1]
    own_rows, pair_rows = tokens // cols, tokens // PAIR_POOL
    out_tokens, projected = pl.pallas_call(
        token_kernel,
        out_shape=(shape((own_rows, width), BF16), shape((pair_rows, out_width), BF16)),
        in_specs=vspec(4),
        out_specs=vspec(2),
        scratch_shapes=[pltpu.VMEM((pieces, tokens, block), BF16)],
        compiler_params=params(12),
        cost_estimate=cost(2 * pair_rows * width * out_width, 2 * width * out_width),
        name="tokens",
    )(embedded, part_out, other_out, rowcol_weight)

    if ring:
        rows_all = projected
        for bit in (1, 2):
            rows_all = jnp.concatenate([rows_all, lax.ppermute(rows_all, "seq", [(i, i ^ bit) for i in range(count)])])
        pairs = [(i * cols + i // 4, (i ^ 4) * cols + i // 4) for i in range(count)]
        far_rows = lax.ppermute(rows_all, ("seq", "col"), pairs)
        rows_all = jnp.where(lax.axis_index("seq") // 4 == col, rows_all, far_rows)
    else:
        rows_all = lax.all_gather(projected, "seq", axis=0, tiled=True)

    span = pair_rows * count // cols
    pair_features = pair_weight.shape[0]
    pair_out = pl.pallas_call(
        pair_kernel,
        out_shape=shape((pair_rows, span, pair_features), BF16),
        in_specs=vspec(3),
        out_specs=pl.BlockSpec(memory_space=VMEM),
        scratch_shapes=[pltpu.VMEM((span, pair_features), F32)],
        compiler_params=params(16),
        cost_estimate=cost(2 * pair_rows * span * pair_features**2, 2 * pair_rows * span * pair_features),
        name="pair",
    )(projected, rows_all, pair_weight)
    return out_tokens, pair_out


def solution(mesh):
    placed = (
        P(("grp", "seq"), "col"),
        P(None, None, "col"),
        P(),
        P("col", "seq"),
        P(),
        P("seq", None),
        P("seq", None),
        P(None, "seq"),
        P(),
        P(),
    )
    return jax.shard_map(
        on_device,
        mesh=mesh,
        in_specs=placed,
        out_specs=(P(("grp", "seq", "col"), None), P(("grp", "seq"), "col", None)),
        check_vma=False,
    )
```

```python
import functools
import math

import jax
import jax.numpy as jnp
from jax import lax
from jax.experimental import pallas as pl
from jax.experimental.pallas import tpu as pltpu
from jax.sharding import PartitionSpec as P

DK = 128
DV = 192
POOL = 4
PAIR_POOL = 16
EPS = 1e-06
VMEM = pltpu.VMEM
F32 = jnp.float32
BF16 = jnp.bfloat16


def gelu(x):
    c = math.sqrt(2.0 / math.pi)
    half = 0.5 * x
    return half + half * jnp.tanh(x * (c + (0.044715 * c) * (x * x)))


def dot_nt(a, b):
    return lax.dot_general(a, b, (((1,), (1,)), ((), ())), preferred_element_type=F32)


def dot_nn(a, b):
    return lax.dot_general(a, b, (((1,), (0,)), ((), ())), preferred_element_type=F32)


def params(mib, **kw):
    return pltpu.CompilerParams(vmem_limit_bytes=mib << 20, **kw)


def vspec(n):
    return [pl.BlockSpec(memory_space=VMEM)] * n


def hspec(n):
    return [pl.BlockSpec(memory_space=pltpu.HBM)] * n


RING = (0, 1, 3, 2)


def planned(count, groups):
    return count == 2 * len(RING) and groups == 2


def pick(index, table):
    value = jnp.int32(table[0])
    for i, entry in enumerate(table[1:], 1):
        value = jnp.where(index == i, jnp.int32(entry), value)
    return value


def owners(count, groups):
    if not planned(count, groups):
        return [jnp.int32(0)]
    group, me = lax.axis_index("grp"), lax.axis_index("seq")
    side, place = me % 2, pick(me // 2, [RING.index(i) for i in range(4)])
    result = []
    for step in (0, 3 + 2 * group, 1 + 2 * group, 2):
        row = pick(lax.rem(place + step, 4), RING)
        result += [2 * row + side, 2 * row + 1 - side]
    return result


class Blocks:
    def __init__(self, own, count):
        self.count = count
        self.at = {"own": own}

    def along(self, source, target):
        pairs = []
        for group in range(2):
            for k in range(4):
                a, b = RING[k], RING[(k + 1) % 4]
                if group:
                    a, b = b, a
                pairs += [(group * self.count + 2 * a + i, group * self.count + 2 * b + i) for i in range(2)]
        self.at[target] = lax.ppermute(self.at[source], ("grp", "seq"), pairs)

    def across(self, source, target):
        self.at[target] = lax.ppermute(self.at[source], "seq", [(i, i ^ 1) for i in range(self.count)])

    def between(self, source, target):
        self.at[target] = lax.ppermute(self.at[source], "grp", [(0, 1), (1, 0)])

    def pieces(self):
        names = ("own", "own2", "step", "step2", "cross", "cross2", "far", "far2")
        return [self.at[name] for name in names]


def after(values, *done):
    return lax.optimization_barrier((values, done))[0]


def window_means(first_row, rows, tokens, taps, positions, columns):
    r = lax.broadcasted_iota(jnp.int32, (rows, columns), 0) + first_row
    k = lax.broadcasted_iota(jnp.int32, (rows, columns), 1)
    reach = taps // 2
    if columns != positions:
        k = jnp.where(k < 2 * reach, jnp.where(k < reach, k - reach, k - reach + positions), -positions)
    tap = r // tokens
    gap = k - (POOL * (r - tap * tokens) + tap - reach)
    return jnp.where((gap >= 0) & (gap < POOL), 1.0 / POOL, 0.0).astype(BF16)


def act_kernel(taps, own_ref, other_ref, gain_ref, out_ref, act, gaincol):
    channels, positions = act.shape
    half = own_ref.shape[0]
    col = lax.axis_index("col")
    gaincol[...] = jnp.broadcast_to(gain_ref[...], (8, channels)).T
    step = 64
    halves = ((own_ref, col), (other_ref, 1 - col))
    squares = jnp.zeros((8, positions), F32)
    for ref, _ in halves:
        for j in range(half // step):
            x = ref[j * step:(j + 1) * step, :].astype(F32)
            x = x * x
            for i in range(step // 8):
                squares = squares + x[i * 8:(i + 1) * 8]
    scale = lax.rsqrt(jnp.sum(squares, axis=0, keepdims=True) / channels + EPS)
    for ref, index in halves:
        for j in range(half // step):
            at = pl.multiple_of(index * half + j * step, step)
            x = ref[j * step:(j + 1) * step, :].astype(F32) * scale
            act[pl.ds(at, step), :] = gelu(x * gaincol[pl.ds(at, step), :1]).astype(BF16)
    rows = out_ref.shape[0]
    out_ref[...] = dot_nt(window_means(0, rows, rows // taps, taps, positions, positions), act[...]).astype(BF16)


def conv_kernel(windows_ref, own_ref, halo_ref, gain_ref, weight_hbm, out_ref, weights, sems):
    taps, _, channels = weights.shape
    copies = [pltpu.make_async_copy(weight_hbm.at[t], weights.at[t], sems.at[t]) for t in range(taps)]
    ahead = 2
    for c in copies[:ahead]:
        c.start()
    tokens, positions = out_ref.shape[0], own_ref.shape[1]
    h = halo_ref[...].astype(F32)
    h = h * lax.rsqrt(jnp.sum(h * h, axis=1, keepdims=True) / channels + EPS) * gain_ref[...]
    h = gelu(h).astype(BF16)
    total = dot_nt(window_means((taps // 2) * tokens, tokens, tokens, taps, positions, positions), own_ref[...])
    for t in range(taps):
        window = windows_ref[t * tokens:(t + 1) * tokens]
        if t != taps // 2:
            edges = dot_nn(window_means(t * tokens, tokens, tokens, taps, positions, h.shape[0]), h)
            window = (window.astype(F32) + edges).astype(BF16)
        copies[t].wait()
        if t + ahead < taps:
            copies[t + ahead].start()
        total = total + dot_nt(window, weights[t])
    out_ref[...] = total.astype(BF16)


def block_owners():
    return owners(lax.axis_size("seq"), lax.axis_size("grp"))


def embed_kernel(pieces, pooled_ref, *refs):
    blocks, out_ref = refs[:pieces], refs[pieces]
    half = pooled_ref.shape[1]
    for ref, owner in zip(blocks, block_owners()):
        out_ref[owner] = dot_nt(pooled_ref[...], ref[:, :half]).astype(BF16)


def keyvalue_kernel(pieces, half, part_ref, other_ref, gain_ref, *refs):
    blocks, (kv_ref, normed_ref, embedded_ref) = refs[:pieces], refs[pieces:]
    count, _, width = part_ref.shape
    e = (part_ref[...].astype(F32) + other_ref[...].astype(F32)).astype(BF16)
    embedded_ref[...] = e
    e = e.astype(F32)
    squares = jnp.sum(jnp.sum(e * e, axis=0), axis=1, keepdims=True)
    scale = lax.rsqrt(squares / (count * width) + EPS)
    normed_ref[...] = (e * scale[None] * gain_ref[...]).astype(BF16)
    total = 0.0
    for ref, owner in zip(blocks, block_owners()):
        total = total + dot_nn(normed_ref[owner], ref[:, half:])
    kv = total.T.astype(BF16)
    kv_ref[...] = kv


def query_kernel(pieces, normed_ref, *refs):
    blocks, query_ref = refs[:pieces], refs[pieces]
    features = query_ref.shape[1]
    total = 0.0
    for ref, owner in zip(blocks, block_owners()):
        total = total + dot_nn(normed_ref[owner], ref[:, :features])
    query_ref[...] = (total * DK ** (-0.5)).astype(BF16)


def attend_kernel(query_ref, own_ref, other_ref, out_ref, keys, values):
    tokens, features = query_ref.shape
    blocks, _, each = own_ref.shape
    first = lax.axis_index("col") == 0
    for i in range(blocks):
        keys[:, i * each:(i + 1) * each] = jnp.where(first, own_ref[i][:DK], other_ref[i][:DK])
        values[:, i * each:(i + 1) * each] = jnp.where(first, other_ref[i], own_ref[i])
    for h in range(features // DK):
        scores = dot_nn(query_ref[:, h * DK:(h + 1) * DK], keys[...])
        weights = jnp.exp(scores - jnp.max(scores, axis=1, keepdims=True))
        total = jnp.sum(weights, axis=1, keepdims=True)
        out_ref[h] = (dot_nt(weights.astype(BF16), values[...]) / total).astype(BF16)


def output_kernel(pieces, features, attended_ref, *refs):
    blocks, out_ref = refs[:pieces], refs[pieces]
    heads = attended_ref.shape[0]
    flat = jnp.concatenate([attended_ref[h] for h in range(heads)], axis=1)
    for ref, owner in zip(blocks, block_owners()):
        out_ref[owner] = dot_nt(flat, ref[:, features:]).astype(BF16)


def token_kernel(embedded_ref, part_ref, other_ref, weight_ref, token_ref, send_ref, whole):
    col = lax.axis_index("col")
    count, rows, width = part_ref.shape
    projected = None
    for s in range(count):
        tokens = (embedded_ref[s].astype(F32) + (part_ref[s].astype(F32) + other_ref[s].astype(F32))).astype(BF16)
        whole[s] = tokens
        pooled = jnp.mean(tokens.astype(F32).reshape(rows // PAIR_POOL, PAIR_POOL, width), axis=1).astype(BF16)
        part = dot_nn(pooled, weight_ref[s * width:(s + 1) * width])
        projected = part if projected is None else projected + part
    own = token_ref.shape[0]
    mine = pl.ds(pl.multiple_of(col * own, own), own)
    token_ref[...] = jnp.concatenate([whole[s, mine] for s in range(count)], axis=1)
    send_ref[...] = projected.astype(BF16)


def pair_kernel(own_ref, all_ref, weight_ref, out_ref, columns_here):
    seq, col = lax.axis_index("seq"), lax.axis_index("col")
    features, each = weight_ref.shape[0], own_ref.shape[0]
    span = columns_here.shape[0] // each
    rows = all_ref[...].astype(F32)[:, features:]
    if rows.shape[0] == columns_here.shape[0]:
        for j in range(span):
            at = pl.multiple_of((j ^ (seq % span)) * each, each)
            columns_here[pl.ds(at, each)] = rows[j * each:(j + 1) * each]
    else:
        half = columns_here.shape[0]
        columns_here[...] = jnp.where(col == 0, rows[:half], rows[half:])
    rows_here = own_ref[...].astype(F32)[:, :features]
    hidden = gelu(rows_here[:, None, :] + columns_here[...][None, :, :])
    r, c, f = hidden.shape
    out_ref[...] = dot_nn(hidden.reshape(r * c, f).astype(BF16), weight_ref[...]).reshape(r, c, f).astype(BF16)


def cost(flops, size):
    return pl.CostEstimate(flops=int(flops), bytes_accessed=int(size), transcendentals=0)


def on_device(signal, conv_weight, conv_gain, embed_weight, attn_gain, query_weight, keyvalue_weight,
              output_weight, rowcol_weight, pair_weight):
    col = lax.axis_index("col")
    count, cols = lax.axis_size("seq"), lax.axis_size("col")
    positions, half = signal.shape
    taps, channels, _ = conv_weight.shape
    reach = taps // 2
    tokens = positions // POOL
    width = embed_weight.shape[1] * count
    features = query_weight.shape[1] // cols
    heads = features // DK
    swap = [(i, (i + 1) % cols) for i in range(cols)]
    shape = jax.ShapeDtypeStruct

    embed_own = jnp.concatenate(
        [embed_weight.T, lax.dynamic_slice_in_dim(keyvalue_weight, col * DK, DV, 1)], axis=1
    )
    later_own = jnp.concatenate(
        [
            lax.dynamic_slice_in_dim(query_weight, col * features, features, 1),
            lax.dynamic_slice_in_dim(output_weight.T, col * heads * DV, heads * DV, 1),
        ],
        axis=1,
    )
    ring = planned(count, lax.axis_size("grp")) and cols == 2
    e, q = (Blocks(x, count) for x in (embed_own, later_own))

    signal_t = signal.T
    up = [(i, i + 1) for i in range(count - 1)]
    if ring:
        e.along("own", "step")
        e.across("own", "own2")
    other_t = lax.ppermute(signal_t, "col", swap)
    before = lax.ppermute(signal[positions - reach:], "seq", up)
    behind = lax.ppermute(signal[:reach], "seq", [(j, i) for i, j in up])
    own_halo = jnp.pad(jnp.concatenate([before, behind], axis=0), ((0, 16 - 2 * reach), (0, 0)))
    other_halo = lax.ppermute(own_halo, "col", swap)
    halo = jnp.where(
        col == 0, jnp.concatenate([own_halo, other_halo], axis=1), jnp.concatenate([other_halo, own_halo], axis=1)
    )
    gain_row = conv_gain.reshape(1, channels)
    windows = pl.pallas_call(
        functools.partial(act_kernel, taps),
        out_shape=shape((taps * tokens, channels), BF16),
        in_specs=vspec(3),
        out_specs=pl.BlockSpec(memory_space=VMEM),
        scratch_shapes=[pltpu.VMEM((channels, positions), BF16), pltpu.VMEM((channels, 8), F32)],
        compiler_params=params(20),
        cost_estimate=cost(2 * taps * tokens * channels * positions, 4 * channels * positions),
        name="act",
    )(signal_t, other_t, gain_row)
    if ring:
        e.at["step"] = after(e.at["step"], e.at["own2"], windows)
        e.along("step", "far")
        e.across("step", "step2")
        e.between("step", "cross")
    pooled = pl.pallas_call(
        conv_kernel,
        out_shape=shape((tokens, half), BF16),
        in_specs=vspec(4) + hspec(1),
        out_specs=pl.BlockSpec(memory_space=VMEM),
        scratch_shapes=[pltpu.VMEM((taps, half, channels), BF16), pltpu.SemaphoreType.DMA((taps,))],
        compiler_params=params(50),
        cost_estimate=cost(2 * taps * tokens * channels * half, 2 * taps * channels * half),
        name="conv",
    )(windows, signal_t, halo, gain_row, conv_weight.transpose(0, 2, 1))
    if ring:
        e.at["far"] = after(e.at["far"], pooled)
        e.at["step2"] = after(e.at["step2"], pooled)
        e.across("far", "far2")
        e.between("step2", "cross2")
        q.at["own"] = after(q.at["own"], pooled, e.at["far"])
        q.along("own", "step")
        q.at["step"] = after(q.at["step"], e.at["far2"], e.at["cross2"])
        q.along("step", "far")
        q.across("step", "step2")
        q.between("step", "cross")
        q.at["own"] = after(q.at["own"], q.at["step2"])
        q.along("step2", "far2")
        q.across("own", "own2")
        q.between("step2", "cross2")
        embed_blocks, later_blocks = e.pieces(), q.pieces()
    else:
        embed_blocks, later_blocks = ([lax.all_gather(x.at["own"], "seq", axis=0, tiled=True)] for x in (e, q))
    pieces = len(embed_blocks)
    block = width // pieces

    part = pl.pallas_call(
        functools.partial(embed_kernel, pieces),
        out_shape=shape((pieces, tokens, block), BF16),
        in_specs=vspec(1 + pieces),
        out_specs=pl.BlockSpec(memory_space=VMEM),
        compiler_params=params(12),
        cost_estimate=cost(2 * tokens * half * width, 2 * half * width),
        name="embed",
    )(pooled, *embed_blocks)
    other_part = lax.ppermute(part, "col", swap)

    keyvalue, normed, embedded = pl.pallas_call(
        functools.partial(keyvalue_kernel, pieces, half),
        out_shape=(
            shape((DV, tokens), BF16),
            shape((pieces, tokens, block), BF16),
            shape((pieces, tokens, block), BF16),
        ),
        in_specs=vspec(3 + pieces),
        out_specs=vspec(3),
        compiler_params=params(16),
        cost_estimate=cost(2 * tokens * width * DV, 2 * width * DV),
        name="keyvalue",
    )(part, other_part, attn_gain.reshape(pieces, 1, block), *embed_blocks)
    if ring:
        here = jnp.stack([keyvalue, lax.ppermute(keyvalue, "seq", [(i, i ^ 1) for i in range(count)])])
        onward = [(2 * RING[k] + i, 2 * RING[(k + 1) % 4] + i) for k in range(4) for i in range(2)]
        ahead = lax.ppermute(here, "seq", onward)
        back = lax.ppermute(here, "seq", [(j, i) for i, j in onward])
        gathered = jnp.concatenate([here, ahead, back, lax.ppermute(ahead, "seq", onward)])
    else:
        gathered = lax.all_gather(keyvalue, "seq", axis=0)
    gathered_other = lax.ppermute(gathered, "col", swap)

    queries = pl.pallas_call(
        functools.partial(query_kernel, pieces),
        out_shape=shape((tokens, features), BF16),
        in_specs=vspec(1 + pieces),
        out_specs=pl.BlockSpec(memory_space=VMEM),
        compiler_params=params(12),
        cost_estimate=cost(2 * tokens * width * features, 2 * width * features),
        name="query",
    )(normed, *later_blocks)

    attended = pl.pallas_call(
        attend_kernel,
        out_shape=shape((heads, tokens, DV), BF16),
        in_specs=vspec(3),
        out_specs=pl.BlockSpec(memory_space=VMEM),
        scratch_shapes=[pltpu.VMEM((DK, count * tokens), BF16), pltpu.VMEM((DV, count * tokens), BF16)],
        compiler_params=params(24),
        cost_estimate=cost(2 * tokens * heads * count * tokens * (DK + DV), 4 * count * tokens * DV),
        name="attend",
    )(queries, gathered, gathered_other)

    part_out = pl.pallas_call(
        functools.partial(output_kernel, pieces, features),
        out_shape=shape((pieces, tokens, block), BF16),
        in_specs=vspec(1 + pieces),
        out_specs=pl.BlockSpec(memory_space=VMEM),
        compiler_params=params(16),
        cost_estimate=cost(2 * tokens * heads * DV * width, 2 * heads * DV * width),
        name="output",
    )(attended, *later_blocks)
    other_out = lax.ppermute(part_out, "col", swap)

    out_width = rowcol_weight.shape[1]
    own_rows, pair_rows = tokens // cols, tokens // PAIR_POOL
    out_tokens, projected = pl.pallas_call(
        token_kernel,
        out_shape=(shape((own_rows, width), BF16), shape((pair_rows, out_width), BF16)),
        in_specs=vspec(4),
        out_specs=vspec(2),
        scratch_shapes=[pltpu.VMEM((pieces, tokens, block), BF16)],
        compiler_params=params(12),
        cost_estimate=cost(2 * pair_rows * width * out_width, 2 * width * out_width),
        name="tokens",
    )(embedded, part_out, other_out, rowcol_weight)

    if ring:
        rows_all = projected
        for bit in (1, 2):
            rows_all = jnp.concatenate([rows_all, lax.ppermute(rows_all, "seq", [(i, i ^ bit) for i in range(count)])])
        pairs = [(i * cols + i // 4, (i ^ 4) * cols + i // 4) for i in range(count)]
        far_rows = lax.ppermute(rows_all, ("seq", "col"), pairs)
        rows_all = jnp.where(lax.axis_index("seq") // 4 == col, rows_all, far_rows)
    else:
        rows_all = lax.all_gather(projected, "seq", axis=0, tiled=True)

    span = pair_rows * count // cols
    pair_features = pair_weight.shape[0]
    pair_out = pl.pallas_call(
        pair_kernel,
        out_shape=shape((pair_rows, span, pair_features), BF16),
        in_specs=vspec(3),
        out_specs=pl.BlockSpec(memory_space=VMEM),
        scratch_shapes=[pltpu.VMEM((span, pair_features), F32)],
        compiler_params=params(16),
        cost_estimate=cost(2 * pair_rows * span * pair_features**2, 2 * pair_rows * span * pair_features),
        name="pair",
    )(projected, rows_all, pair_weight)
    return out_tokens, pair_out


def solution(mesh):
    placed = (
        P(("grp", "seq"), "col"),
        P(None, None, "col"),
        P(),
        P("col", "seq"),
        P(),
        P("seq", None),
        P("seq", None),
        P(None, "seq"),
        P(),
        P(),
    )
    return jax.shard_map(
        on_device,
        mesh=mesh,
        in_specs=placed,
        out_specs=(P(("grp", "seq", "col"), None), P(("grp", "seq"), "col", None)),
        check_vma=False,
    )
```

```python
import functools
import math

import jax
import jax.numpy as jnp
from jax import lax
from jax.experimental import pallas as pl
from jax.experimental.pallas import tpu as pltpu
from jax.sharding import PartitionSpec as P

DK = 128
DV = 192
POOL = 4
PAIR_POOL = 16
EPS = 1e-06
VMEM = pltpu.VMEM
F32 = jnp.float32
BF16 = jnp.bfloat16


def gelu(x):
    c = math.sqrt(2.0 / math.pi)
    half = 0.5 * x
    return half + half * jnp.tanh(x * (c + (0.044715 * c) * (x * x)))


def dot_nt(a, b):
    return lax.dot_general(a, b, (((1,), (1,)), ((), ())), preferred_element_type=F32)


def dot_nn(a, b):
    return lax.dot_general(a, b, (((1,), (0,)), ((), ())), preferred_element_type=F32)


def params(mib, **kw):
    return pltpu.CompilerParams(vmem_limit_bytes=mib << 20, **kw)


def vspec(n):
    return [pl.BlockSpec(memory_space=VMEM)] * n


def hspec(n):
    return [pl.BlockSpec(memory_space=pltpu.HBM)] * n


RING = (0, 1, 3, 2)


def planned(count, groups):
    return count == 2 * len(RING) and groups == 2


def pick(index, table):
    value = jnp.int32(table[0])
    for i, entry in enumerate(table[1:], 1):
        value = jnp.where(index == i, jnp.int32(entry), value)
    return value


def owners(count, groups):
    if not planned(count, groups):
        return [jnp.int32(0)]
    group, me = lax.axis_index("grp"), lax.axis_index("seq")
    side, place = me % 2, pick(me // 2, [RING.index(i) for i in range(4)])
    result = []
    for step in (0, 3 + 2 * group, 1 + 2 * group, 2):
        row = pick(lax.rem(place + step, 4), RING)
        result += [2 * row + side, 2 * row + 1 - side]
    return result


class Blocks:
    def __init__(self, own, count):
        self.count = count
        self.at = {"own": own}

    def along(self, source, target):
        pairs = []
        for group in range(2):
            for k in range(4):
                a, b = RING[k], RING[(k + 1) % 4]
                if group:
                    a, b = b, a
                pairs += [(group * self.count + 2 * a + i, group * self.count + 2 * b + i) for i in range(2)]
        self.at[target] = lax.ppermute(self.at[source], ("grp", "seq"), pairs)

    def across(self, source, target):
        self.at[target] = lax.ppermute(self.at[source], "seq", [(i, i ^ 1) for i in range(self.count)])

    def between(self, source, target):
        self.at[target] = lax.ppermute(self.at[source], "grp", [(0, 1), (1, 0)])

    def pieces(self):
        names = ("own", "own2", "step", "step2", "cross", "cross2", "far", "far2")
        return [self.at[name] for name in names]


def after(values, *done):
    return lax.optimization_barrier((values, done))[0]


def window_means(first_row, rows, tokens, taps, positions, columns):
    r = lax.broadcasted_iota(jnp.int32, (rows, columns), 0) + first_row
    k = lax.broadcasted_iota(jnp.int32, (rows, columns), 1)
    reach = taps // 2
    if columns != positions:
        k = jnp.where(k < 2 * reach, jnp.where(k < reach, k - reach, k - reach + positions), -positions)
    tap = r // tokens
    gap = k - (POOL * (r - tap * tokens) + tap - reach)
    return jnp.where((gap >= 0) & (gap < POOL), 1.0 / POOL, 0.0).astype(BF16)


def act_kernel(taps, own_ref, other_ref, gain_ref, out_ref, residual_ref, act, gaincol):
    channels, positions = act.shape
    half = own_ref.shape[0]
    col = lax.axis_index("col")
    gaincol[...] = jnp.broadcast_to(gain_ref[...], (8, channels)).T
    step = 64
    halves = ((own_ref, col), (other_ref, 1 - col))
    squares = jnp.zeros((8, positions), F32)
    for ref, _ in halves:
        for j in range(half // step):
            x = ref[j * step:(j + 1) * step, :].astype(F32)
            x = x * x
            for i in range(step // 8):
                squares = squares + x[i * 8:(i + 1) * 8]
    scale = lax.rsqrt(jnp.sum(squares, axis=0, keepdims=True) / channels + EPS)
    for ref, index in halves:
        for j in range(half // step):
            at = pl.multiple_of(index * half + j * step, step)
            x = ref[j * step:(j + 1) * step, :].astype(F32) * scale
            act[pl.ds(at, step), :] = gelu(x * gaincol[pl.ds(at, step), :1]).astype(BF16)
    rows, tokens = out_ref.shape[0], residual_ref.shape[0]
    means = window_means(0, rows, tokens, taps, positions, positions)
    out_ref[...] = dot_nt(means, act[...]).astype(BF16)
    middle = (taps // 2) * tokens
    residual_ref[...] = dot_nt(means[middle:middle + tokens], own_ref[...])


def conv_kernel(positions, windows_ref, residual_ref, halo_ref, gain_ref, weight_hbm, out_ref, weights, sems):
    taps, _, channels = weights.shape
    copies = [pltpu.make_async_copy(weight_hbm.at[t], weights.at[t], sems.at[t]) for t in range(taps)]
    ahead = 2
    for c in copies[:ahead]:
        c.start()
    tokens = out_ref.shape[0]
    h = halo_ref[...].astype(F32)
    h = h * lax.rsqrt(jnp.sum(h * h, axis=1, keepdims=True) / channels + EPS) * gain_ref[...]
    h = gelu(h).astype(BF16)
    total = residual_ref[...]
    for t in range(taps):
        window = windows_ref[t * tokens:(t + 1) * tokens]
        if t != taps // 2:
            edges = dot_nn(window_means(t * tokens, tokens, tokens, taps, positions, h.shape[0]), h)
            window = (window.astype(F32) + edges).astype(BF16)
        copies[t].wait()
        if t + ahead < taps:
            copies[t + ahead].start()
        total = total + dot_nt(window, weights[t])
    out_ref[...] = total.astype(BF16)


def block_owners():
    return owners(lax.axis_size("seq"), lax.axis_size("grp"))


def embed_kernel(pieces, pooled_ref, *refs):
    blocks, (out_ref, rest_ref) = refs[:pieces], refs[pieces:]
    half = pooled_ref.shape[1]
    for ref, owner in zip(blocks, block_owners()):
        out_ref[owner] = dot_nt(pooled_ref[...], ref[:, :half]).astype(BF16)
        rest_ref[owner] = ref[:, half:]


def keyvalue_kernel(part_ref, other_ref, gain_ref, weight_ref, kv_ref, normed_ref, embedded_ref):
    count, _, width = part_ref.shape
    e = (part_ref[...].astype(F32) + other_ref[...].astype(F32)).astype(BF16)
    embedded_ref[...] = e
    e = e.astype(F32)
    squares = jnp.sum(jnp.sum(e * e, axis=0), axis=1, keepdims=True)
    scale = lax.rsqrt(squares / (count * width) + EPS)
    normed_ref[...] = (e * scale[None] * gain_ref[...]).astype(BF16)
    total = 0.0
    for s in range(count):
        total = total + dot_nn(normed_ref[s], weight_ref[s])
    kv = total.T.astype(BF16)
    kv_ref[...] = kv


def query_kernel(pieces, normed_ref, *refs):
    blocks, query_ref = refs[:pieces], refs[pieces]
    features = query_ref.shape[1]
    total = 0.0
    for ref, owner in zip(blocks, block_owners()):
        total = total + dot_nn(normed_ref[owner], ref[:, :features])
    query_ref[...] = (total * DK ** (-0.5)).astype(BF16)


def attend_kernel(query_ref, own_ref, other_ref, out_ref, keys, values):
    tokens, features = query_ref.shape
    blocks, _, each = own_ref.shape
    first = lax.axis_index("col") == 0
    for i in range(blocks):
        keys[:, i * each:(i + 1) * each] = jnp.where(first, own_ref[i][:DK], other_ref[i][:DK])
        values[:, i * each:(i + 1) * each] = jnp.where(first, other_ref[i], own_ref[i])
    for h in range(features // DK):
        scores = dot_nn(query_ref[:, h * DK:(h + 1) * DK], keys[...])
        weights = jnp.exp(scores - jnp.max(scores, axis=1, keepdims=True))
        total = jnp.sum(weights, axis=1, keepdims=True)
        out_ref[h] = (dot_nt(weights.astype(BF16), values[...]) / total).astype(BF16)


def output_kernel(pieces, features, attended_ref, embedded_ref, pair_weight_ref, *refs):
    blocks, (out_ref, pair_ref) = refs[:pieces], refs[pieces:]
    heads = attended_ref.shape[0]
    flat = jnp.concatenate([attended_ref[h] for h in range(heads)], axis=1)
    _, rows, width = out_ref.shape
    share = jnp.where(lax.axis_index("col") == 0, 1.0, 0.0)
    projected = 0.0
    for ref, owner in zip(blocks, block_owners()):
        part = dot_nt(flat, ref[:, features:])
        out_ref[owner] = part.astype(BF16)
        part = part + share * embedded_ref[owner].astype(F32)
        pooled = jnp.mean(part.reshape(rows // PAIR_POOL, PAIR_POOL, width), axis=1).astype(BF16)
        weight = pair_weight_ref[pl.ds(pl.multiple_of(owner * width, width), width)]
        projected = projected + dot_nn(pooled, weight)
    pair_ref[...] = projected.astype(BF16)


def token_kernel(embedded_ref, part_ref, other_ref, token_ref):
    col = lax.axis_index("col")
    own = token_ref.shape[0]
    mine = pl.ds(pl.multiple_of(col * own, own), own)
    blocks = [
        embedded_ref[s, mine].astype(F32) + (part_ref[s, mine].astype(F32) + other_ref[s, mine].astype(F32))
        for s in range(part_ref.shape[0])
    ]
    token_ref[...] = jnp.concatenate(blocks, axis=1).astype(BF16)


def pair_kernel(own_ref, all_ref, weight_ref, out_ref, columns_here):
    seq, col = lax.axis_index("seq"), lax.axis_index("col")
    features, each = weight_ref.shape[0], own_ref.shape[0]
    span = columns_here.shape[0] // each
    rows = all_ref[...].astype(F32)[:, features:]
    if rows.shape[0] == columns_here.shape[0]:
        for j in range(span):
            at = pl.multiple_of((j ^ (seq % span)) * each, each)
            columns_here[pl.ds(at, each)] = rows[j * each:(j + 1) * each]
    else:
        half = columns_here.shape[0]
        columns_here[...] = jnp.where(col == 0, rows[:half], rows[half:])
    rows_here = own_ref[...].astype(F32)[:, :features]
    hidden = gelu(rows_here[:, None, :] + columns_here[...][None, :, :])
    r, c, f = hidden.shape
    out_ref[...] = dot_nn(hidden.reshape(r * c, f).astype(BF16), weight_ref[...]).reshape(r, c, f).astype(BF16)


def cost(flops, size):
    return pl.CostEstimate(flops=int(flops), bytes_accessed=int(size), transcendentals=0)


def on_device(signal, conv_weight, conv_gain, embed_weight, attn_gain, query_weight, keyvalue_weight,
              output_weight, rowcol_weight, pair_weight):
    col = lax.axis_index("col")
    count, cols = lax.axis_size("seq"), lax.axis_size("col")
    positions, half = signal.shape
    taps, channels, _ = conv_weight.shape
    reach = taps // 2
    tokens = positions // POOL
    width = embed_weight.shape[1] * count
    features = query_weight.shape[1] // cols
    heads = features // DK
    swap = [(i, (i + 1) % cols) for i in range(cols)]
    shape = jax.ShapeDtypeStruct

    embed_own = jnp.concatenate(
        [embed_weight.T, lax.dynamic_slice_in_dim(keyvalue_weight, col * DK, DV, 1)], axis=1
    )
    later_own = jnp.concatenate(
        [
            lax.dynamic_slice_in_dim(query_weight, col * features, features, 1),
            lax.dynamic_slice_in_dim(output_weight.T, col * heads * DV, heads * DV, 1),
        ],
        axis=1,
    )
    ring = planned(count, lax.axis_size("grp")) and cols == 2
    e, q = (Blocks(x, count) for x in (embed_own, later_own))

    signal_t = signal.T
    up = [(i, i + 1) for i in range(count - 1)]
    if ring:
        e.along("own", "step")
        e.across("own", "own2")
    other_t = lax.ppermute(signal_t, "col", swap)
    before = lax.ppermute(signal[positions - reach:], "seq", up)
    behind = lax.ppermute(signal[:reach], "seq", [(j, i) for i, j in up])
    own_halo = jnp.pad(jnp.concatenate([before, behind], axis=0), ((0, 16 - 2 * reach), (0, 0)))
    other_halo = lax.ppermute(own_halo, "col", swap)
    halo = jnp.where(
        col == 0, jnp.concatenate([own_halo, other_halo], axis=1), jnp.concatenate([other_halo, own_halo], axis=1)
    )
    gain_row = conv_gain.reshape(1, channels)
    windows, residual = pl.pallas_call(
        functools.partial(act_kernel, taps),
        out_shape=(shape((taps * tokens, channels), BF16), shape((tokens, half), F32)),
        in_specs=vspec(3),
        out_specs=vspec(2),
        scratch_shapes=[pltpu.VMEM((channels, positions), BF16), pltpu.VMEM((channels, 8), F32)],
        compiler_params=params(20),
        cost_estimate=cost(2 * taps * tokens * channels * positions, 4 * channels * positions),
        name="act",
    )(signal_t, other_t, gain_row)
    if ring:
        e.at["step"] = after(e.at["step"], e.at["own2"], windows)
        e.along("step", "far")
        e.across("step", "step2")
        e.between("step", "cross")
    pooled = pl.pallas_call(
        functools.partial(conv_kernel, positions),
        out_shape=shape((tokens, half), BF16),
        in_specs=vspec(4) + hspec(1),
        out_specs=pl.BlockSpec(memory_space=VMEM),
        scratch_shapes=[pltpu.VMEM((taps, half, channels), BF16), pltpu.SemaphoreType.DMA((taps,))],
        compiler_params=params(50),
        cost_estimate=cost(2 * taps * tokens * channels * half, 2 * taps * channels * half),
        name="conv",
    )(windows, residual, halo, gain_row, conv_weight.transpose(0, 2, 1))
    if ring:
        e.at["far"] = after(e.at["far"], pooled, e.at["cross"])
        e.at["step2"] = after(e.at["step2"], pooled, e.at["cross"])
        e.across("far", "far2")
        e.between("step2", "cross2")
        q.at["own"] = after(q.at["own"], pooled, e.at["far"])
        q.along("own", "step")
        q.across("own", "own2")
        q.at["step"] = after(q.at["step"], e.at["far2"], e.at["cross2"])
        q.along("step", "far")
        q.across("step", "step2")
        q.between("step", "cross")
        q.across("far", "far2")
        q.between("step2", "cross2")
        embed_blocks, later_blocks = e.pieces(), q.pieces()
    else:
        embed_blocks, later_blocks = ([lax.all_gather(x.at["own"], "seq", axis=0, tiled=True)] for x in (e, q))
    pieces = len(embed_blocks)
    block = width // pieces

    part, keyvalue_blocks = pl.pallas_call(
        functools.partial(embed_kernel, pieces),
        out_shape=(shape((pieces, tokens, block), BF16), shape((pieces, block, DV), BF16)),
        in_specs=vspec(1 + pieces),
        out_specs=vspec(2),
        compiler_params=params(12),
        cost_estimate=cost(2 * tokens * half * width, 2 * half * width),
        name="embed",
    )(pooled, *embed_blocks)
    other_part = lax.ppermute(part, "col", swap)
    if ring:
        other_part = after(other_part, q.at["own2"])

    keyvalue, normed, embedded = pl.pallas_call(
        keyvalue_kernel,
        out_shape=(
            shape((DV, tokens), BF16),
            shape((pieces, tokens, block), BF16),
            shape((pieces, tokens, block), BF16),
        ),
        in_specs=vspec(4),
        out_specs=vspec(3),
        compiler_params=params(16),
        cost_estimate=cost(2 * tokens * width * DV, 2 * width * DV),
        name="keyvalue",
    )(part, other_part, attn_gain.reshape(pieces, 1, block), keyvalue_blocks)
    if ring:
        here = jnp.stack([keyvalue, lax.ppermute(keyvalue, "seq", [(i, i ^ 1) for i in range(count)])])
        here = after(here, q.at["far"], q.at["step2"], q.at["cross"])
        onward = [(2 * RING[k] + i, 2 * RING[(k + 1) % 4] + i) for k in range(4) for i in range(2)]
        ahead = lax.ppermute(here, "seq", onward)
        back = lax.ppermute(here, "seq", [(j, i) for i, j in onward])
        gathered = jnp.concatenate([here, ahead, back, lax.ppermute(ahead, "seq", onward)])
    else:
        gathered = lax.all_gather(keyvalue, "seq", axis=0)
    gathered_other = lax.ppermute(gathered, "col", swap)

    queries = pl.pallas_call(
        functools.partial(query_kernel, pieces),
        out_shape=shape((tokens, features), BF16),
        in_specs=vspec(1 + pieces),
        out_specs=pl.BlockSpec(memory_space=VMEM),
        compiler_params=params(12),
        cost_estimate=cost(2 * tokens * width * features, 2 * width * features),
        name="query",
    )(normed, *later_blocks)

    attended = pl.pallas_call(
        attend_kernel,
        out_shape=shape((heads, tokens, DV), BF16),
        in_specs=vspec(3),
        out_specs=pl.BlockSpec(memory_space=VMEM),
        scratch_shapes=[pltpu.VMEM((DK, count * tokens), BF16), pltpu.VMEM((DV, count * tokens), BF16)],
        compiler_params=params(24),
        cost_estimate=cost(2 * tokens * heads * count * tokens * (DK + DV), 4 * count * tokens * DV),
        name="attend",
    )(queries, gathered, gathered_other)

    out_width = rowcol_weight.shape[1]
    own_rows, pair_rows = tokens // cols, tokens // PAIR_POOL
    part_out, part_pair = pl.pallas_call(
        functools.partial(output_kernel, pieces, features),
        out_shape=(shape((pieces, tokens, block), BF16), shape((pair_rows, out_width), BF16)),
        in_specs=vspec(3 + pieces),
        out_specs=vspec(2),
        compiler_params=params(16),
        cost_estimate=cost(2 * tokens * heads * DV * width, 2 * heads * DV * width),
        name="output",
    )(attended, embedded, rowcol_weight, *later_blocks)
    other_pair = lax.ppermute(part_pair, "col", swap)
    other_out = lax.ppermute(part_out, "col", swap)
    projected = (part_pair.astype(F32) + other_pair.astype(F32)).astype(BF16)
    out_tokens = pl.pallas_call(
        token_kernel,
        out_shape=shape((own_rows, width), BF16),
        in_specs=vspec(3),
        out_specs=pl.BlockSpec(memory_space=VMEM),
        compiler_params=params(12),
        cost_estimate=cost(3 * own_rows * width, 8 * own_rows * width),
        name="tokens",
    )(embedded, part_out, other_out)

    if ring:
        rows_all = projected
        for bit in (1, 2):
            rows_all = jnp.concatenate([rows_all, lax.ppermute(rows_all, "seq", [(i, i ^ bit) for i in range(count)])])
        pairs = [(i * cols + i // 4, (i ^ 4) * cols + i // 4) for i in range(count)]
        far_rows = lax.ppermute(rows_all, ("seq", "col"), pairs)
        rows_all = jnp.where(lax.axis_index("seq") // 4 == col, rows_all, far_rows)
    else:
        rows_all = lax.all_gather(projected, "seq", axis=0, tiled=True)

    span = pair_rows * count // cols
    pair_features = pair_weight.shape[0]
    pair_out = pl.pallas_call(
        pair_kernel,
        out_shape=shape((pair_rows, span, pair_features), BF16),
        in_specs=vspec(3),
        out_specs=pl.BlockSpec(memory_space=VMEM),
        scratch_shapes=[pltpu.VMEM((span, pair_features), F32)],
        compiler_params=params(16),
        cost_estimate=cost(2 * pair_rows * span * pair_features**2, 2 * pair_rows * span * pair_features),
        name="pair",
    )(projected, rows_all, pair_weight)
    return out_tokens, pair_out


def solution(mesh):
    placed = (
        P(("grp", "seq"), "col"),
        P(None, None, "col"),
        P(),
        P("col", "seq"),
        P(),
        P("seq", None),
        P("seq", None),
        P(None, "seq"),
        P(),
        P(),
    )
    return jax.shard_map(
        on_device,
        mesh=mesh,
        in_specs=placed,
        out_specs=(P(("grp", "seq", "col"), None), P(("grp", "seq"), "col", None)),
        check_vma=False,
    )
```

```python
import functools
import math

import jax
import jax.numpy as jnp
from jax import lax
from jax.experimental import pallas as pl
from jax.experimental.pallas import tpu as pltpu
from jax.sharding import PartitionSpec as P

DK = 128
DV = 192
POOL = 4
PAIR_POOL = 16
EPS = 1e-06
VMEM = pltpu.VMEM
F32 = jnp.float32
BF16 = jnp.bfloat16


def gelu(x):
    c = math.sqrt(2.0 / math.pi)
    half = 0.5 * x
    return half + half * jnp.tanh(x * (c + (0.044715 * c) * (x * x)))


def dot_nt(a, b):
    return lax.dot_general(a, b, (((1,), (1,)), ((), ())), preferred_element_type=F32)


def dot_nn(a, b):
    return lax.dot_general(a, b, (((1,), (0,)), ((), ())), preferred_element_type=F32)


def params(mib, **kw):
    return pltpu.CompilerParams(vmem_limit_bytes=mib << 20, **kw)


def vspec(n):
    return [pl.BlockSpec(memory_space=VMEM)] * n


def hspec(n):
    return [pl.BlockSpec(memory_space=pltpu.HBM)] * n


RING = (0, 1, 3, 2)


def planned(count, groups):
    return count == 2 * len(RING) and groups == 2


def pick(index, table):
    value = jnp.int32(table[0])
    for i, entry in enumerate(table[1:], 1):
        value = jnp.where(index == i, jnp.int32(entry), value)
    return value


def owners(count, groups):
    if not planned(count, groups):
        return [jnp.int32(0)]
    group, me = lax.axis_index("grp"), lax.axis_index("seq")
    side, place = me % 2, pick(me // 2, [RING.index(i) for i in range(4)])
    result = []
    for step in (0, 3 + 2 * group, 1 + 2 * group, 2):
        row = pick(lax.rem(place + step, 4), RING)
        result += [2 * row + side, 2 * row + 1 - side]
    return result


class Blocks:
    def __init__(self, own, count):
        self.count = count
        self.at = {"own": own}

    def along(self, source, target):
        pairs = []
        for group in range(2):
            for k in range(4):
                a, b = RING[k], RING[(k + 1) % 4]
                if group:
                    a, b = b, a
                pairs += [(group * self.count + 2 * a + i, group * self.count + 2 * b + i) for i in range(2)]
        self.at[target] = lax.ppermute(self.at[source], ("grp", "seq"), pairs)

    def across(self, source, target):
        self.at[target] = lax.ppermute(self.at[source], "seq", [(i, i ^ 1) for i in range(self.count)])

    def between(self, source, target):
        self.at[target] = lax.ppermute(self.at[source], "grp", [(0, 1), (1, 0)])

    def pieces(self):
        names = ("own", "own2", "step", "step2", "cross", "cross2", "far", "far2")
        return [self.at[name] for name in names]


def after(values, *done):
    return lax.optimization_barrier((values, done))[0]


def window_means(first_row, rows, tokens, taps, positions, columns):
    r = lax.broadcasted_iota(jnp.int32, (rows, columns), 0) + first_row
    k = lax.broadcasted_iota(jnp.int32, (rows, columns), 1)
    reach = taps // 2
    if columns != positions:
        k = jnp.where(k < 2 * reach, jnp.where(k < reach, k - reach, k - reach + positions), -positions)
    tap = r // tokens
    gap = k - (POOL * (r - tap * tokens) + tap - reach)
    return jnp.where((gap >= 0) & (gap < POOL), 1.0 / POOL, 0.0).astype(BF16)


def act_kernel(taps, own_ref, other_ref, gain_ref, out_ref, residual_ref, act, gaincol):
    channels, positions = act.shape
    half = own_ref.shape[0]
    col = lax.axis_index("col")
    gaincol[...] = jnp.broadcast_to(gain_ref[...], (8, channels)).T
    step = 64
    halves = ((own_ref, col), (other_ref, 1 - col))
    squares = jnp.zeros((8, positions), F32)
    for ref, _ in halves:
        for j in range(half // step):
            x = ref[j * step:(j + 1) * step, :].astype(F32)
            x = x * x
            for i in range(step // 8):
                squares = squares + x[i * 8:(i + 1) * 8]
    scale = lax.rsqrt(jnp.sum(squares, axis=0, keepdims=True) / channels + EPS)
    for ref, index in halves:
        for j in range(half // step):
            at = pl.multiple_of(index * half + j * step, step)
            x = ref[j * step:(j + 1) * step, :].astype(F32) * scale
            act[pl.ds(at, step), :] = gelu(x * gaincol[pl.ds(at, step), :1]).astype(BF16)
    rows, tokens = out_ref.shape[0], residual_ref.shape[0]
    means = window_means(0, rows, tokens, taps, positions, positions)
    out_ref[...] = dot_nt(means, act[...]).astype(BF16)
    middle = (taps // 2) * tokens
    residual_ref[...] = dot_nt(means[middle:middle + tokens], own_ref[...])


def conv_kernel(positions, windows_ref, residual_ref, halo_ref, gain_ref, weight_hbm, out_ref, weights, sems):
    taps, _, channels = weights.shape
    copies = [pltpu.make_async_copy(weight_hbm.at[t], weights.at[t], sems.at[t]) for t in range(taps)]
    ahead = 2
    for c in copies[:ahead]:
        c.start()
    tokens = out_ref.shape[0]
    h = halo_ref[...].astype(F32)
    h = h * lax.rsqrt(jnp.sum(h * h, axis=1, keepdims=True) / channels + EPS) * gain_ref[...]
    h = gelu(h).astype(BF16)
    total = residual_ref[...]
    for t in range(taps):
        window = windows_ref[t * tokens:(t + 1) * tokens]
        if t != taps // 2:
            edges = dot_nn(window_means(t * tokens, tokens, tokens, taps, positions, h.shape[0]), h)
            window = (window.astype(F32) + edges).astype(BF16)
        copies[t].wait()
        if t + ahead < taps:
            copies[t + ahead].start()
        total = total + dot_nt(window, weights[t])
    out_ref[...] = total.astype(BF16)


def block_owners():
    return owners(lax.axis_size("seq"), lax.axis_size("grp"))


def embed_kernel(pieces, pooled_ref, *refs):
    blocks, (out_ref, rest_ref) = refs[:pieces], refs[pieces:]
    half = pooled_ref.shape[1]
    for ref, owner in zip(blocks, block_owners()):
        out_ref[owner] = dot_nt(pooled_ref[...], ref[:, :half]).astype(BF16)
        rest_ref[owner] = ref[:, half:]


def keyvalue_kernel(part_ref, other_ref, gain_ref, weight_ref, kv_ref, normed_ref, embedded_ref):
    count, _, width = part_ref.shape
    e = (part_ref[...].astype(F32) + other_ref[...].astype(F32)).astype(BF16)
    embedded_ref[...] = e
    e = e.astype(F32)
    squares = jnp.sum(jnp.sum(e * e, axis=0), axis=1, keepdims=True)
    scale = lax.rsqrt(squares / (count * width) + EPS)
    normed_ref[...] = (e * scale[None] * gain_ref[...]).astype(BF16)
    total = 0.0
    for s in range(count):
        total = total + dot_nn(normed_ref[s], weight_ref[s])
    kv = total.T.astype(BF16)
    kv_ref[...] = kv


def later_blocks_of(refs):
    places = block_owners()
    per = len(places) // len(refs)
    rows = refs[0].shape[0] // per
    for i, place in enumerate(places):
        start = (i % per) * rows
        yield refs[i // per], slice(start, start + rows), place


def query_kernel(sides, *refs):
    normed, pieces, query_ref = refs[:sides], refs[sides:-1], refs[-1]
    features = query_ref.shape[1]
    tokens = normed[0].shape[1]
    totals = [0.0] * sides
    for ref, rows, place in later_blocks_of(pieces):
        weight = ref[rows, :features]
        totals = [t + dot_nn(n[place], weight) for t, n in zip(totals, normed)]
    for i, total in enumerate(totals):
        query_ref[i * tokens:(i + 1) * tokens] = (total * DK ** (-0.5)).astype(BF16)


def attend_kernel(query_ref, own_ref, other_ref, out_ref, keys, values):
    tokens, features = query_ref.shape
    blocks, _, each = own_ref.shape
    first = lax.axis_index("col") == 0
    for i in range(blocks):
        keys[:, i * each:(i + 1) * each] = jnp.where(first, own_ref[i][:DK], other_ref[i][:DK])
        values[:, i * each:(i + 1) * each] = jnp.where(first, other_ref[i], own_ref[i])
    for h in range(features // DK):
        scores = dot_nn(query_ref[:, h * DK:(h + 1) * DK], keys[...])
        weights = jnp.exp(scores - jnp.max(scores, axis=1, keepdims=True))
        total = jnp.sum(weights, axis=1, keepdims=True)
        out_ref[h] = (dot_nt(weights.astype(BF16), values[...]) / total).astype(BF16)


def output_kernel(sides, features, attended_ref, embedded_ref, pair_weight_ref, *refs):
    pieces, outs, pair_ref = refs[:-1 - sides], refs[-1 - sides:-1], refs[-1]
    heads = attended_ref.shape[0]
    flat = jnp.concatenate([attended_ref[h] for h in range(heads)], axis=1)
    _, tokens, width = outs[0].shape
    share = jnp.where(lax.axis_index("col") == 0, 1.0, 0.0)
    projected = 0.0
    for ref, rows, place in later_blocks_of(pieces):
        part = dot_nt(flat, ref[rows, features:])
        for i, out in enumerate(outs):
            out[place] = part[i * tokens:(i + 1) * tokens].astype(BF16)
        pooled = jnp.mean(part.reshape(sides * tokens // PAIR_POOL, PAIR_POOL, width), axis=1)
        first = jnp.mean(embedded_ref[place].astype(F32).reshape(tokens // PAIR_POOL, PAIR_POOL, width), axis=1) * share
        if sides > 1:
            first = jnp.concatenate([first, jnp.zeros((pooled.shape[0] - first.shape[0], width), F32)], axis=0)
        weight = pair_weight_ref[pl.ds(pl.multiple_of(place * width, width), width)]
        projected = projected + dot_nn((pooled + first).astype(BF16), weight)
    pair_ref[...] = projected.astype(BF16)


def token_kernel(embedded_ref, part_ref, other_ref, token_ref):
    col = lax.axis_index("col")
    own = token_ref.shape[0]
    mine = pl.ds(pl.multiple_of(col * own, own), own)
    blocks = [
        embedded_ref[s, mine].astype(F32) + (part_ref[s, mine].astype(F32) + other_ref[s, mine].astype(F32))
        for s in range(part_ref.shape[0])
    ]
    token_ref[...] = jnp.concatenate(blocks, axis=1).astype(BF16)


def pair_kernel(own_ref, all_ref, weight_ref, out_ref, columns_here):
    seq, col = lax.axis_index("seq"), lax.axis_index("col")
    features, each = weight_ref.shape[0], own_ref.shape[0]
    span = columns_here.shape[0] // each
    rows = all_ref[...].astype(F32)[:, features:]
    if rows.shape[0] == columns_here.shape[0]:
        for j in range(span):
            at = pl.multiple_of((j ^ (seq % span)) * each, each)
            columns_here[pl.ds(at, each)] = rows[j * each:(j + 1) * each]
    else:
        half = columns_here.shape[0]
        columns_here[...] = jnp.where(col == 0, rows[:half], rows[half:])
    rows_here = own_ref[...].astype(F32)[:, :features]
    hidden = gelu(rows_here[:, None, :] + columns_here[...][None, :, :])
    r, c, f = hidden.shape
    out_ref[...] = dot_nn(hidden.reshape(r * c, f).astype(BF16), weight_ref[...]).reshape(r, c, f).astype(BF16)


def cost(flops, size):
    return pl.CostEstimate(flops=int(flops), bytes_accessed=int(size), transcendentals=0)


def on_device(signal, conv_weight, conv_gain, embed_weight, attn_gain, query_weight, keyvalue_weight,
              output_weight, rowcol_weight, pair_weight):
    col = lax.axis_index("col")
    count, cols = lax.axis_size("seq"), lax.axis_size("col")
    positions, half = signal.shape
    taps, channels, _ = conv_weight.shape
    reach = taps // 2
    tokens = positions // POOL
    width = embed_weight.shape[1] * count
    features = query_weight.shape[1] // cols
    heads = features // DK
    swap = [(i, (i + 1) % cols) for i in range(cols)]
    shape = jax.ShapeDtypeStruct

    embed_own = jnp.concatenate(
        [embed_weight.T, lax.dynamic_slice_in_dim(keyvalue_weight, col * DK, DV, 1)], axis=1
    )
    ring = planned(count, lax.axis_size("grp")) and cols == 2
    sides = 2 if ring else 1
    side = lax.axis_index("seq") % sides
    pair_swap = [(i, i ^ 1) for i in range(count)]
    heads, features = heads // sides, features // sides

    def later_part(which):
        place = col * sides + which
        return jnp.concatenate(
            [
                lax.dynamic_slice_in_dim(query_weight, place * features, features, 1),
                lax.dynamic_slice_in_dim(output_weight.T, place * heads * DV, heads * DV, 1),
            ],
            axis=1,
        )

    e = Blocks(embed_own, count)

    signal_t = signal.T
    up = [(i, i + 1) for i in range(count - 1)]
    if ring:
        e.along("own", "step")
        e.across("own", "own2")
    other_t = lax.ppermute(signal_t, "col", swap)
    before = lax.ppermute(signal[positions - reach:], "seq", up)
    behind = lax.ppermute(signal[:reach], "seq", [(j, i) for i, j in up])
    own_halo = jnp.pad(jnp.concatenate([before, behind], axis=0), ((0, 16 - 2 * reach), (0, 0)))
    other_halo = lax.ppermute(own_halo, "col", swap)
    halo = jnp.where(
        col == 0, jnp.concatenate([own_halo, other_halo], axis=1), jnp.concatenate([other_halo, own_halo], axis=1)
    )
    if ring:
        other_t = after(other_t, e.at["step"], e.at["own2"])
    gain_row = conv_gain.reshape(1, channels)
    windows, residual = pl.pallas_call(
        functools.partial(act_kernel, taps),
        out_shape=(shape((taps * tokens, channels), BF16), shape((tokens, half), F32)),
        in_specs=vspec(3),
        out_specs=vspec(2),
        scratch_shapes=[pltpu.VMEM((channels, positions), BF16), pltpu.VMEM((channels, 8), F32)],
        compiler_params=params(20),
        cost_estimate=cost(2 * taps * tokens * channels * positions, 4 * channels * positions),
        name="act",
    )(signal_t, other_t, gain_row)
    if ring:
        e.at["step"] = after(e.at["step"], e.at["own2"])
        e.along("step", "far")
        e.across("step", "step2")
        e.between("step", "cross")
    pooled = pl.pallas_call(
        functools.partial(conv_kernel, positions),
        out_shape=shape((tokens, half), BF16),
        in_specs=vspec(4) + hspec(1),
        out_specs=pl.BlockSpec(memory_space=VMEM),
        scratch_shapes=[pltpu.VMEM((taps, half, channels), BF16), pltpu.SemaphoreType.DMA((taps,))],
        compiler_params=params(50),
        cost_estimate=cost(2 * taps * tokens * channels * half, 2 * taps * channels * half),
        name="conv",
    )(windows, residual, halo, gain_row, conv_weight.transpose(0, 2, 1))
    if ring:
        e.at["far"] = after(e.at["far"], pooled, e.at["cross"])
        e.at["step2"] = after(e.at["step2"], pooled, e.at["cross"])
        e.across("far", "far2")
        e.between("step2", "cross2")
        theirs = after(later_part(1 - side), pooled, e.at["cross"])
        received = lax.ppermute(theirs, "seq", pair_swap)
        pooled = after(pooled, received)
        q = Blocks(jnp.concatenate([later_part(side), received]), count)
        q.at["own"] = after(q.at["own"], e.at["far2"])
        q.along("own", "step")
        q.along("step", "far")
        q.between("step", "cross")
        embed_blocks = e.pieces()
        later_blocks = [q.at[name] for name in ("own", "step", "cross", "far")]
    else:
        embed_blocks, later_blocks = (
            [lax.all_gather(x, "seq", axis=0, tiled=True)] for x in (embed_own, later_part(0))
        )
    pieces = len(embed_blocks)
    block = width // pieces

    part, keyvalue_blocks = pl.pallas_call(
        functools.partial(embed_kernel, pieces),
        out_shape=(shape((pieces, tokens, block), BF16), shape((pieces, block, DV), BF16)),
        in_specs=vspec(1 + pieces),
        out_specs=vspec(2),
        compiler_params=params(12),
        cost_estimate=cost(2 * tokens * half * width, 2 * half * width),
        name="embed",
    )(pooled, *embed_blocks)
    other_part = lax.ppermute(part, "col", swap)

    keyvalue, normed, embedded = pl.pallas_call(
        keyvalue_kernel,
        out_shape=(
            shape((DV, tokens), BF16),
            shape((pieces, tokens, block), BF16),
            shape((pieces, tokens, block), BF16),
        ),
        in_specs=vspec(4),
        out_specs=vspec(3),
        compiler_params=params(16),
        cost_estimate=cost(2 * tokens * width * DV, 2 * width * DV),
        name="keyvalue",
    )(part, other_part, attn_gain.reshape(pieces, 1, block), keyvalue_blocks)
    both_normed = [normed]
    if ring:
        here = jnp.stack([keyvalue, lax.ppermute(keyvalue, "seq", pair_swap)])
        both_normed.append(lax.ppermute(normed, "seq", pair_swap))
        onward = [(2 * RING[k] + i, 2 * RING[(k + 1) % 4] + i) for k in range(4) for i in range(2)]
        ahead = lax.ppermute(here, "seq", onward)
        back = lax.ppermute(here, "seq", [(j, i) for i, j in onward])
        gathered = jnp.concatenate([here, ahead, back, lax.ppermute(ahead, "seq", onward)])
    else:
        gathered = lax.all_gather(keyvalue, "seq", axis=0)
    gathered_other = lax.ppermute(gathered, "col", swap)

    queries = pl.pallas_call(
        functools.partial(query_kernel, sides),
        out_shape=shape((sides * tokens, features), BF16),
        in_specs=vspec(sides + len(later_blocks)),
        out_specs=pl.BlockSpec(memory_space=VMEM),
        compiler_params=params(12),
        cost_estimate=cost(2 * sides * tokens * width * features, 2 * width * features),
        name="query",
    )(*both_normed, *later_blocks)

    attended = pl.pallas_call(
        attend_kernel,
        out_shape=shape((heads, sides * tokens, DV), BF16),
        in_specs=vspec(3),
        out_specs=pl.BlockSpec(memory_space=VMEM),
        scratch_shapes=[pltpu.VMEM((DK, count * tokens), BF16), pltpu.VMEM((DV, count * tokens), BF16)],
        compiler_params=params(24),
        cost_estimate=cost(2 * tokens * heads * count * tokens * (DK + DV), 4 * count * tokens * DV),
        name="attend",
    )(queries, gathered, gathered_other)

    out_width = rowcol_weight.shape[1]
    own_rows, pair_rows = tokens // cols, tokens // PAIR_POOL
    *part_outs, part_pair = pl.pallas_call(
        functools.partial(output_kernel, sides, features),
        out_shape=tuple(
            [shape((pieces, tokens, block), BF16)] * sides + [shape((sides * pair_rows, out_width), BF16)]
        ),
        in_specs=vspec(3 + len(later_blocks)),
        out_specs=vspec(sides + 1),
        compiler_params=params(16),
        cost_estimate=cost(2 * sides * tokens * heads * DV * width, 2 * heads * DV * width),
        name="output",
    )(attended, embedded, rowcol_weight, *later_blocks)

    def total(*parts):
        return sum(x.astype(F32) for x in parts).astype(BF16)

    part_out = part_outs[0]
    if ring:
        turned = lax.ppermute(part_pair, "seq", pair_swap)
        part_pair = total(part_pair, jnp.concatenate([turned[pair_rows:], turned[:pair_rows]]))
    projected = total(part_pair, lax.ppermute(part_pair, "col", swap))
    if ring:
        part_out = total(part_out, lax.ppermute(part_outs[1], "seq", pair_swap))
    other_out = lax.ppermute(part_out, "col", swap)
    out_tokens = pl.pallas_call(
        token_kernel,
        out_shape=shape((own_rows, width), BF16),
        in_specs=vspec(3),
        out_specs=pl.BlockSpec(memory_space=VMEM),
        compiler_params=params(12),
        cost_estimate=cost(3 * own_rows * width, 8 * own_rows * width),
        name="tokens",
    )(embedded, part_out, other_out)

    if ring:
        rows_all = projected
        rows_all = jnp.concatenate([rows_all, lax.ppermute(rows_all, "seq", [(i, i ^ 2) for i in range(count)])])
        pairs = [(i * cols + i // 4, (i ^ 4) * cols + i // 4) for i in range(count)]
        far_rows = lax.ppermute(rows_all, ("seq", "col"), pairs)
        rows_all = jnp.where(lax.axis_index("seq") // 4 == col, rows_all, far_rows)
    else:
        rows_all = lax.all_gather(projected, "seq", axis=0, tiled=True)

    span = pair_rows * count // cols
    pair_features = pair_weight.shape[0]
    pair_out = pl.pallas_call(
        pair_kernel,
        out_shape=shape((pair_rows, span, pair_features), BF16),
        in_specs=vspec(3),
        out_specs=pl.BlockSpec(memory_space=VMEM),
        scratch_shapes=[pltpu.VMEM((span, pair_features), F32)],
        compiler_params=params(16),
        cost_estimate=cost(2 * pair_rows * span * pair_features**2, 2 * pair_rows * span * pair_features),
        name="pair",
    )(projected[:pair_rows], rows_all, pair_weight)
    return out_tokens, pair_out


def solution(mesh):
    placed = (
        P(("grp", "seq"), "col"),
        P(None, None, "col"),
        P(),
        P("col", "seq"),
        P(),
        P("seq", None),
        P("seq", None),
        P(None, "seq"),
        P(),
        P(),
    )
    return jax.shard_map(
        on_device,
        mesh=mesh,
        in_specs=placed,
        out_specs=(P(("grp", "seq", "col"), None), P(("grp", "seq"), "col", None)),
        check_vma=False,
    )
```

```python
import functools
import math

import jax
import jax.numpy as jnp
from jax import lax
from jax.experimental import pallas as pl
from jax.experimental.pallas import tpu as pltpu
from jax.sharding import PartitionSpec as P

DK = 128
DV = 192
POOL = 4
PAIR_POOL = 16
EPS = 1e-06
VMEM = pltpu.VMEM
F32 = jnp.float32
BF16 = jnp.bfloat16


def gelu(x):
    c = math.sqrt(2.0 / math.pi)
    half = 0.5 * x
    return half + half * jnp.tanh(x * (c + (0.044715 * c) * (x * x)))


def dot_nt(a, b):
    return lax.dot_general(a, b, (((1,), (1,)), ((), ())), preferred_element_type=F32)


def dot_nn(a, b):
    return lax.dot_general(a, b, (((1,), (0,)), ((), ())), preferred_element_type=F32)


def params(mib, **kw):
    return pltpu.CompilerParams(vmem_limit_bytes=mib << 20, **kw)


def vspec(n):
    return [pl.BlockSpec(memory_space=VMEM)] * n


def hspec(n):
    return [pl.BlockSpec(memory_space=pltpu.HBM)] * n


RING = (0, 1, 3, 2)


def planned(count, groups):
    return count == 2 * len(RING) and groups == 2


def pick(index, table):
    value = jnp.int32(table[0])
    for i, entry in enumerate(table[1:], 1):
        value = jnp.where(index == i, jnp.int32(entry), value)
    return value


def owners(count, groups):
    if not planned(count, groups):
        return [jnp.int32(0)]
    group, me = lax.axis_index("grp"), lax.axis_index("seq")
    side, place = me % 2, pick(me // 2, [RING.index(i) for i in range(4)])
    result = []
    for step in (0, 3 + 2 * group, 1 + 2 * group, 2):
        row = pick(lax.rem(place + step, 4), RING)
        result += [2 * row + side, 2 * row + 1 - side]
    return result


class Blocks:
    def __init__(self, own, count):
        self.count = count
        self.at = {"own": own}

    def along(self, source, target):
        pairs = []
        for group in range(2):
            for k in range(4):
                a, b = RING[k], RING[(k + 1) % 4]
                if group:
                    a, b = b, a
                pairs += [(group * self.count + 2 * a + i, group * self.count + 2 * b + i) for i in range(2)]
        self.at[target] = lax.ppermute(self.at[source], ("grp", "seq"), pairs)

    def across(self, source, target):
        self.at[target] = lax.ppermute(self.at[source], "seq", [(i, i ^ 1) for i in range(self.count)])

    def between(self, source, target):
        self.at[target] = lax.ppermute(self.at[source], "grp", [(0, 1), (1, 0)])

    def pieces(self):
        names = ("own", "own2", "step", "step2", "cross", "cross2", "far", "far2")
        return [self.at[name] for name in names]


def after(values, *done):
    return lax.optimization_barrier((values, done))[0]


def window_means(first_row, rows, tokens, taps, positions, columns):
    r = lax.broadcasted_iota(jnp.int32, (rows, columns), 0) + first_row
    k = lax.broadcasted_iota(jnp.int32, (rows, columns), 1)
    reach = taps // 2
    if columns != positions:
        k = jnp.where(k < 2 * reach, jnp.where(k < reach, k - reach, k - reach + positions), -positions)
    tap = r // tokens
    gap = k - (POOL * (r - tap * tokens) + tap - reach)
    return jnp.where((gap >= 0) & (gap < POOL), 1.0 / POOL, 0.0).astype(BF16)


def act_kernel(taps, own_ref, other_ref, gain_ref, out_ref, residual_ref, act, gaincol):
    channels, positions = act.shape
    half = own_ref.shape[0]
    col = lax.axis_index("col")
    gaincol[...] = jnp.broadcast_to(gain_ref[...], (8, channels)).T
    step = 64
    halves = ((own_ref, col), (other_ref, 1 - col))
    squares = jnp.zeros((8, positions), F32)
    for ref, _ in halves:
        for j in range(half // step):
            x = ref[j * step:(j + 1) * step, :].astype(F32)
            x = x * x
            for i in range(step // 8):
                squares = squares + x[i * 8:(i + 1) * 8]
    scale = lax.rsqrt(jnp.sum(squares, axis=0, keepdims=True) / channels + EPS)
    for ref, index in halves:
        for j in range(half // step):
            at = pl.multiple_of(index * half + j * step, step)
            x = ref[j * step:(j + 1) * step, :].astype(F32) * scale
            act[pl.ds(at, step), :] = gelu(x * gaincol[pl.ds(at, step), :1]).astype(BF16)
    rows, tokens = out_ref.shape[0], residual_ref.shape[0]
    means = window_means(0, rows, tokens, taps, positions, positions)
    out_ref[...] = dot_nt(means, act[...]).astype(BF16)
    middle = (taps // 2) * tokens
    residual_ref[...] = dot_nt(means[middle:middle + tokens], own_ref[...])


def conv_kernel(positions, windows_ref, residual_ref, halo_ref, gain_ref, weight_hbm, out_ref, weights, sems):
    taps, _, channels = weights.shape
    copies = [pltpu.make_async_copy(weight_hbm.at[t], weights.at[t], sems.at[t]) for t in range(taps)]
    ahead = 2
    for c in copies[:ahead]:
        c.start()
    tokens = out_ref.shape[0]
    h = halo_ref[...].astype(F32)
    h = h * lax.rsqrt(jnp.sum(h * h, axis=1, keepdims=True) / channels + EPS) * gain_ref[...]
    h = gelu(h).astype(BF16)
    total = residual_ref[...]
    for t in range(taps):
        window = windows_ref[t * tokens:(t + 1) * tokens]
        if t != taps // 2:
            edges = dot_nn(window_means(t * tokens, tokens, tokens, taps, positions, h.shape[0]), h)
            window = (window.astype(F32) + edges).astype(BF16)
        copies[t].wait()
        if t + ahead < taps:
            copies[t + ahead].start()
        total = total + dot_nt(window, weights[t])
    out_ref[...] = total.astype(BF16)


def block_owners():
    return owners(lax.axis_size("seq"), lax.axis_size("grp"))


def embed_kernel(pieces, pooled_ref, *refs):
    blocks, (out_ref, rest_ref) = refs[:pieces], refs[pieces:]
    half = pooled_ref.shape[1]
    for ref, owner in zip(blocks, block_owners()):
        out_ref[owner] = dot_nt(pooled_ref[...], ref[:, :half]).astype(BF16)
        rest_ref[owner] = ref[:, half:]


def keyvalue_kernel(part_ref, other_ref, gain_ref, weight_ref, kv_ref, normed_ref, embedded_ref):
    count, _, width = part_ref.shape
    e = (part_ref[...].astype(F32) + other_ref[...].astype(F32)).astype(BF16)
    embedded_ref[...] = e
    e = e.astype(F32)
    squares = jnp.sum(jnp.sum(e * e, axis=0), axis=1, keepdims=True)
    scale = lax.rsqrt(squares / (count * width) + EPS)
    normed_ref[...] = (e * scale[None] * gain_ref[...]).astype(BF16)
    total = 0.0
    for s in range(count):
        total = total + dot_nn(normed_ref[s], weight_ref[s])
    kv = total.T.astype(BF16)
    kv_ref[...] = kv


def later_blocks_of(refs):
    places = block_owners()
    per = len(places) // len(refs)
    rows = refs[0].shape[0] // per
    for i, place in enumerate(places):
        start = (i % per) * rows
        yield refs[i // per], slice(start, start + rows), place


def query_kernel(sides, *refs):
    normed, pieces, query_ref = refs[:sides], refs[sides:-1], refs[-1]
    features = query_ref.shape[1]
    tokens = normed[0].shape[1]
    totals = [0.0] * sides
    for ref, rows, place in later_blocks_of(pieces):
        weight = ref[rows, :features]
        totals = [t + dot_nn(n[place], weight) for t, n in zip(totals, normed)]
    for i, total in enumerate(totals):
        query_ref[i * tokens:(i + 1) * tokens] = (total * DK ** (-0.5)).astype(BF16)


def attend_kernel(query_ref, own_ref, other_ref, out_ref, keys, values):
    tokens, features = query_ref.shape
    blocks, _, each = own_ref.shape
    first = lax.axis_index("col") == 0
    for i in range(blocks):
        keys[:, i * each:(i + 1) * each] = jnp.where(first, own_ref[i][:DK], other_ref[i][:DK])
        values[:, i * each:(i + 1) * each] = jnp.where(first, other_ref[i], own_ref[i])
    for h in range(features // DK):
        scores = dot_nn(query_ref[:, h * DK:(h + 1) * DK], keys[...])
        weights = jnp.exp(scores - jnp.max(scores, axis=1, keepdims=True))
        total = jnp.sum(weights, axis=1, keepdims=True)
        out_ref[h] = (dot_nt(weights.astype(BF16), values[...]) / total).astype(BF16)


def output_kernel(sides, features, attended_ref, embedded_ref, pair_weight_ref, *refs):
    pieces, (keep_ref, give_ref, pair_ref, whole) = refs[:-4], refs[-4:]
    heads = attended_ref.shape[0]
    flat = jnp.concatenate([attended_ref[h] for h in range(heads)], axis=1)
    _, tokens, width = embedded_ref.shape
    col = lax.axis_index("col")
    share = jnp.where(col == 0, 1.0, 0.0)
    projected = 0.0
    for ref, rows, place in later_blocks_of(pieces):
        part = dot_nt(flat, ref[rows, features:])
        whole[place] = part.astype(BF16)
        pooled = jnp.mean(part.reshape(sides * tokens // PAIR_POOL, PAIR_POOL, width), axis=1)
        first = jnp.mean(embedded_ref[place].astype(F32).reshape(tokens // PAIR_POOL, PAIR_POOL, width), axis=1) * share
        if sides > 1:
            first = jnp.concatenate([first, jnp.zeros((pooled.shape[0] - first.shape[0], width), F32)], axis=0)
        weight = pair_weight_ref[pl.ds(pl.multiple_of(place * width, width), width)]
        projected = projected + dot_nn((pooled + first).astype(BF16), weight)
    pair_ref[...] = projected.astype(BF16)
    own = keep_ref.shape[1] // sides
    for i in range(sides):
        rows = slice(i * own, (i + 1) * own)
        keep_ref[:, rows] = whole[:, pl.ds(pl.multiple_of(i * tokens + col * own, own), own)]
        give_ref[:, rows] = whole[:, pl.ds(pl.multiple_of(i * tokens + (1 - col) * own, own), own)]


def token_kernel(embedded_ref, *refs):
    parts, token_ref = refs[:-1], refs[-1]
    own = token_ref.shape[0]
    mine = pl.ds(pl.multiple_of(lax.axis_index("col") * own, own), own)
    blocks = [
        embedded_ref[s, mine].astype(F32) + sum(part[s].astype(F32) for part in parts)
        for s in range(embedded_ref.shape[0])
    ]
    token_ref[...] = jnp.concatenate(blocks, axis=1).astype(BF16)


def pair_kernel(own_ref, all_ref, weight_ref, out_ref, columns_here):
    seq, col = lax.axis_index("seq"), lax.axis_index("col")
    features, each = weight_ref.shape[0], own_ref.shape[0]
    span = columns_here.shape[0] // each
    rows = all_ref[...].astype(F32)[:, features:]
    if rows.shape[0] == columns_here.shape[0]:
        for j in range(span):
            at = pl.multiple_of((j ^ (seq % span)) * each, each)
            columns_here[pl.ds(at, each)] = rows[j * each:(j + 1) * each]
    else:
        half = columns_here.shape[0]
        columns_here[...] = jnp.where(col == 0, rows[:half], rows[half:])
    rows_here = own_ref[...].astype(F32)[:, :features]
    hidden = gelu(rows_here[:, None, :] + columns_here[...][None, :, :])
    r, c, f = hidden.shape
    out_ref[...] = dot_nn(hidden.reshape(r * c, f).astype(BF16), weight_ref[...]).reshape(r, c, f).astype(BF16)


def cost(flops, size):
    return pl.CostEstimate(flops=int(flops), bytes_accessed=int(size), transcendentals=0)


def on_device(signal, conv_weight, conv_gain, embed_weight, attn_gain, query_weight, keyvalue_weight,
              output_weight, rowcol_weight, pair_weight):
    col = lax.axis_index("col")
    count, cols = lax.axis_size("seq"), lax.axis_size("col")
    positions, half = signal.shape
    taps, channels, _ = conv_weight.shape
    reach = taps // 2
    tokens = positions // POOL
    width = embed_weight.shape[1] * count
    features = query_weight.shape[1] // cols
    heads = features // DK
    swap = [(i, (i + 1) % cols) for i in range(cols)]
    shape = jax.ShapeDtypeStruct

    embed_own = jnp.concatenate(
        [embed_weight.T, lax.dynamic_slice_in_dim(keyvalue_weight, col * DK, DV, 1)], axis=1
    )
    ring = planned(count, lax.axis_size("grp")) and cols == 2
    sides = 2 if ring else 1
    side = lax.axis_index("seq") % sides
    pair_swap = [(i, i ^ 1) for i in range(count)]
    heads, features = heads // sides, features // sides

    def later_part(which):
        place = col * sides + which
        return jnp.concatenate(
            [
                lax.dynamic_slice_in_dim(query_weight, place * features, features, 1),
                lax.dynamic_slice_in_dim(output_weight.T, place * heads * DV, heads * DV, 1),
            ],
            axis=1,
        )

    e = Blocks(embed_own, count)

    signal_t = signal.T
    up = [(i, i + 1) for i in range(count - 1)]
    if ring:
        e.along("own", "step")
        e.across("own", "own2")
    other_t = lax.ppermute(signal_t, "col", swap)
    before = lax.ppermute(signal[positions - reach:], "seq", up)
    behind = lax.ppermute(signal[:reach], "seq", [(j, i) for i, j in up])
    if ring:
        before, behind = after((before, behind), e.at["step"], e.at["own2"])
    own_halo = jnp.pad(jnp.concatenate([before, behind], axis=0), ((0, 16 - 2 * reach), (0, 0)))
    other_halo = lax.ppermute(own_halo, "col", swap)
    halo = jnp.where(
        col == 0, jnp.concatenate([own_halo, other_halo], axis=1), jnp.concatenate([other_halo, own_halo], axis=1)
    )
    if ring:
        other_t = after(other_t, e.at["step"], e.at["own2"])
    gain_row = conv_gain.reshape(1, channels)
    windows, residual = pl.pallas_call(
        functools.partial(act_kernel, taps),
        out_shape=(shape((taps * tokens, channels), BF16), shape((tokens, half), F32)),
        in_specs=vspec(3),
        out_specs=vspec(2),
        scratch_shapes=[pltpu.VMEM((channels, positions), BF16), pltpu.VMEM((channels, 8), F32)],
        compiler_params=params(20),
        cost_estimate=cost(2 * taps * tokens * channels * positions, 4 * channels * positions),
        name="act",
    )(signal_t, other_t, gain_row)
    if ring:
        e.at["step"] = after(e.at["step"], e.at["own2"])
        e.along("step", "far")
        e.across("step", "step2")
        e.between("step", "cross")
    pooled = pl.pallas_call(
        functools.partial(conv_kernel, positions),
        out_shape=shape((tokens, half), BF16),
        in_specs=vspec(4) + hspec(1),
        out_specs=pl.BlockSpec(memory_space=VMEM),
        scratch_shapes=[pltpu.VMEM((taps, half, channels), BF16), pltpu.SemaphoreType.DMA((taps,))],
        compiler_params=params(50),
        cost_estimate=cost(2 * taps * tokens * channels * half, 2 * taps * channels * half),
        name="conv",
    )(windows, residual, halo, gain_row, conv_weight.transpose(0, 2, 1))
    if ring:
        e.at["far"] = after(e.at["far"], pooled, e.at["cross"])
        e.at["step2"] = after(e.at["step2"], pooled, e.at["cross"])
        e.along("step2", "far2")
        e.between("step2", "cross2")
        theirs = after(later_part(1 - side), pooled, e.at["cross"])
        received = lax.ppermute(theirs, "seq", pair_swap)
        pooled = after(pooled, received)
        q = Blocks(jnp.concatenate([later_part(side), received]), count)
        q.at["own"] = after(q.at["own"], e.at["far2"])
        q.along("own", "step")
        q.along("step", "far")
        q.between("step", "cross")
        embed_blocks = e.pieces()
        later_blocks = [q.at[name] for name in ("own", "step", "cross", "far")]
    else:
        embed_blocks, later_blocks = (
            [lax.all_gather(x, "seq", axis=0, tiled=True)] for x in (embed_own, later_part(0))
        )
    pieces = len(embed_blocks)
    block = width // pieces

    part, keyvalue_blocks = pl.pallas_call(
        functools.partial(embed_kernel, pieces),
        out_shape=(shape((pieces, tokens, block), BF16), shape((pieces, block, DV), BF16)),
        in_specs=vspec(1 + pieces),
        out_specs=vspec(2),
        compiler_params=params(12),
        cost_estimate=cost(2 * tokens * half * width, 2 * half * width),
        name="embed",
    )(pooled, *embed_blocks)
    other_part = lax.ppermute(part, "col", swap)

    keyvalue, normed, embedded = pl.pallas_call(
        keyvalue_kernel,
        out_shape=(
            shape((DV, tokens), BF16),
            shape((pieces, tokens, block), BF16),
            shape((pieces, tokens, block), BF16),
        ),
        in_specs=vspec(4),
        out_specs=vspec(3),
        compiler_params=params(16),
        cost_estimate=cost(2 * tokens * width * DV, 2 * width * DV),
        name="keyvalue",
    )(part, other_part, attn_gain.reshape(pieces, 1, block), keyvalue_blocks)
    both_normed = [normed]
    if ring:
        here = jnp.stack([keyvalue, lax.ppermute(keyvalue, "seq", pair_swap)])
        both_normed.append(lax.ppermute(normed, "seq", pair_swap))
        onward = [(2 * RING[k] + i, 2 * RING[(k + 1) % 4] + i) for k in range(4) for i in range(2)]
        opposite = [(2 * RING[k] + i, 2 * RING[(k + 2) % 4] + i) for k in range(4) for i in range(2)]
        turns = [onward, [(j, i) for i, j in onward], opposite]
        gathered = jnp.concatenate([here] + [lax.ppermute(here, "seq", turn) for turn in turns])
    else:
        gathered = lax.all_gather(keyvalue, "seq", axis=0)
    gathered_other = lax.ppermute(gathered, "col", swap)

    queries = pl.pallas_call(
        functools.partial(query_kernel, sides),
        out_shape=shape((sides * tokens, features), BF16),
        in_specs=vspec(sides + len(later_blocks)),
        out_specs=pl.BlockSpec(memory_space=VMEM),
        compiler_params=params(12),
        cost_estimate=cost(2 * sides * tokens * width * features, 2 * width * features),
        name="query",
    )(*both_normed, *later_blocks)

    attended = pl.pallas_call(
        attend_kernel,
        out_shape=shape((heads, sides * tokens, DV), BF16),
        in_specs=vspec(3),
        out_specs=pl.BlockSpec(memory_space=VMEM),
        scratch_shapes=[pltpu.VMEM((DK, count * tokens), BF16), pltpu.VMEM((DV, count * tokens), BF16)],
        compiler_params=params(24),
        cost_estimate=cost(2 * tokens * heads * count * tokens * (DK + DV), 4 * count * tokens * DV),
        name="attend",
    )(queries, gathered, gathered_other)

    out_width = rowcol_weight.shape[1]
    own_rows, pair_rows = tokens // cols, tokens // PAIR_POOL
    kept = shape((pieces, sides * own_rows, block), BF16)
    keep, give, part_pair = pl.pallas_call(
        functools.partial(output_kernel, sides, features),
        out_shape=(kept, kept, shape((sides * pair_rows, out_width), BF16)),
        in_specs=vspec(3 + len(later_blocks)),
        out_specs=vspec(3),
        scratch_shapes=[pltpu.VMEM((pieces, sides * tokens, block), BF16)],
        compiler_params=params(16),
        cost_estimate=cost(2 * sides * tokens * heads * DV * width, 2 * heads * DV * width),
        name="output",
    )(attended, embedded, rowcol_weight, *later_blocks)

    def total(*parts):
        return sum(x.astype(F32) for x in parts).astype(BF16)

    if ring:
        turned = lax.ppermute(part_pair, "seq", pair_swap)
        part_pair = total(part_pair, jnp.concatenate([turned[pair_rows:], turned[:pair_rows]]))
    projected = total(part_pair, lax.ppermute(part_pair, "col", swap))
    sums = total(keep, lax.ppermute(give, "col", swap))

    if ring:
        rows_all = after(projected, sums)
        rows_all = jnp.concatenate([rows_all, lax.ppermute(rows_all, "seq", [(i, i ^ 2) for i in range(count)])])
        pairs = [(i * cols + i // 4, (i ^ 4) * cols + i // 4) for i in range(count)]
        far_rows = lax.ppermute(rows_all, ("seq", "col"), pairs)
        rows_all = jnp.where(lax.axis_index("seq") // 4 == col, rows_all, far_rows)
    else:
        rows_all = lax.all_gather(projected, "seq", axis=0, tiled=True)

    parts = [sums[:, :own_rows]]
    if ring:
        parts.append(after(lax.ppermute(sums[:, own_rows:], "seq", pair_swap), far_rows))
    out_tokens = pl.pallas_call(
        token_kernel,
        out_shape=shape((own_rows, width), BF16),
        in_specs=vspec(1 + len(parts)),
        out_specs=pl.BlockSpec(memory_space=VMEM),
        compiler_params=params(12),
        cost_estimate=cost(3 * own_rows * width, 8 * own_rows * width),
        name="tokens",
    )(embedded, *parts)

    span = pair_rows * count // cols
    pair_features = pair_weight.shape[0]
    pair_out = pl.pallas_call(
        pair_kernel,
        out_shape=shape((pair_rows, span, pair_features), BF16),
        in_specs=vspec(3),
        out_specs=pl.BlockSpec(memory_space=VMEM),
        scratch_shapes=[pltpu.VMEM((span, pair_features), F32)],
        compiler_params=params(16),
        cost_estimate=cost(2 * pair_rows * span * pair_features**2, 2 * pair_rows * span * pair_features),
        name="pair",
    )(projected[:pair_rows], rows_all, pair_weight)
    return out_tokens, pair_out


def solution(mesh):
    placed = (
        P(("grp", "seq"), "col"),
        P(None, None, "col"),
        P(),
        P("col", "seq"),
        P(),
        P("seq", None),
        P("seq", None),
        P(None, "seq"),
        P(),
        P(),
    )
    return jax.shard_map(
        on_device,
        mesh=mesh,
        in_specs=placed,
        out_specs=(P(("grp", "seq", "col"), None), P(("grp", "seq"), "col", None)),
        check_vma=False,
    )
```

```python
import functools
import math

import jax
import jax.numpy as jnp
from jax import lax
from jax.experimental import pallas as pl
from jax.experimental.pallas import tpu as pltpu
from jax.sharding import PartitionSpec as P

DK = 128
DV = 192
POOL = 4
PAIR_POOL = 16
EPS = 1e-06
VMEM = pltpu.VMEM
F32 = jnp.float32
BF16 = jnp.bfloat16


def gelu(x):
    c = math.sqrt(2.0 / math.pi)
    half = 0.5 * x
    return half + half * jnp.tanh(x * (c + (0.044715 * c) * (x * x)))


def dot_nt(a, b):
    return lax.dot_general(a, b, (((1,), (1,)), ((), ())), preferred_element_type=F32)


def dot_nn(a, b):
    return lax.dot_general(a, b, (((1,), (0,)), ((), ())), preferred_element_type=F32)


def params(mib, **kw):
    return pltpu.CompilerParams(vmem_limit_bytes=mib << 20, **kw)


def vspec(n):
    return [pl.BlockSpec(memory_space=VMEM)] * n


def hspec(n):
    return [pl.BlockSpec(memory_space=pltpu.HBM)] * n


RING = (0, 1, 3, 2)


def planned(count, groups):
    return count == 2 * len(RING) and groups == 2


def pick(index, table):
    value = jnp.int32(table[0])
    for i, entry in enumerate(table[1:], 1):
        value = jnp.where(index == i, jnp.int32(entry), value)
    return value


def owners(count, groups):
    if not planned(count, groups):
        return [jnp.int32(0)]
    group, me = lax.axis_index("grp"), lax.axis_index("seq")
    side, place = me % 2, pick(me // 2, [RING.index(i) for i in range(4)])
    result = []
    for step in (0, 3 + 2 * group, 1 + 2 * group, 2):
        row = pick(lax.rem(place + step, 4), RING)
        result += [2 * row + side, 2 * row + 1 - side]
    return result


class Blocks:
    def __init__(self, own, count):
        self.count = count
        self.at = {"own": own}

    def along(self, source, target):
        pairs = []
        for group in range(2):
            for k in range(4):
                a, b = RING[k], RING[(k + 1) % 4]
                if group:
                    a, b = b, a
                pairs += [(group * self.count + 2 * a + i, group * self.count + 2 * b + i) for i in range(2)]
        self.at[target] = lax.ppermute(self.at[source], ("grp", "seq"), pairs)

    def across(self, source, target):
        self.at[target] = lax.ppermute(self.at[source], "seq", [(i, i ^ 1) for i in range(self.count)])

    def between(self, source, target):
        self.at[target] = lax.ppermute(self.at[source], "grp", [(0, 1), (1, 0)])

    def pieces(self):
        names = ("own", "own2", "step", "step2", "cross", "cross2", "far", "far2")
        return [self.at[name] for name in names]


def after(values, *done):
    return lax.optimization_barrier((values, done))[0]


def window_means(first_row, rows, tokens, taps, positions, columns):
    r = lax.broadcasted_iota(jnp.int32, (rows, columns), 0) + first_row
    k = lax.broadcasted_iota(jnp.int32, (rows, columns), 1)
    reach = taps // 2
    if columns != positions:
        k = jnp.where(k < 2 * reach, jnp.where(k < reach, k - reach, k - reach + positions), -positions)
    tap = r // tokens
    gap = k - (POOL * (r - tap * tokens) + tap - reach)
    return jnp.where((gap >= 0) & (gap < POOL), 1.0 / POOL, 0.0).astype(BF16)


def act_kernel(taps, own_ref, other_ref, gain_ref, out_ref, residual_ref, act, gaincol):
    channels, positions = act.shape
    half = own_ref.shape[0]
    col = lax.axis_index("col")
    gaincol[...] = jnp.broadcast_to(gain_ref[...], (8, channels)).T
    step = 64
    halves = ((own_ref, col), (other_ref, 1 - col))
    squares = jnp.zeros((8, positions), F32)
    for ref, _ in halves:
        for j in range(half // step):
            x = ref[j * step:(j + 1) * step, :].astype(F32)
            x = x * x
            for i in range(step // 8):
                squares = squares + x[i * 8:(i + 1) * 8]
    scale = lax.rsqrt(jnp.sum(squares, axis=0, keepdims=True) / channels + EPS)
    for ref, index in halves:
        for j in range(half // step):
            at = pl.multiple_of(index * half + j * step, step)
            x = ref[j * step:(j + 1) * step, :].astype(F32) * scale
            act[pl.ds(at, step), :] = gelu(x * gaincol[pl.ds(at, step), :1]).astype(BF16)
    rows, tokens = out_ref.shape[0], residual_ref.shape[0]
    means = window_means(0, rows, tokens, taps, positions, positions)
    out_ref[...] = dot_nt(means, act[...]).astype(BF16)
    middle = (taps // 2) * tokens
    residual_ref[...] = dot_nt(means[middle:middle + tokens], own_ref[...])


def conv_kernel(positions, windows_ref, residual_ref, halo_ref, gain_ref, weight_hbm, out_ref, weights, sems):
    taps, _, channels = weights.shape
    copies = [pltpu.make_async_copy(weight_hbm.at[t], weights.at[t], sems.at[t]) for t in range(taps)]
    ahead = 2
    for c in copies[:ahead]:
        c.start()
    tokens = out_ref.shape[0]
    h = halo_ref[...].astype(F32)
    h = h * lax.rsqrt(jnp.sum(h * h, axis=1, keepdims=True) / channels + EPS) * gain_ref[...]
    h = gelu(h).astype(BF16)
    total = residual_ref[...]
    for t in range(taps):
        window = windows_ref[t * tokens:(t + 1) * tokens]
        if t != taps // 2:
            edges = dot_nn(window_means(t * tokens, tokens, tokens, taps, positions, h.shape[0]), h)
            window = (window.astype(F32) + edges).astype(BF16)
        copies[t].wait()
        if t + ahead < taps:
            copies[t + ahead].start()
        total = total + dot_nt(window, weights[t])
    out_ref[...] = total.astype(BF16)


def block_owners():
    return owners(lax.axis_size("seq"), lax.axis_size("grp"))


def embed_kernel(pieces, pooled_ref, *refs):
    blocks, (out_ref, rest_ref) = refs[:pieces], refs[pieces:]
    half = pooled_ref.shape[1]
    for ref, owner in zip(blocks, block_owners()):
        out_ref[owner] = dot_nt(pooled_ref[...], ref[:, :half]).astype(BF16)
        rest_ref[owner] = ref[:, half:]


def keyvalue_kernel(part_ref, other_ref, gain_ref, weight_ref, kv_ref, normed_ref, embedded_ref):
    count, _, width = part_ref.shape
    e = (part_ref[...].astype(F32) + other_ref[...].astype(F32)).astype(BF16)
    embedded_ref[...] = e
    e = e.astype(F32)
    squares = jnp.sum(jnp.sum(e * e, axis=0), axis=1, keepdims=True)
    scale = lax.rsqrt(squares / (count * width) + EPS)
    normed_ref[...] = (e * scale[None] * gain_ref[...]).astype(BF16)
    total = 0.0
    for s in range(count):
        total = total + dot_nn(normed_ref[s], weight_ref[s])
    kv = total.T.astype(BF16)
    kv_ref[...] = kv


def later_blocks_of(refs):
    places = block_owners()
    per = len(places) // len(refs)
    rows = refs[0].shape[0] // per
    for i, place in enumerate(places):
        start = (i % per) * rows
        yield refs[i // per], slice(start, start + rows), place


def query_kernel(sides, *refs):
    normed, pieces, query_ref = refs[:sides], refs[sides:-1], refs[-1]
    features = query_ref.shape[1]
    tokens = normed[0].shape[1]
    totals = [0.0] * sides
    for ref, rows, place in later_blocks_of(pieces):
        weight = ref[rows, :features]
        totals = [t + dot_nn(n[place], weight) for t, n in zip(totals, normed)]
    for i, total in enumerate(totals):
        query_ref[i * tokens:(i + 1) * tokens] = (total * DK ** (-0.5)).astype(BF16)


def attend_kernel(query_ref, own_ref, other_ref, out_ref, keys, values):
    tokens, features = query_ref.shape
    blocks, _, each = own_ref.shape
    first = lax.axis_index("col") == 0
    for i in range(blocks):
        keys[:, i * each:(i + 1) * each] = jnp.where(first, own_ref[i][:DK], other_ref[i][:DK])
        values[:, i * each:(i + 1) * each] = jnp.where(first, other_ref[i], own_ref[i])
    for h in range(features // DK):
        scores = dot_nn(query_ref[:, h * DK:(h + 1) * DK], keys[...])
        weights = jnp.exp(scores - jnp.max(scores, axis=1, keepdims=True))
        total = jnp.sum(weights, axis=1, keepdims=True)
        out_ref[h] = (dot_nt(weights.astype(BF16), values[...]) / total).astype(BF16)


def output_kernel(sides, features, attended_ref, embedded_ref, pair_weight_ref, *refs):
    pieces, (keep_ref, give_ref, pair_ref, whole) = refs[:-4], refs[-4:]
    heads = attended_ref.shape[0]
    flat = jnp.concatenate([attended_ref[h] for h in range(heads)], axis=1)
    _, tokens, width = embedded_ref.shape
    col = lax.axis_index("col")
    share = jnp.where(col == 0, 1.0, 0.0)
    projected = 0.0
    for ref, rows, place in later_blocks_of(pieces):
        part = dot_nt(flat, ref[rows, features:])
        whole[place] = part.astype(BF16)
        pooled = jnp.mean(part.reshape(sides * tokens // PAIR_POOL, PAIR_POOL, width), axis=1)
        first = jnp.mean(embedded_ref[place].astype(F32).reshape(tokens // PAIR_POOL, PAIR_POOL, width), axis=1) * share
        if sides > 1:
            first = jnp.concatenate([first, jnp.zeros((pooled.shape[0] - first.shape[0], width), F32)], axis=0)
        weight = pair_weight_ref[pl.ds(pl.multiple_of(place * width, width), width)]
        projected = projected + dot_nn((pooled + first).astype(BF16), weight)
    pair_ref[...] = projected.astype(BF16)
    own = keep_ref.shape[1] // sides
    for i in range(sides):
        rows = slice(i * own, (i + 1) * own)
        keep_ref[:, rows] = whole[:, pl.ds(pl.multiple_of(i * tokens + col * own, own), own)]
        give_ref[:, rows] = whole[:, pl.ds(pl.multiple_of(i * tokens + (1 - col) * own, own), own)]


def token_kernel(embedded_ref, *refs):
    parts, token_ref = refs[:-1], refs[-1]
    own = token_ref.shape[0]
    mine = pl.ds(pl.multiple_of(lax.axis_index("col") * own, own), own)
    blocks = [
        embedded_ref[s, mine].astype(F32) + sum(part[s].astype(F32) for part in parts)
        for s in range(embedded_ref.shape[0])
    ]
    token_ref[...] = jnp.concatenate(blocks, axis=1).astype(BF16)


def pair_kernel(own_ref, all_ref, weight_ref, out_ref, columns_here):
    seq, col = lax.axis_index("seq"), lax.axis_index("col")
    features, each = weight_ref.shape[0], own_ref.shape[0]
    span = columns_here.shape[0] // each
    rows = all_ref[...].astype(F32)[:, features:]
    if rows.shape[0] == columns_here.shape[0]:
        for j in range(span):
            at = pl.multiple_of((j ^ (seq % span)) * each, each)
            columns_here[pl.ds(at, each)] = rows[j * each:(j + 1) * each]
    else:
        half = columns_here.shape[0]
        columns_here[...] = jnp.where(col == 0, rows[:half], rows[half:])
    rows_here = own_ref[...].astype(F32)[:, :features]
    hidden = gelu(rows_here[:, None, :] + columns_here[...][None, :, :])
    r, c, f = hidden.shape
    out_ref[...] = dot_nn(hidden.reshape(r * c, f).astype(BF16), weight_ref[...]).reshape(r, c, f).astype(BF16)


def cost(flops, size):
    return pl.CostEstimate(flops=int(flops), bytes_accessed=int(size), transcendentals=0)


def on_device(signal, conv_weight, conv_gain, embed_weight, attn_gain, query_weight, keyvalue_weight,
              output_weight, rowcol_weight, pair_weight):
    col = lax.axis_index("col")
    count, cols = lax.axis_size("seq"), lax.axis_size("col")
    positions, half = signal.shape
    taps, channels, _ = conv_weight.shape
    reach = taps // 2
    tokens = positions // POOL
    width = embed_weight.shape[1] * count
    features = query_weight.shape[1] // cols
    heads = features // DK
    swap = [(i, (i + 1) % cols) for i in range(cols)]
    shape = jax.ShapeDtypeStruct

    embed_own = jnp.concatenate(
        [embed_weight.T, lax.dynamic_slice_in_dim(keyvalue_weight, col * DK, DV, 1)], axis=1
    )
    ring = planned(count, lax.axis_size("grp")) and cols == 2
    sides = 2 if ring else 1
    side = lax.axis_index("seq") % sides
    pair_swap = [(i, i ^ 1) for i in range(count)]
    heads, features = heads // sides, features // sides

    def later_part(which):
        place = col * sides + which
        return jnp.concatenate(
            [
                lax.dynamic_slice_in_dim(query_weight, place * features, features, 1),
                lax.dynamic_slice_in_dim(output_weight.T, place * heads * DV, heads * DV, 1),
            ],
            axis=1,
        )

    e = Blocks(embed_own, count)

    signal_t = signal.T
    up = [(i, i + 1) for i in range(count - 1)]
    if ring:
        e.along("own", "step")
        e.across("own", "own2")
    other_t = lax.ppermute(signal_t, "col", swap)
    before = lax.ppermute(signal[positions - reach:], "seq", up)
    behind = lax.ppermute(signal[:reach], "seq", [(j, i) for i, j in up])
    if ring:
        other_t = after(other_t, e.at["step"], e.at["own2"])
    gain_row = conv_gain.reshape(1, channels)
    windows, residual = pl.pallas_call(
        functools.partial(act_kernel, taps),
        out_shape=(shape((taps * tokens, channels), BF16), shape((tokens, half), F32)),
        in_specs=vspec(3),
        out_specs=vspec(2),
        scratch_shapes=[pltpu.VMEM((channels, positions), BF16), pltpu.VMEM((channels, 8), F32)],
        compiler_params=params(20),
        cost_estimate=cost(2 * taps * tokens * channels * positions, 4 * channels * positions),
        name="act",
    )(signal_t, other_t, gain_row)
    if ring:
        before, behind = after((before, behind), windows)
    own_halo = jnp.pad(jnp.concatenate([before, behind], axis=0), ((0, 16 - 2 * reach), (0, 0)))
    other_halo = lax.ppermute(own_halo, "col", swap)
    halo = jnp.where(
        col == 0, jnp.concatenate([own_halo, other_halo], axis=1), jnp.concatenate([other_halo, own_halo], axis=1)
    )
    if ring:
        e.at["step"] = after(e.at["step"], e.at["own2"])
        e.along("step", "far")
        e.across("step", "step2")
        e.between("step", "cross")
    pooled = pl.pallas_call(
        functools.partial(conv_kernel, positions),
        out_shape=shape((tokens, half), BF16),
        in_specs=vspec(4) + hspec(1),
        out_specs=pl.BlockSpec(memory_space=VMEM),
        scratch_shapes=[pltpu.VMEM((taps, half, channels), BF16), pltpu.SemaphoreType.DMA((taps,))],
        compiler_params=params(50),
        cost_estimate=cost(2 * taps * tokens * channels * half, 2 * taps * channels * half),
        name="conv",
    )(windows, residual, halo, gain_row, conv_weight.transpose(0, 2, 1))
    if ring:
        e.at["far"] = after(e.at["far"], pooled, e.at["cross"])
        e.at["step2"] = after(e.at["step2"], pooled, e.at["cross"])
        e.along("step2", "far2")
        e.between("step2", "cross2")
        theirs = after(later_part(1 - side), pooled, e.at["cross"])
        received = lax.ppermute(theirs, "seq", pair_swap)
        pooled = after(pooled, received)
        q = Blocks(jnp.concatenate([later_part(side), received]), count)
        q.at["own"] = after(q.at["own"], e.at["far2"])
        q.along("own", "step")
        q.along("step", "far")
        q.between("step", "cross")
        embed_blocks = e.pieces()
        later_blocks = [q.at[name] for name in ("own", "step", "cross", "far")]
    else:
        embed_blocks, later_blocks = (
            [lax.all_gather(x, "seq", axis=0, tiled=True)] for x in (embed_own, later_part(0))
        )
    pieces = len(embed_blocks)
    block = width // pieces

    part, keyvalue_blocks = pl.pallas_call(
        functools.partial(embed_kernel, pieces),
        out_shape=(shape((pieces, tokens, block), BF16), shape((pieces, block, DV), BF16)),
        in_specs=vspec(1 + pieces),
        out_specs=vspec(2),
        compiler_params=params(12),
        cost_estimate=cost(2 * tokens * half * width, 2 * half * width),
        name="embed",
    )(pooled, *embed_blocks)
    other_part = lax.ppermute(part, "col", swap)

    keyvalue, normed, embedded = pl.pallas_call(
        keyvalue_kernel,
        out_shape=(
            shape((DV, tokens), BF16),
            shape((pieces, tokens, block), BF16),
            shape((pieces, tokens, block), BF16),
        ),
        in_specs=vspec(4),
        out_specs=vspec(3),
        compiler_params=params(16),
        cost_estimate=cost(2 * tokens * width * DV, 2 * width * DV),
        name="keyvalue",
    )(part, other_part, attn_gain.reshape(pieces, 1, block), keyvalue_blocks)
    both_normed = [normed]
    if ring:
        both_normed.append(lax.ppermute(normed, "seq", pair_swap))
        turns = [[(2 * RING[k] + i, 2 * RING[(k + t) % 4] + i) for k in range(4) for i in range(2)] for t in (1, 3, 2)]
        row = jnp.stack([keyvalue] + [lax.ppermute(keyvalue, "seq", turn) for turn in turns])
        gathered = jnp.concatenate([row, lax.ppermute(row, "seq", pair_swap)])
    else:
        gathered = lax.all_gather(keyvalue, "seq", axis=0)
    gathered_other = lax.ppermute(gathered, "col", swap)

    queries = pl.pallas_call(
        functools.partial(query_kernel, sides),
        out_shape=shape((sides * tokens, features), BF16),
        in_specs=vspec(sides + len(later_blocks)),
        out_specs=pl.BlockSpec(memory_space=VMEM),
        compiler_params=params(12),
        cost_estimate=cost(2 * sides * tokens * width * features, 2 * width * features),
        name="query",
    )(*both_normed, *later_blocks)

    attended = pl.pallas_call(
        attend_kernel,
        out_shape=shape((heads, sides * tokens, DV), BF16),
        in_specs=vspec(3),
        out_specs=pl.BlockSpec(memory_space=VMEM),
        scratch_shapes=[pltpu.VMEM((DK, count * tokens), BF16), pltpu.VMEM((DV, count * tokens), BF16)],
        compiler_params=params(24),
        cost_estimate=cost(2 * tokens * heads * count * tokens * (DK + DV), 4 * count * tokens * DV),
        name="attend",
    )(queries, gathered, gathered_other)

    out_width = rowcol_weight.shape[1]
    own_rows, pair_rows = tokens // cols, tokens // PAIR_POOL
    kept = shape((pieces, sides * own_rows, block), BF16)
    keep, give, part_pair = pl.pallas_call(
        functools.partial(output_kernel, sides, features),
        out_shape=(kept, kept, shape((sides * pair_rows, out_width), BF16)),
        in_specs=vspec(3 + len(later_blocks)),
        out_specs=vspec(3),
        scratch_shapes=[pltpu.VMEM((pieces, sides * tokens, block), BF16)],
        compiler_params=params(16),
        cost_estimate=cost(2 * sides * tokens * heads * DV * width, 2 * heads * DV * width),
        name="output",
    )(attended, embedded, rowcol_weight, *later_blocks)

    def total(*parts):
        return sum(x.astype(F32) for x in parts).astype(BF16)

    if ring:
        turned = lax.ppermute(part_pair, "seq", pair_swap)
        part_pair = total(part_pair, jnp.concatenate([turned[pair_rows:], turned[:pair_rows]]))
    projected = total(part_pair, lax.ppermute(part_pair, "col", swap))
    sums = total(keep, lax.ppermute(give, "col", swap))

    if ring:
        sent = sums[:, own_rows:]
        rows_all = after(projected, sent)
        rows_all = jnp.concatenate([rows_all, lax.ppermute(rows_all, "seq", [(i, i ^ 2) for i in range(count)])])
        pairs = [(i * cols + i // 4, (i ^ 4) * cols + i // 4) for i in range(count)]
        far_rows = lax.ppermute(rows_all, ("seq", "col"), pairs)
        rows_all = jnp.where(lax.axis_index("seq") // 4 == col, rows_all, far_rows)
    else:
        rows_all = lax.all_gather(projected, "seq", axis=0, tiled=True)

    parts = [sums[:, :own_rows]]
    if ring:
        parts.append(lax.ppermute(sent, "seq", pair_swap))
    out_tokens = pl.pallas_call(
        token_kernel,
        out_shape=shape((own_rows, width), BF16),
        in_specs=vspec(1 + len(parts)),
        out_specs=pl.BlockSpec(memory_space=VMEM),
        compiler_params=params(12),
        cost_estimate=cost(3 * own_rows * width, 8 * own_rows * width),
        name="tokens",
    )(embedded, *parts)

    span = pair_rows * count // cols
    pair_features = pair_weight.shape[0]
    pair_out = pl.pallas_call(
        pair_kernel,
        out_shape=shape((pair_rows, span, pair_features), BF16),
        in_specs=vspec(3),
        out_specs=pl.BlockSpec(memory_space=VMEM),
        scratch_shapes=[pltpu.VMEM((span, pair_features), F32)],
        compiler_params=params(16),
        cost_estimate=cost(2 * pair_rows * span * pair_features**2, 2 * pair_rows * span * pair_features),
        name="pair",
    )(after(projected[:pair_rows], out_tokens), rows_all, pair_weight)
    return out_tokens, pair_out


def solution(mesh):
    placed = (
        P(("grp", "seq"), "col"),
        P(None, None, "col"),
        P(),
        P("col", "seq"),
        P(),
        P("seq", None),
        P("seq", None),
        P(None, "seq"),
        P(),
        P(),
    )
    return jax.shard_map(
        on_device,
        mesh=mesh,
        in_specs=placed,
        out_specs=(P(("grp", "seq", "col"), None), P(("grp", "seq"), "col", None)),
        check_vma=False,
    )
```

```python
import functools
import math

import jax
import jax.numpy as jnp
from jax import lax
from jax.experimental import pallas as pl
from jax.experimental.pallas import tpu as pltpu
from jax.sharding import PartitionSpec as P

DK = 128
DV = 192
POOL = 4
PAIR_POOL = 16
EPS = 1e-06
VMEM = pltpu.VMEM
F32 = jnp.float32
BF16 = jnp.bfloat16


def gelu(x):
    c = math.sqrt(2.0 / math.pi)
    half = 0.5 * x
    return half + half * jnp.tanh(x * (c + (0.044715 * c) * (x * x)))


def dot_nt(a, b):
    return lax.dot_general(a, b, (((1,), (1,)), ((), ())), preferred_element_type=F32)


def dot_nn(a, b):
    return lax.dot_general(a, b, (((1,), (0,)), ((), ())), preferred_element_type=F32)


def params(mib, **kw):
    return pltpu.CompilerParams(vmem_limit_bytes=mib << 20, **kw)


def vspec(n):
    return [pl.BlockSpec(memory_space=VMEM)] * n


def hspec(n):
    return [pl.BlockSpec(memory_space=pltpu.HBM)] * n


RING = (0, 1, 3, 2)


def planned(count, groups):
    return count == 2 * len(RING) and groups == 2


def pick(index, table):
    value = jnp.int32(table[0])
    for i, entry in enumerate(table[1:], 1):
        value = jnp.where(index == i, jnp.int32(entry), value)
    return value


def owners(count, groups):
    if not planned(count, groups):
        return [jnp.int32(0)]
    group, me = lax.axis_index("grp"), lax.axis_index("seq")
    side, place = me % 2, pick(me // 2, [RING.index(i) for i in range(4)])
    result = []
    for step in (0, 3 + 2 * group, 1 + 2 * group, 2):
        row = pick(lax.rem(place + step, 4), RING)
        result += [2 * row + side, 2 * row + 1 - side]
    return result


class Blocks:
    def __init__(self, own, count):
        self.count = count
        self.at = {"own": own}

    def along(self, source, target):
        pairs = []
        for group in range(2):
            for k in range(4):
                a, b = RING[k], RING[(k + 1) % 4]
                if group:
                    a, b = b, a
                pairs += [(group * self.count + 2 * a + i, group * self.count + 2 * b + i) for i in range(2)]
        self.at[target] = lax.ppermute(self.at[source], ("grp", "seq"), pairs)

    def across(self, source, target):
        self.at[target] = lax.ppermute(self.at[source], "seq", [(i, i ^ 1) for i in range(self.count)])

    def between(self, source, target):
        self.at[target] = lax.ppermute(self.at[source], "grp", [(0, 1), (1, 0)])

    def pieces(self):
        names = ("own", "own2", "step", "step2", "cross", "cross2", "far", "far2")
        return [self.at[name] for name in names]


def after(values, *done):
    return lax.optimization_barrier((values, done))[0]


def window_means(first_row, rows, tokens, taps, positions, columns):
    r = lax.broadcasted_iota(jnp.int32, (rows, columns), 0) + first_row
    k = lax.broadcasted_iota(jnp.int32, (rows, columns), 1)
    reach = taps // 2
    if columns != positions:
        k = jnp.where(k < 2 * reach, jnp.where(k < reach, k - reach, k - reach + positions), -positions)
    tap = r // tokens
    gap = k - (POOL * (r - tap * tokens) + tap - reach)
    return jnp.where((gap >= 0) & (gap < POOL), 1.0 / POOL, 0.0).astype(BF16)


def act_kernel(taps, own_ref, other_ref, gain_ref, out_ref, residual_ref, act, gaincol):
    channels, positions = act.shape
    half = own_ref.shape[0]
    col = lax.axis_index("col")
    gaincol[...] = jnp.broadcast_to(gain_ref[...], (8, channels)).T
    step = 64
    halves = ((own_ref, col), (other_ref, 1 - col))
    squares = jnp.zeros((8, positions), F32)
    for ref, _ in halves:
        for j in range(half // step):
            x = ref[j * step:(j + 1) * step, :].astype(F32)
            x = x * x
            for i in range(step // 8):
                squares = squares + x[i * 8:(i + 1) * 8]
    scale = lax.rsqrt(jnp.sum(squares, axis=0, keepdims=True) / channels + EPS)
    for ref, index in halves:
        for j in range(half // step):
            at = pl.multiple_of(index * half + j * step, step)
            x = ref[j * step:(j + 1) * step, :].astype(F32) * scale
            act[pl.ds(at, step), :] = gelu(x * gaincol[pl.ds(at, step), :1]).astype(BF16)
    rows, tokens = out_ref.shape[0], residual_ref.shape[0]
    means = window_means(0, rows, tokens, taps, positions, positions)
    out_ref[...] = dot_nt(means, act[...]).astype(BF16)
    middle = (taps // 2) * tokens
    residual_ref[...] = dot_nt(means[middle:middle + tokens], own_ref[...])


def conv_kernel(positions, windows_ref, residual_ref, halo_ref, gain_ref, weight_hbm, out_ref, weights, sems):
    taps, _, channels = weights.shape
    copies = [pltpu.make_async_copy(weight_hbm.at[t], weights.at[t], sems.at[t]) for t in range(taps)]
    ahead = 2
    for c in copies[:ahead]:
        c.start()
    tokens = out_ref.shape[0]
    h = halo_ref[...].astype(F32)
    h = h * lax.rsqrt(jnp.sum(h * h, axis=1, keepdims=True) / channels + EPS) * gain_ref[...]
    h = gelu(h).astype(BF16)
    total = residual_ref[...]
    for t in range(taps):
        window = windows_ref[t * tokens:(t + 1) * tokens]
        if t != taps // 2:
            edges = dot_nn(window_means(t * tokens, tokens, tokens, taps, positions, h.shape[0]), h)
            window = (window.astype(F32) + edges).astype(BF16)
        copies[t].wait()
        if t + ahead < taps:
            copies[t + ahead].start()
        total = total + dot_nt(window, weights[t])
    out_ref[...] = total.astype(BF16)


def block_owners():
    return owners(lax.axis_size("seq"), lax.axis_size("grp"))


def embed_kernel(pieces, pooled_ref, *refs):
    blocks, (out_ref, rest_ref) = refs[:pieces], refs[pieces:]
    half = pooled_ref.shape[1]
    for ref, owner in zip(blocks, block_owners()):
        out_ref[owner] = dot_nt(pooled_ref[...], ref[:, :half]).astype(BF16)
        rest_ref[owner] = ref[:, half:]


def keyvalue_kernel(part_ref, other_ref, gain_ref, weight_ref, kv_ref, normed_ref, embedded_ref):
    count, _, width = part_ref.shape
    e = (part_ref[...].astype(F32) + other_ref[...].astype(F32)).astype(BF16)
    embedded_ref[...] = e
    e = e.astype(F32)
    squares = jnp.sum(jnp.sum(e * e, axis=0), axis=1, keepdims=True)
    scale = lax.rsqrt(squares / (count * width) + EPS)
    normed_ref[...] = (e * scale[None] * gain_ref[...]).astype(BF16)
    total = 0.0
    for s in range(count):
        total = total + dot_nn(normed_ref[s], weight_ref[s])
    kv = total.T.astype(BF16)
    kv_ref[...] = kv


def later_blocks_of(refs):
    places = block_owners()
    per = len(places) // len(refs)
    rows = refs[0].shape[0] // per
    for i, place in enumerate(places):
        start = (i % per) * rows
        yield refs[i // per], slice(start, start + rows), place


def query_kernel(sides, *refs):
    normed, pieces, query_ref = refs[:sides], refs[sides:-1], refs[-1]
    features = query_ref.shape[1]
    tokens = normed[0].shape[1]
    totals = [0.0] * sides
    for ref, rows, place in later_blocks_of(pieces):
        weight = ref[rows, :features]
        totals = [t + dot_nn(n[place], weight) for t, n in zip(totals, normed)]
    for i, total in enumerate(totals):
        query_ref[i * tokens:(i + 1) * tokens] = (total * DK ** (-0.5)).astype(BF16)


def attend_kernel(query_ref, own_ref, other_ref, out_ref, keys, values):
    tokens, features = query_ref.shape
    blocks, _, each = own_ref.shape
    first = lax.axis_index("col") == 0
    for i in range(blocks):
        keys[:, i * each:(i + 1) * each] = jnp.where(first, own_ref[i][:DK], other_ref[i][:DK])
        values[:, i * each:(i + 1) * each] = jnp.where(first, other_ref[i], own_ref[i])
    for h in range(features // DK):
        scores = dot_nn(query_ref[:, h * DK:(h + 1) * DK], keys[...])
        weights = jnp.exp(scores - jnp.max(scores, axis=1, keepdims=True))
        total = jnp.sum(weights, axis=1, keepdims=True)
        out_ref[h] = (dot_nt(weights.astype(BF16), values[...]) / total).astype(BF16)


def output_kernel(sides, features, attended_ref, embedded_ref, pair_weight_ref, *refs):
    pieces, (keep_ref, give_ref, pair_ref, whole) = refs[:-4], refs[-4:]
    heads = attended_ref.shape[0]
    flat = jnp.concatenate([attended_ref[h] for h in range(heads)], axis=1)
    _, tokens, width = embedded_ref.shape
    col = lax.axis_index("col")
    share = jnp.where(col == 0, 1.0, 0.0)
    projected = 0.0
    for ref, rows, place in later_blocks_of(pieces):
        part = dot_nt(flat, ref[rows, features:])
        whole[place] = part.astype(BF16)
        pooled = jnp.mean(part.reshape(sides * tokens // PAIR_POOL, PAIR_POOL, width), axis=1)
        first = jnp.mean(embedded_ref[place].astype(F32).reshape(tokens // PAIR_POOL, PAIR_POOL, width), axis=1) * share
        if sides > 1:
            first = jnp.concatenate([first, jnp.zeros((pooled.shape[0] - first.shape[0], width), F32)], axis=0)
        weight = pair_weight_ref[pl.ds(pl.multiple_of(place * width, width), width)]
        projected = projected + dot_nn((pooled + first).astype(BF16), weight)
    pair_ref[...] = projected.astype(BF16)
    own = keep_ref.shape[1] // sides
    for i in range(sides):
        rows = slice(i * own, (i + 1) * own)
        keep_ref[:, rows] = whole[:, pl.ds(pl.multiple_of(i * tokens + col * own, own), own)]
        give_ref[:, rows] = whole[:, pl.ds(pl.multiple_of(i * tokens + (1 - col) * own, own), own)]


def token_kernel(embedded_ref, *refs):
    parts, token_ref = refs[:-1], refs[-1]
    own = token_ref.shape[0]
    mine = pl.ds(pl.multiple_of(lax.axis_index("col") * own, own), own)
    blocks = [
        embedded_ref[s, mine].astype(F32) + sum(part[s].astype(F32) for part in parts)
        for s in range(embedded_ref.shape[0])
    ]
    token_ref[...] = jnp.concatenate(blocks, axis=1).astype(BF16)


def pair_kernel(own_ref, all_ref, weight_ref, out_ref, columns_here):
    seq, col = lax.axis_index("seq"), lax.axis_index("col")
    features, each = weight_ref.shape[0], own_ref.shape[0]
    span = columns_here.shape[0] // each
    rows = all_ref[...].astype(F32)[:, features:]
    if rows.shape[0] == columns_here.shape[0]:
        for j in range(span):
            at = pl.multiple_of((j ^ (seq % span)) * each, each)
            columns_here[pl.ds(at, each)] = rows[j * each:(j + 1) * each]
    else:
        half = columns_here.shape[0]
        columns_here[...] = jnp.where(col == 0, rows[:half], rows[half:])
    rows_here = own_ref[...].astype(F32)[:, :features]
    hidden = gelu(rows_here[:, None, :] + columns_here[...][None, :, :])
    r, c, f = hidden.shape
    out_ref[...] = dot_nn(hidden.reshape(r * c, f).astype(BF16), weight_ref[...]).reshape(r, c, f).astype(BF16)


def cost(flops, size):
    return pl.CostEstimate(flops=int(flops), bytes_accessed=int(size), transcendentals=0)


def on_device(signal, conv_weight, conv_gain, embed_weight, attn_gain, query_weight, keyvalue_weight,
              output_weight, rowcol_weight, pair_weight):
    col = lax.axis_index("col")
    count, cols = lax.axis_size("seq"), lax.axis_size("col")
    positions, half = signal.shape
    taps, channels, _ = conv_weight.shape
    reach = taps // 2
    tokens = positions // POOL
    width = embed_weight.shape[1] * count
    features = query_weight.shape[1] // cols
    heads = features // DK
    swap = [(i, (i + 1) % cols) for i in range(cols)]
    shape = jax.ShapeDtypeStruct

    embed_own = jnp.concatenate(
        [embed_weight.T, lax.dynamic_slice_in_dim(keyvalue_weight, col * DK, DV, 1)], axis=1
    )
    ring = planned(count, lax.axis_size("grp")) and cols == 2
    sides = 2 if ring else 1
    side = lax.axis_index("seq") % sides
    pair_swap = [(i, i ^ 1) for i in range(count)]
    heads, features = heads // sides, features // sides

    def later_part(which):
        place = col * sides + which
        return jnp.concatenate(
            [
                lax.dynamic_slice_in_dim(query_weight, place * features, features, 1),
                lax.dynamic_slice_in_dim(output_weight.T, place * heads * DV, heads * DV, 1),
            ],
            axis=1,
        )

    e = Blocks(embed_own, count)

    signal_t = signal.T
    up = [(i, i + 1) for i in range(count - 1)]
    if ring:
        e.along("own", "step")
        e.across("own", "own2")
    before = lax.ppermute(signal[positions - reach:], "seq", up)
    behind = lax.ppermute(signal[:reach], "seq", [(j, i) for i, j in up])
    later_mine, later_theirs = later_part(side), later_part(1 - side) if ring else None
    ready = signal_t
    if ring:
        ready = after(signal_t, e.at["step"], e.at["own2"], before, behind, later_mine, later_theirs)
    other_t = lax.ppermute(ready, "col", swap)
    own_halo = jnp.pad(jnp.concatenate([before, behind], axis=0), ((0, 16 - 2 * reach), (0, 0)))
    other_halo = lax.ppermute(own_halo, "col", swap)
    halo = jnp.where(
        col == 0, jnp.concatenate([own_halo, other_halo], axis=1), jnp.concatenate([other_halo, own_halo], axis=1)
    )
    gain_row = conv_gain.reshape(1, channels)
    windows, residual = pl.pallas_call(
        functools.partial(act_kernel, taps),
        out_shape=(shape((taps * tokens, channels), BF16), shape((tokens, half), F32)),
        in_specs=vspec(3),
        out_specs=vspec(2),
        scratch_shapes=[pltpu.VMEM((channels, positions), BF16), pltpu.VMEM((channels, 8), F32)],
        compiler_params=params(20),
        cost_estimate=cost(2 * taps * tokens * channels * positions, 4 * channels * positions),
        name="act",
    )(signal_t, other_t, gain_row)
    if ring:
        e.at["step"] = after(e.at["step"], e.at["own2"])
        e.along("step", "far")
        e.across("step", "step2")
        e.between("step", "cross")
    pooled = pl.pallas_call(
        functools.partial(conv_kernel, positions),
        out_shape=shape((tokens, half), BF16),
        in_specs=vspec(4) + hspec(1),
        out_specs=pl.BlockSpec(memory_space=VMEM),
        scratch_shapes=[pltpu.VMEM((taps, half, channels), BF16), pltpu.SemaphoreType.DMA((taps,))],
        compiler_params=params(50),
        cost_estimate=cost(2 * taps * tokens * channels * half, 2 * taps * channels * half),
        name="conv",
    )(windows, residual, halo, gain_row, conv_weight.transpose(0, 2, 1))
    if ring:
        e.at["far"] = after(e.at["far"], pooled, e.at["cross"])
        e.at["step2"] = after(e.at["step2"], pooled, e.at["cross"])
        e.along("step2", "far2")
        e.between("step2", "cross2")
        theirs = after(later_theirs, pooled, e.at["cross"])
        received = lax.ppermute(theirs, "seq", pair_swap)
        pooled = after(pooled, received)
        q = Blocks(jnp.concatenate([later_mine, received]), count)
        q.at["own"] = after(q.at["own"], e.at["far2"])
        q.along("own", "step")
        q.along("step", "far")
        q.between("step", "cross")
        embed_blocks = e.pieces()
        later_blocks = [q.at[name] for name in ("own", "step", "cross", "far")]
    else:
        embed_blocks, later_blocks = (
            [lax.all_gather(x, "seq", axis=0, tiled=True)] for x in (embed_own, later_mine)
        )
    pieces = len(embed_blocks)
    block = width // pieces

    part, keyvalue_blocks = pl.pallas_call(
        functools.partial(embed_kernel, pieces),
        out_shape=(shape((pieces, tokens, block), BF16), shape((pieces, block, DV), BF16)),
        in_specs=vspec(1 + pieces),
        out_specs=vspec(2),
        compiler_params=params(12),
        cost_estimate=cost(2 * tokens * half * width, 2 * half * width),
        name="embed",
    )(pooled, *embed_blocks)
    other_part = lax.ppermute(part, "col", swap)

    keyvalue, normed, embedded = pl.pallas_call(
        keyvalue_kernel,
        out_shape=(
            shape((DV, tokens), BF16),
            shape((pieces, tokens, block), BF16),
            shape((pieces, tokens, block), BF16),
        ),
        in_specs=vspec(4),
        out_specs=vspec(3),
        compiler_params=params(16),
        cost_estimate=cost(2 * tokens * width * DV, 2 * width * DV),
        name="keyvalue",
    )(part, other_part, attn_gain.reshape(pieces, 1, block), keyvalue_blocks)
    both_normed = [normed]
    if ring:
        here = jnp.stack([keyvalue, lax.ppermute(keyvalue, "seq", pair_swap)])
        both_normed.append(lax.ppermute(normed, "seq", pair_swap))
        onward = [(2 * RING[k] + i, 2 * RING[(k + 1) % 4] + i) for k in range(4) for i in range(2)]
        opposite = [(2 * RING[k] + i, 2 * RING[(k + 2) % 4] + i) for k in range(4) for i in range(2)]
        turns = [onward, [(j, i) for i, j in onward], opposite]
        gathered = jnp.concatenate([here] + [lax.ppermute(here, "seq", turn) for turn in turns])
    else:
        gathered = lax.all_gather(keyvalue, "seq", axis=0)
    gathered_other = lax.ppermute(gathered, "col", swap)

    queries = pl.pallas_call(
        functools.partial(query_kernel, sides),
        out_shape=shape((sides * tokens, features), BF16),
        in_specs=vspec(sides + len(later_blocks)),
        out_specs=pl.BlockSpec(memory_space=VMEM),
        compiler_params=params(12),
        cost_estimate=cost(2 * sides * tokens * width * features, 2 * width * features),
        name="query",
    )(*both_normed, *later_blocks)

    attended = pl.pallas_call(
        attend_kernel,
        out_shape=shape((heads, sides * tokens, DV), BF16),
        in_specs=vspec(3),
        out_specs=pl.BlockSpec(memory_space=VMEM),
        scratch_shapes=[pltpu.VMEM((DK, count * tokens), BF16), pltpu.VMEM((DV, count * tokens), BF16)],
        compiler_params=params(24),
        cost_estimate=cost(2 * tokens * heads * count * tokens * (DK + DV), 4 * count * tokens * DV),
        name="attend",
    )(queries, gathered, gathered_other)

    out_width = rowcol_weight.shape[1]
    own_rows, pair_rows = tokens // cols, tokens // PAIR_POOL
    kept = shape((pieces, sides * own_rows, block), BF16)
    keep, give, part_pair = pl.pallas_call(
        functools.partial(output_kernel, sides, features),
        out_shape=(kept, kept, shape((sides * pair_rows, out_width), BF16)),
        in_specs=vspec(3 + len(later_blocks)),
        out_specs=vspec(3),
        scratch_shapes=[pltpu.VMEM((pieces, sides * tokens, block), BF16)],
        compiler_params=params(16),
        cost_estimate=cost(2 * sides * tokens * heads * DV * width, 2 * heads * DV * width),
        name="output",
    )(attended, embedded, rowcol_weight, *later_blocks)

    def total(*parts):
        return sum(x.astype(F32) for x in parts).astype(BF16)

    if ring:
        turned = lax.ppermute(part_pair, "seq", pair_swap)
        part_pair = total(part_pair, jnp.concatenate([turned[pair_rows:], turned[:pair_rows]]))
    projected = total(part_pair, lax.ppermute(part_pair, "col", swap))
    sums = total(keep, lax.ppermute(give, "col", swap))

    if ring:
        sent = sums[:, own_rows:]
        crossed = lax.ppermute(sent, "seq", pair_swap)
        rows_all = after(projected, sent)
        rows_all = jnp.concatenate([rows_all, lax.ppermute(rows_all, "seq", [(i, i ^ 2) for i in range(count)])])
        rows_all = after(rows_all, crossed)
        pairs = [(i * cols + i // 4, (i ^ 4) * cols + i // 4) for i in range(count)]
        far_rows = lax.ppermute(rows_all, ("seq", "col"), pairs)
        rows_all = jnp.where(lax.axis_index("seq") // 4 == col, rows_all, far_rows)
    else:
        rows_all = lax.all_gather(projected, "seq", axis=0, tiled=True)

    parts = [sums[:, :own_rows]]
    if ring:
        parts.append(crossed)
    out_tokens = pl.pallas_call(
        token_kernel,
        out_shape=shape((own_rows, width), BF16),
        in_specs=vspec(1 + len(parts)),
        out_specs=pl.BlockSpec(memory_space=VMEM),
        compiler_params=params(12),
        cost_estimate=cost(3 * own_rows * width, 8 * own_rows * width),
        name="tokens",
    )(embedded, *parts)

    span = pair_rows * count // cols
    pair_features = pair_weight.shape[0]
    pair_out = pl.pallas_call(
        pair_kernel,
        out_shape=shape((pair_rows, span, pair_features), BF16),
        in_specs=vspec(3),
        out_specs=pl.BlockSpec(memory_space=VMEM),
        scratch_shapes=[pltpu.VMEM((span, pair_features), F32)],
        compiler_params=params(16),
        cost_estimate=cost(2 * pair_rows * span * pair_features**2, 2 * pair_rows * span * pair_features),
        name="pair",
    )(projected[:pair_rows], rows_all, pair_weight)
    return out_tokens, pair_out


def solution(mesh):
    placed = (
        P(("grp", "seq"), "col"),
        P(None, None, "col"),
        P(),
        P("col", "seq"),
        P(),
        P("seq", None),
        P("seq", None),
        P(None, "seq"),
        P(),
        P(),
    )
    return jax.shard_map(
        on_device,
        mesh=mesh,
        in_specs=placed,
        out_specs=(P(("grp", "seq", "col"), None), P(("grp", "seq"), "col", None)),
        check_vma=False,
    )
```

```python
import functools
import math

import jax
import jax.numpy as jnp
from jax import lax
from jax.experimental import pallas as pl
from jax.experimental.pallas import tpu as pltpu
from jax.sharding import PartitionSpec as P

DK = 128
DV = 192
POOL = 4
PAIR_POOL = 16
EPS = 1e-06
VMEM = pltpu.VMEM
F32 = jnp.float32
BF16 = jnp.bfloat16


def gelu(x):
    c = math.sqrt(2.0 / math.pi)
    half = 0.5 * x
    return half + half * jnp.tanh(x * (c + (0.044715 * c) * (x * x)))


def dot_nt(a, b):
    return lax.dot_general(a, b, (((1,), (1,)), ((), ())), preferred_element_type=F32)


def dot_nn(a, b):
    return lax.dot_general(a, b, (((1,), (0,)), ((), ())), preferred_element_type=F32)


def params(mib, **kw):
    return pltpu.CompilerParams(vmem_limit_bytes=mib << 20, **kw)


def vspec(n):
    return [pl.BlockSpec(memory_space=VMEM)] * n


def hspec(n):
    return [pl.BlockSpec(memory_space=pltpu.HBM)] * n


RING = (0, 1, 3, 2)


def planned(count, groups):
    return count == 2 * len(RING) and groups == 2


def pick(index, table):
    value = jnp.int32(table[0])
    for i, entry in enumerate(table[1:], 1):
        value = jnp.where(index == i, jnp.int32(entry), value)
    return value


def owners(count, groups):
    if not planned(count, groups):
        return [jnp.int32(0)]
    group, me = lax.axis_index("grp"), lax.axis_index("seq")
    side, place = me % 2, pick(me // 2, [RING.index(i) for i in range(4)])
    result = []
    for step in (0, 3 + 2 * group, 1 + 2 * group, 2):
        row = pick(lax.rem(place + step, 4), RING)
        result += [2 * row + side, 2 * row + 1 - side]
    return result


class Blocks:
    def __init__(self, own, count):
        self.count = count
        self.at = {"own": own}

    def along(self, source, target):
        pairs = []
        for group in range(2):
            for k in range(4):
                a, b = RING[k], RING[(k + 1) % 4]
                if group:
                    a, b = b, a
                pairs += [(group * self.count + 2 * a + i, group * self.count + 2 * b + i) for i in range(2)]
        self.at[target] = lax.ppermute(self.at[source], ("grp", "seq"), pairs)

    def across(self, source, target):
        self.at[target] = lax.ppermute(self.at[source], "seq", [(i, i ^ 1) for i in range(self.count)])

    def between(self, source, target):
        self.at[target] = lax.ppermute(self.at[source], "grp", [(0, 1), (1, 0)])

    def pieces(self):
        names = ("own", "own2", "step", "step2", "cross", "cross2", "far", "far2")
        return [self.at[name] for name in names]


def after(values, *done):
    return lax.optimization_barrier((values, done))[0]


def window_means(first_row, rows, tokens, taps, positions, columns):
    r = lax.broadcasted_iota(jnp.int32, (rows, columns), 0) + first_row
    k = lax.broadcasted_iota(jnp.int32, (rows, columns), 1)
    reach = taps // 2
    if columns != positions:
        k = jnp.where(k < 2 * reach, jnp.where(k < reach, k - reach, k - reach + positions), -positions)
    tap = r // tokens
    gap = k - (POOL * (r - tap * tokens) + tap - reach)
    return jnp.where((gap >= 0) & (gap < POOL), 1.0 / POOL, 0.0).astype(BF16)


def act_kernel(taps, own_ref, other_ref, gain_ref, out_ref, residual_ref, act, gaincol):
    channels, positions = act.shape
    half = own_ref.shape[0]
    col = lax.axis_index("col")
    gaincol[...] = jnp.broadcast_to(gain_ref[...], (8, channels)).T
    step = 64
    halves = ((own_ref, col), (other_ref, 1 - col))
    squares = jnp.zeros((8, positions), F32)
    for ref, _ in halves:
        for j in range(half // step):
            x = ref[j * step:(j + 1) * step, :].astype(F32)
            x = x * x
            for i in range(step // 8):
                squares = squares + x[i * 8:(i + 1) * 8]
    scale = lax.rsqrt(jnp.sum(squares, axis=0, keepdims=True) / channels + EPS)
    for ref, index in halves:
        for j in range(half // step):
            at = pl.multiple_of(index * half + j * step, step)
            x = ref[j * step:(j + 1) * step, :].astype(F32) * scale
            act[pl.ds(at, step), :] = gelu(x * gaincol[pl.ds(at, step), :1]).astype(BF16)
    rows, tokens = out_ref.shape[0], residual_ref.shape[0]
    means = window_means(0, rows, tokens, taps, positions, positions)
    out_ref[...] = dot_nt(means, act[...]).astype(BF16)
    middle = (taps // 2) * tokens
    residual_ref[...] = dot_nt(means[middle:middle + tokens], own_ref[...])


def conv_kernel(positions, windows_ref, residual_ref, halo_ref, gain_ref, weight_hbm, out_ref, weights, sems):
    taps, _, channels = weights.shape
    copies = [pltpu.make_async_copy(weight_hbm.at[t], weights.at[t], sems.at[t]) for t in range(taps)]
    ahead = 2
    for c in copies[:ahead]:
        c.start()
    tokens = out_ref.shape[0]
    h = halo_ref[...].astype(F32)
    h = h * lax.rsqrt(jnp.sum(h * h, axis=1, keepdims=True) / channels + EPS) * gain_ref[...]
    h = gelu(h).astype(BF16)
    total = residual_ref[...]
    for t in range(taps):
        window = windows_ref[t * tokens:(t + 1) * tokens]
        if t != taps // 2:
            edges = dot_nn(window_means(t * tokens, tokens, tokens, taps, positions, h.shape[0]), h)
            window = (window.astype(F32) + edges).astype(BF16)
        copies[t].wait()
        if t + ahead < taps:
            copies[t + ahead].start()
        total = total + dot_nt(window, weights[t])
    out_ref[...] = total.astype(BF16)


def block_owners():
    return owners(lax.axis_size("seq"), lax.axis_size("grp"))


def embed_kernel(pieces, pooled_ref, *refs):
    blocks, (out_ref, rest_ref) = refs[:pieces], refs[pieces:]
    half = pooled_ref.shape[1]
    for ref, owner in zip(blocks, block_owners()):
        out_ref[owner] = dot_nt(pooled_ref[...], ref[:, :half]).astype(BF16)
        rest_ref[owner] = ref[:, half:]


def keyvalue_kernel(part_ref, other_ref, gain_ref, weight_ref, kv_ref, normed_ref, embedded_ref):
    count, _, width = part_ref.shape
    e = (part_ref[...].astype(F32) + other_ref[...].astype(F32)).astype(BF16)
    embedded_ref[...] = e
    e = e.astype(F32)
    squares = jnp.sum(jnp.sum(e * e, axis=0), axis=1, keepdims=True)
    scale = lax.rsqrt(squares / (count * width) + EPS)
    normed_ref[...] = (e * scale[None] * gain_ref[...]).astype(BF16)
    total = 0.0
    for s in range(count):
        total = total + dot_nn(normed_ref[s], weight_ref[s])
    kv = total.T.astype(BF16)
    kv_ref[...] = kv


def later_blocks_of(refs):
    places = block_owners()
    per = len(places) // len(refs)
    rows = refs[0].shape[0] // per
    for i, place in enumerate(places):
        start = (i % per) * rows
        yield refs[i // per], slice(start, start + rows), place


def query_kernel(sides, *refs):
    normed, pieces, query_ref = refs[:sides], refs[sides:-1], refs[-1]
    features = query_ref.shape[1]
    tokens = normed[0].shape[1]
    totals = [0.0] * sides
    for ref, rows, place in later_blocks_of(pieces):
        weight = ref[rows, :features]
        totals = [t + dot_nn(n[place], weight) for t, n in zip(totals, normed)]
    for i, total in enumerate(totals):
        query_ref[i * tokens:(i + 1) * tokens] = (total * DK ** (-0.5)).astype(BF16)


def attend_kernel(query_ref, own_ref, other_ref, out_ref, keys, values):
    tokens, features = query_ref.shape
    blocks, _, each = own_ref.shape
    first = lax.axis_index("col") == 0
    for i in range(blocks):
        keys[:, i * each:(i + 1) * each] = jnp.where(first, own_ref[i][:DK], other_ref[i][:DK])
        values[:, i * each:(i + 1) * each] = jnp.where(first, other_ref[i], own_ref[i])
    for h in range(features // DK):
        scores = dot_nn(query_ref[:, h * DK:(h + 1) * DK], keys[...])
        weights = jnp.exp(scores - jnp.max(scores, axis=1, keepdims=True))
        total = jnp.sum(weights, axis=1, keepdims=True)
        out_ref[h] = (dot_nt(weights.astype(BF16), values[...]) / total).astype(BF16)


def output_kernel(sides, features, attended_ref, embedded_ref, pair_weight_ref, *refs):
    pieces, (keep_ref, give_ref, pair_ref, whole) = refs[:-4], refs[-4:]
    heads = attended_ref.shape[0]
    flat = jnp.concatenate([attended_ref[h] for h in range(heads)], axis=1)
    _, tokens, width = embedded_ref.shape
    col = lax.axis_index("col")
    share = jnp.where(col == 0, 1.0, 0.0)
    projected = 0.0
    for ref, rows, place in later_blocks_of(pieces):
        part = dot_nt(flat, ref[rows, features:])
        whole[place] = part.astype(BF16)
        pooled = jnp.mean(part.reshape(sides * tokens // PAIR_POOL, PAIR_POOL, width), axis=1)
        first = jnp.mean(embedded_ref[place].astype(F32).reshape(tokens // PAIR_POOL, PAIR_POOL, width), axis=1) * share
        if sides > 1:
            first = jnp.concatenate([first, jnp.zeros((pooled.shape[0] - first.shape[0], width), F32)], axis=0)
        weight = pair_weight_ref[pl.ds(pl.multiple_of(place * width, width), width)]
        projected = projected + dot_nn((pooled + first).astype(BF16), weight)
    pair_ref[...] = projected.astype(BF16)
    own = keep_ref.shape[0] // sides
    for i in range(sides):
        for ref, core in ((keep_ref, col), (give_ref, 1 - col)):
            rows = pl.ds(pl.multiple_of(i * tokens + core * own, own), own)
            ref[i * own:(i + 1) * own] = jnp.concatenate([whole[s, rows] for s in range(whole.shape[0])], axis=1)


def token_kernel(embedded_ref, *refs):
    parts, token_ref = refs[:-1], refs[-1]
    own = token_ref.shape[0]
    mine = pl.ds(pl.multiple_of(lax.axis_index("col") * own, own), own)
    embedded = jnp.concatenate([embedded_ref[s, mine] for s in range(embedded_ref.shape[0])], axis=1)
    token_ref[...] = (embedded.astype(F32) + sum(part[...].astype(F32) for part in parts)).astype(BF16)


def pair_kernel(own_ref, all_ref, weight_ref, out_ref, columns_here):
    seq, col = lax.axis_index("seq"), lax.axis_index("col")
    features, each = weight_ref.shape[0], own_ref.shape[0]
    span = columns_here.shape[0] // each
    rows = all_ref[...].astype(F32)[:, features:]
    if rows.shape[0] == columns_here.shape[0]:
        for j in range(span):
            at = pl.multiple_of((j ^ (seq % span)) * each, each)
            columns_here[pl.ds(at, each)] = rows[j * each:(j + 1) * each]
    else:
        half = columns_here.shape[0]
        columns_here[...] = jnp.where(col == 0, rows[:half], rows[half:])
    rows_here = own_ref[...].astype(F32)[:, :features]
    hidden = gelu(rows_here[:, None, :] + columns_here[...][None, :, :])
    r, c, f = hidden.shape
    out_ref[...] = dot_nn(hidden.reshape(r * c, f).astype(BF16), weight_ref[...]).reshape(r, c, f).astype(BF16)


def cost(flops, size):
    return pl.CostEstimate(flops=int(flops), bytes_accessed=int(size), transcendentals=0)


def on_device(signal, conv_weight, conv_gain, embed_weight, attn_gain, query_weight, keyvalue_weight,
              output_weight, rowcol_weight, pair_weight):
    col = lax.axis_index("col")
    count, cols = lax.axis_size("seq"), lax.axis_size("col")
    positions, half = signal.shape
    taps, channels, _ = conv_weight.shape
    reach = taps // 2
    tokens = positions // POOL
    width = embed_weight.shape[1] * count
    features = query_weight.shape[1] // cols
    heads = features // DK
    swap = [(i, (i + 1) % cols) for i in range(cols)]
    shape = jax.ShapeDtypeStruct

    embed_own = jnp.concatenate(
        [embed_weight.T, lax.dynamic_slice_in_dim(keyvalue_weight, col * DK, DV, 1)], axis=1
    )
    ring = planned(count, lax.axis_size("grp")) and cols == 2
    sides = 2 if ring else 1
    side = lax.axis_index("seq") % sides
    pair_swap = [(i, i ^ 1) for i in range(count)]
    heads, features = heads // sides, features // sides

    def later_part(which):
        place = col * sides + which
        return jnp.concatenate(
            [
                lax.dynamic_slice_in_dim(query_weight, place * features, features, 1),
                lax.dynamic_slice_in_dim(output_weight.T, place * heads * DV, heads * DV, 1),
            ],
            axis=1,
        )

    e = Blocks(embed_own, count)

    signal_t = signal.T
    up = [(i, i + 1) for i in range(count - 1)]
    if ring:
        e.along("own", "step")
        e.across("own", "own2")
    before = lax.ppermute(signal[positions - reach:], "seq", up)
    behind = lax.ppermute(signal[:reach], "seq", [(j, i) for i, j in up])
    later_mine, later_theirs = later_part(side), later_part(1 - side) if ring else None
    ready = signal_t
    if ring:
        ready = after(signal_t, e.at["step"], e.at["own2"], before, behind, later_mine, later_theirs)
    other_t = lax.ppermute(ready, "col", swap)
    own_halo = jnp.pad(jnp.concatenate([before, behind], axis=0), ((0, 16 - 2 * reach), (0, 0)))
    other_halo = lax.ppermute(own_halo, "col", swap)
    halo = jnp.where(
        col == 0, jnp.concatenate([own_halo, other_halo], axis=1), jnp.concatenate([other_halo, own_halo], axis=1)
    )
    gain_row = conv_gain.reshape(1, channels)
    windows, residual = pl.pallas_call(
        functools.partial(act_kernel, taps),
        out_shape=(shape((taps * tokens, channels), BF16), shape((tokens, half), F32)),
        in_specs=vspec(3),
        out_specs=vspec(2),
        scratch_shapes=[pltpu.VMEM((channels, positions), BF16), pltpu.VMEM((channels, 8), F32)],
        compiler_params=params(20),
        cost_estimate=cost(2 * taps * tokens * channels * positions, 4 * channels * positions),
        name="act",
    )(signal_t, other_t, gain_row)
    if ring:
        e.at["step"] = after(e.at["step"], e.at["own2"])
        e.along("step", "far")
        e.across("step", "step2")
        e.between("step", "cross")
    pooled = pl.pallas_call(
        functools.partial(conv_kernel, positions),
        out_shape=shape((tokens, half), BF16),
        in_specs=vspec(4) + hspec(1),
        out_specs=pl.BlockSpec(memory_space=VMEM),
        scratch_shapes=[pltpu.VMEM((taps, half, channels), BF16), pltpu.SemaphoreType.DMA((taps,))],
        compiler_params=params(50),
        cost_estimate=cost(2 * taps * tokens * channels * half, 2 * taps * channels * half),
        name="conv",
    )(windows, residual, halo, gain_row, conv_weight.transpose(0, 2, 1))
    if ring:
        e.at["far"] = after(e.at["far"], pooled, e.at["cross"])
        e.at["step2"] = after(e.at["step2"], pooled, e.at["cross"])
        e.along("step2", "far2")
        e.between("step2", "cross2")
        theirs = after(later_theirs, pooled, e.at["cross"])
        received = lax.ppermute(theirs, "seq", pair_swap)
        pooled = after(pooled, received)
        q = Blocks(jnp.concatenate([later_mine, received]), count)
        q.at["own"] = after(q.at["own"], e.at["far2"])
        q.along("own", "step")
        embed_blocks = e.pieces()
    else:
        embed_blocks, later_blocks = (
            [lax.all_gather(x, "seq", axis=0, tiled=True)] for x in (embed_own, later_mine)
        )
    pieces = len(embed_blocks)
    block = width // pieces

    part, keyvalue_blocks = pl.pallas_call(
        functools.partial(embed_kernel, pieces),
        out_shape=(shape((pieces, tokens, block), BF16), shape((pieces, block, DV), BF16)),
        in_specs=vspec(1 + pieces),
        out_specs=vspec(2),
        compiler_params=params(12),
        cost_estimate=cost(2 * tokens * half * width, 2 * half * width),
        name="embed",
    )(pooled, *embed_blocks)
    other_part = lax.ppermute(part, "col", swap)

    keyvalue, normed, embedded = pl.pallas_call(
        keyvalue_kernel,
        out_shape=(
            shape((DV, tokens), BF16),
            shape((pieces, tokens, block), BF16),
            shape((pieces, tokens, block), BF16),
        ),
        in_specs=vspec(4),
        out_specs=vspec(3),
        compiler_params=params(16),
        cost_estimate=cost(2 * tokens * width * DV, 2 * width * DV),
        name="keyvalue",
    )(part, other_part, attn_gain.reshape(pieces, 1, block), keyvalue_blocks)
    both_normed = [normed]
    if ring:
        here = jnp.stack([keyvalue, lax.ppermute(keyvalue, "seq", pair_swap)])
        both_normed.append(lax.ppermute(normed, "seq", pair_swap))
        q.at["step"] = after(q.at["step"], both_normed[1])
        q.along("step", "far")
        q.between("step", "cross")
        later_blocks = [q.at[name] for name in ("own", "step", "cross", "far")]
        onward = [(2 * RING[k] + i, 2 * RING[(k + 1) % 4] + i) for k in range(4) for i in range(2)]
        opposite = [(2 * RING[k] + i, 2 * RING[(k + 2) % 4] + i) for k in range(4) for i in range(2)]
        turns = [onward, [(j, i) for i, j in onward], opposite]
        gathered = jnp.concatenate([here] + [lax.ppermute(here, "seq", turn) for turn in turns])
    else:
        gathered = lax.all_gather(keyvalue, "seq", axis=0)
    gathered_other = lax.ppermute(gathered, "col", swap)

    queries = pl.pallas_call(
        functools.partial(query_kernel, sides),
        out_shape=shape((sides * tokens, features), BF16),
        in_specs=vspec(sides + len(later_blocks)),
        out_specs=pl.BlockSpec(memory_space=VMEM),
        compiler_params=params(12),
        cost_estimate=cost(2 * sides * tokens * width * features, 2 * width * features),
        name="query",
    )(*both_normed, *later_blocks)

    attended = pl.pallas_call(
        attend_kernel,
        out_shape=shape((heads, sides * tokens, DV), BF16),
        in_specs=vspec(3),
        out_specs=pl.BlockSpec(memory_space=VMEM),
        scratch_shapes=[pltpu.VMEM((DK, count * tokens), BF16), pltpu.VMEM((DV, count * tokens), BF16)],
        compiler_params=params(24),
        cost_estimate=cost(2 * tokens * heads * count * tokens * (DK + DV), 4 * count * tokens * DV),
        name="attend",
    )(queries, gathered, gathered_other)

    out_width = rowcol_weight.shape[1]
    own_rows, pair_rows = tokens // cols, tokens // PAIR_POOL
    kept = shape((sides * own_rows, width), BF16)
    keep, give, part_pair = pl.pallas_call(
        functools.partial(output_kernel, sides, features),
        out_shape=(kept, kept, shape((sides * pair_rows, out_width), BF16)),
        in_specs=vspec(3 + len(later_blocks)),
        out_specs=vspec(3),
        scratch_shapes=[pltpu.VMEM((pieces, sides * tokens, block), BF16)],
        compiler_params=params(16),
        cost_estimate=cost(2 * sides * tokens * heads * DV * width, 2 * heads * DV * width),
        name="output",
    )(attended, embedded, rowcol_weight, *later_blocks)

    def total(*parts):
        return sum(x.astype(F32) for x in parts).astype(BF16)

    if ring:
        turned = lax.ppermute(part_pair, "seq", pair_swap)
        part_pair = total(part_pair, jnp.concatenate([turned[pair_rows:], turned[:pair_rows]]))
    projected = total(part_pair, lax.ppermute(part_pair, "col", swap))
    sums = total(keep, lax.ppermute(give, "col", swap))

    if ring:
        sent = sums[own_rows:]
        crossed = lax.ppermute(sent, "seq", pair_swap)
        rows_all = after(projected, sent)
        rows_all = jnp.concatenate([rows_all, lax.ppermute(rows_all, "seq", [(i, i ^ 2) for i in range(count)])])
        rows_all = after(rows_all, crossed)
        pairs = [(i * cols + i // 4, (i ^ 4) * cols + i // 4) for i in range(count)]
        far_rows = lax.ppermute(rows_all, ("seq", "col"), pairs)
        rows_all = jnp.where(lax.axis_index("seq") // 4 == col, rows_all, far_rows)
    else:
        rows_all = lax.all_gather(projected, "seq", axis=0, tiled=True)

    parts = [sums[:own_rows]]
    if ring:
        parts.append(crossed)
    out_tokens = pl.pallas_call(
        token_kernel,
        out_shape=shape((own_rows, width), BF16),
        in_specs=vspec(1 + len(parts)),
        out_specs=pl.BlockSpec(memory_space=VMEM),
        compiler_params=params(12),
        cost_estimate=cost(3 * own_rows * width, 8 * own_rows * width),
        name="tokens",
    )(embedded, *parts)

    span = pair_rows * count // cols
    pair_features = pair_weight.shape[0]
    pair_out = pl.pallas_call(
        pair_kernel,
        out_shape=shape((pair_rows, span, pair_features), BF16),
        in_specs=vspec(3),
        out_specs=pl.BlockSpec(memory_space=VMEM),
        scratch_shapes=[pltpu.VMEM((span, pair_features), F32)],
        compiler_params=params(16),
        cost_estimate=cost(2 * pair_rows * span * pair_features**2, 2 * pair_rows * span * pair_features),
        name="pair",
    )(projected[:pair_rows], rows_all, pair_weight)
    return out_tokens, pair_out


def solution(mesh):
    placed = (
        P(("grp", "seq"), "col"),
        P(None, None, "col"),
        P(),
        P("col", "seq"),
        P(),
        P("seq", None),
        P("seq", None),
        P(None, "seq"),
        P(),
        P(),
    )
    return jax.shard_map(
        on_device,
        mesh=mesh,
        in_specs=placed,
        out_specs=(P(("grp", "seq", "col"), None), P(("grp", "seq"), "col", None)),
        check_vma=False,
    )
```

```python
import functools
import math

import jax
import jax.numpy as jnp
from jax import lax
from jax.experimental import pallas as pl
from jax.experimental.pallas import tpu as pltpu
from jax.sharding import PartitionSpec as P

DK = 128
DV = 192
POOL = 4
PAIR_POOL = 16
EPS = 1e-06
VMEM = pltpu.VMEM
F32 = jnp.float32
BF16 = jnp.bfloat16


def gelu(x):
    c = math.sqrt(2.0 / math.pi)
    half = 0.5 * x
    return half + half * jnp.tanh(x * (c + (0.044715 * c) * (x * x)))


def dot_nt(a, b):
    return lax.dot_general(a, b, (((1,), (1,)), ((), ())), preferred_element_type=F32)


def dot_nn(a, b):
    return lax.dot_general(a, b, (((1,), (0,)), ((), ())), preferred_element_type=F32)


def params(mib, **kw):
    return pltpu.CompilerParams(vmem_limit_bytes=mib << 20, **kw)


def vspec(n):
    return [pl.BlockSpec(memory_space=VMEM)] * n


def hspec(n):
    return [pl.BlockSpec(memory_space=pltpu.HBM)] * n


RING = (0, 1, 3, 2)


def planned(count, groups):
    return count == 2 * len(RING) and groups == 2


def pick(index, table):
    value = jnp.int32(table[0])
    for i, entry in enumerate(table[1:], 1):
        value = jnp.where(index == i, jnp.int32(entry), value)
    return value


def owners(count, groups):
    if not planned(count, groups):
        return [jnp.int32(0)]
    group, me = lax.axis_index("grp"), lax.axis_index("seq")
    side, place = me % 2, pick(me // 2, [RING.index(i) for i in range(4)])
    result = []
    for step in (0, 3 + 2 * group, 1 + 2 * group, 2):
        row = pick(lax.rem(place + step, 4), RING)
        result += [2 * row + side, 2 * row + 1 - side]
    return result


class Blocks:
    def __init__(self, own, count):
        self.count = count
        self.at = {"own": own}

    def along(self, source, target):
        pairs = []
        for group in range(2):
            for k in range(4):
                a, b = RING[k], RING[(k + 1) % 4]
                if group:
                    a, b = b, a
                pairs += [(group * self.count + 2 * a + i, group * self.count + 2 * b + i) for i in range(2)]
        self.at[target] = lax.ppermute(self.at[source], ("grp", "seq"), pairs)

    def across(self, source, target):
        self.at[target] = lax.ppermute(self.at[source], "seq", [(i, i ^ 1) for i in range(self.count)])

    def between(self, source, target):
        self.at[target] = lax.ppermute(self.at[source], "grp", [(0, 1), (1, 0)])

    def pieces(self):
        names = ("own", "own2", "step", "step2", "cross", "cross2", "far", "far2")
        return [self.at[name] for name in names]


def after(values, *done):
    return lax.optimization_barrier((values, done))[0]


def window_means(first_row, rows, tokens, taps, positions, columns):
    r = lax.broadcasted_iota(jnp.int32, (rows, columns), 0) + first_row
    k = lax.broadcasted_iota(jnp.int32, (rows, columns), 1)
    reach = taps // 2
    if columns != positions:
        k = jnp.where(k < 2 * reach, jnp.where(k < reach, k - reach, k - reach + positions), -positions)
    tap = r // tokens
    gap = k - (POOL * (r - tap * tokens) + tap - reach)
    return jnp.where((gap >= 0) & (gap < POOL), 1.0 / POOL, 0.0).astype(BF16)


def act_kernel(taps, own_ref, other_ref, gain_ref, out_ref, residual_ref, act, gaincol):
    channels, positions = act.shape
    half = own_ref.shape[0]
    col = lax.axis_index("col")
    gaincol[...] = jnp.broadcast_to(gain_ref[...], (8, channels)).T
    step = 64
    halves = ((own_ref, col), (other_ref, 1 - col))
    squares = jnp.zeros((8, positions), F32)
    for ref, _ in halves:
        for j in range(half // step):
            x = ref[j * step:(j + 1) * step, :].astype(F32)
            x = x * x
            for i in range(step // 8):
                squares = squares + x[i * 8:(i + 1) * 8]
    scale = lax.rsqrt(jnp.sum(squares, axis=0, keepdims=True) / channels + EPS)
    for ref, index in halves:
        for j in range(half // step):
            at = pl.multiple_of(index * half + j * step, step)
            x = ref[j * step:(j + 1) * step, :].astype(F32) * scale
            act[pl.ds(at, step), :] = gelu(x * gaincol[pl.ds(at, step), :1]).astype(BF16)
    rows, tokens = out_ref.shape[0], residual_ref.shape[0]
    means = window_means(0, rows, tokens, taps, positions, positions)
    out_ref[...] = dot_nt(means, act[...]).astype(BF16)
    middle = (taps // 2) * tokens
    residual_ref[...] = dot_nt(means[middle:middle + tokens], own_ref[...])


def conv_kernel(positions, windows_ref, residual_ref, halo_ref, gain_ref, weight_hbm, out_ref, weights, sems):
    taps, _, channels = weights.shape
    copies = [pltpu.make_async_copy(weight_hbm.at[t], weights.at[t], sems.at[t]) for t in range(taps)]
    ahead = 2
    for c in copies[:ahead]:
        c.start()
    tokens = out_ref.shape[0]
    h = halo_ref[...].astype(F32)
    h = h * lax.rsqrt(jnp.sum(h * h, axis=1, keepdims=True) / channels + EPS) * gain_ref[...]
    h = gelu(h).astype(BF16)
    total = residual_ref[...]
    for t in range(taps):
        window = windows_ref[t * tokens:(t + 1) * tokens]
        if t != taps // 2:
            edges = dot_nn(window_means(t * tokens, tokens, tokens, taps, positions, h.shape[0]), h)
            window = (window.astype(F32) + edges).astype(BF16)
        copies[t].wait()
        if t + ahead < taps:
            copies[t + ahead].start()
        total = total + dot_nt(window, weights[t])
    out_ref[...] = total.astype(BF16)


def block_owners():
    return owners(lax.axis_size("seq"), lax.axis_size("grp"))


def embed_kernel(pieces, pooled_ref, *refs):
    blocks, (out_ref, rest_ref) = refs[:pieces], refs[pieces:]
    half = pooled_ref.shape[1]
    for ref, owner in zip(blocks, block_owners()):
        out_ref[owner] = dot_nt(pooled_ref[...], ref[:, :half]).astype(BF16)
        rest_ref[owner] = ref[:, half:]


def keyvalue_kernel(part_ref, other_ref, gain_ref, weight_ref, kv_ref, normed_ref, embedded_ref):
    count, _, width = part_ref.shape
    e = (part_ref[...].astype(F32) + other_ref[...].astype(F32)).astype(BF16)
    embedded_ref[...] = e
    e = e.astype(F32)
    squares = jnp.sum(jnp.sum(e * e, axis=0), axis=1, keepdims=True)
    scale = lax.rsqrt(squares / (count * width) + EPS)
    normed_ref[...] = (e * scale[None] * gain_ref[...]).astype(BF16)
    total = 0.0
    for s in range(count):
        total = total + dot_nn(normed_ref[s], weight_ref[s])
    kv = total.T.astype(BF16)
    kv_ref[...] = kv


def later_blocks_of(refs):
    places = block_owners()
    per = len(places) // len(refs)
    rows = refs[0].shape[0] // per
    for i, place in enumerate(places):
        start = (i % per) * rows
        yield refs[i // per], slice(start, start + rows), place


def query_kernel(sides, *refs):
    normed, pieces, query_ref = refs[:sides], refs[sides:-1], refs[-1]
    features = query_ref.shape[1]
    tokens = normed[0].shape[1]
    totals = [0.0] * sides
    for ref, rows, place in later_blocks_of(pieces):
        weight = ref[rows, :features]
        totals = [t + dot_nn(n[place], weight) for t, n in zip(totals, normed)]
    for i, total in enumerate(totals):
        query_ref[i * tokens:(i + 1) * tokens] = (total * DK ** (-0.5)).astype(BF16)


def attend_kernel(query_ref, own_ref, other_ref, out_ref, keys, values):
    tokens, features = query_ref.shape
    blocks, _, each = own_ref.shape
    first = lax.axis_index("col") == 0
    for i in range(blocks):
        keys[:, i * each:(i + 1) * each] = jnp.where(first, own_ref[i][:DK], other_ref[i][:DK])
        values[:, i * each:(i + 1) * each] = jnp.where(first, other_ref[i], own_ref[i])
    for h in range(features // DK):
        scores = dot_nn(query_ref[:, h * DK:(h + 1) * DK], keys[...])
        weights = jnp.exp(scores - jnp.max(scores, axis=1, keepdims=True))
        total = jnp.sum(weights, axis=1, keepdims=True)
        out_ref[h] = (dot_nt(weights.astype(BF16), values[...]) / total).astype(BF16)


def output_kernel(sides, features, attended_ref, embedded_ref, pair_weight_ref, *refs):
    pieces, (keep_ref, give_ref, pair_ref, whole) = refs[:-4], refs[-4:]
    heads = attended_ref.shape[0]
    flat = jnp.concatenate([attended_ref[h] for h in range(heads)], axis=1)
    _, tokens, width = embedded_ref.shape
    col = lax.axis_index("col")
    share = jnp.where(col == 0, 1.0, 0.0)
    projected = 0.0
    for ref, rows, place in later_blocks_of(pieces):
        part = dot_nt(flat, ref[rows, features:])
        whole[place] = part.astype(BF16)
        pooled = jnp.mean(part.reshape(sides * tokens // PAIR_POOL, PAIR_POOL, width), axis=1)
        first = jnp.mean(embedded_ref[place].astype(F32).reshape(tokens // PAIR_POOL, PAIR_POOL, width), axis=1) * share
        if sides > 1:
            first = jnp.concatenate([first, jnp.zeros((pooled.shape[0] - first.shape[0], width), F32)], axis=0)
        weight = pair_weight_ref[pl.ds(pl.multiple_of(place * width, width), width)]
        projected = projected + dot_nn((pooled + first).astype(BF16), weight)
    pair_ref[...] = projected.astype(BF16)
    own = keep_ref.shape[0] // sides
    for i in range(sides):
        for ref, core in ((keep_ref, col), (give_ref, 1 - col)):
            rows = pl.ds(pl.multiple_of(i * tokens + core * own, own), own)
            ref[i * own:(i + 1) * own] = jnp.concatenate([whole[s, rows] for s in range(whole.shape[0])], axis=1)


def token_kernel(embedded_ref, *refs):
    parts, token_ref = refs[:-1], refs[-1]
    own = token_ref.shape[0]
    mine = pl.ds(pl.multiple_of(lax.axis_index("col") * own, own), own)
    embedded = jnp.concatenate([embedded_ref[s, mine] for s in range(embedded_ref.shape[0])], axis=1)
    token_ref[...] = (embedded.astype(F32) + sum(part[...].astype(F32) for part in parts)).astype(BF16)


def pair_kernel(own_ref, all_ref, weight_ref, out_ref, columns_here):
    seq, col = lax.axis_index("seq"), lax.axis_index("col")
    features, each = weight_ref.shape[0], own_ref.shape[0]
    span = columns_here.shape[0] // each
    rows = all_ref[...].astype(F32)[:, features:]
    if rows.shape[0] == columns_here.shape[0]:
        for j in range(span):
            at = pl.multiple_of((j ^ (seq % span)) * each, each)
            columns_here[pl.ds(at, each)] = rows[j * each:(j + 1) * each]
    else:
        half = columns_here.shape[0]
        columns_here[...] = jnp.where(col == 0, rows[:half], rows[half:])
    rows_here = own_ref[...].astype(F32)[:, :features]
    hidden = gelu(rows_here[:, None, :] + columns_here[...][None, :, :])
    r, c, f = hidden.shape
    out_ref[...] = dot_nn(hidden.reshape(r * c, f).astype(BF16), weight_ref[...]).reshape(r, c, f).astype(BF16)


def cost(flops, size):
    return pl.CostEstimate(flops=int(flops), bytes_accessed=int(size), transcendentals=0)


def on_device(signal, conv_weight, conv_gain, embed_weight, attn_gain, query_weight, keyvalue_weight,
              output_weight, rowcol_weight, pair_weight):
    col = lax.axis_index("col")
    count, cols = lax.axis_size("seq"), lax.axis_size("col")
    positions, half = signal.shape
    taps, channels, _ = conv_weight.shape
    reach = taps // 2
    tokens = positions // POOL
    width = embed_weight.shape[1] * count
    features = query_weight.shape[1] // cols
    heads = features // DK
    swap = [(i, (i + 1) % cols) for i in range(cols)]
    shape = jax.ShapeDtypeStruct

    embed_own = jnp.concatenate(
        [embed_weight.T, lax.dynamic_slice_in_dim(keyvalue_weight, col * DK, DV, 1)], axis=1
    )
    ring = planned(count, lax.axis_size("grp")) and cols == 2
    sides = 2 if ring else 1
    side = lax.axis_index("seq") % sides
    pair_swap = [(i, i ^ 1) for i in range(count)]
    heads, features = heads // sides, features // sides

    def later_part(which):
        place = col * sides + which
        return jnp.concatenate(
            [
                lax.dynamic_slice_in_dim(query_weight, place * features, features, 1),
                lax.dynamic_slice_in_dim(output_weight.T, place * heads * DV, heads * DV, 1),
            ],
            axis=1,
        )

    e = Blocks(embed_own, count)

    signal_t = signal.T
    up = [(i, i + 1) for i in range(count - 1)]
    if ring:
        e.along("own", "step")
        e.across("own", "own2")
    before = lax.ppermute(signal[positions - reach:], "seq", up)
    behind = lax.ppermute(signal[:reach], "seq", [(j, i) for i, j in up])
    later_mine, later_theirs = later_part(side), later_part(1 - side) if ring else None
    ready = signal_t
    if ring:
        ready = after(signal_t, e.at["step"], e.at["own2"], before, behind, later_mine, later_theirs)
    other_t = lax.ppermute(ready, "col", swap)
    own_halo = jnp.pad(jnp.concatenate([before, behind], axis=0), ((0, 16 - 2 * reach), (0, 0)))
    other_halo = lax.ppermute(own_halo, "col", swap)
    halo = jnp.where(
        col == 0, jnp.concatenate([own_halo, other_halo], axis=1), jnp.concatenate([other_halo, own_halo], axis=1)
    )
    gain_row = conv_gain.reshape(1, channels)
    windows, residual = pl.pallas_call(
        functools.partial(act_kernel, taps),
        out_shape=(shape((taps * tokens, channels), BF16), shape((tokens, half), F32)),
        in_specs=vspec(3),
        out_specs=vspec(2),
        scratch_shapes=[pltpu.VMEM((channels, positions), BF16), pltpu.VMEM((channels, 8), F32)],
        compiler_params=params(20),
        cost_estimate=cost(2 * taps * tokens * channels * positions, 4 * channels * positions),
        name="act",
    )(signal_t, other_t, gain_row)
    if ring:
        e.at["step"] = after(e.at["step"], e.at["own2"])
        e.along("step", "far")
        e.across("step", "step2")
        e.between("step", "cross")
    pooled = pl.pallas_call(
        functools.partial(conv_kernel, positions),
        out_shape=shape((tokens, half), BF16),
        in_specs=vspec(4) + hspec(1),
        out_specs=pl.BlockSpec(memory_space=VMEM),
        scratch_shapes=[pltpu.VMEM((taps, half, channels), BF16), pltpu.SemaphoreType.DMA((taps,))],
        compiler_params=params(50),
        cost_estimate=cost(2 * taps * tokens * channels * half, 2 * taps * channels * half),
        name="conv",
    )(windows, residual, halo, gain_row, conv_weight.transpose(0, 2, 1))
    if ring:
        e.at["far"] = after(e.at["far"], pooled, e.at["cross"])
        e.at["step2"] = after(e.at["step2"], pooled, e.at["cross"])
        e.along("step2", "far2")
        e.between("step2", "cross2")
        theirs = after(later_theirs, pooled, e.at["cross"])
        received = lax.ppermute(theirs, "seq", pair_swap)
        pooled = after(pooled, received)
        q = Blocks(jnp.concatenate([later_mine, received]), count)
        q.at["own"] = after(q.at["own"], e.at["far2"])
        q.along("own", "step")
        embed_blocks = e.pieces()
    else:
        embed_blocks, later_blocks = (
            [lax.all_gather(x, "seq", axis=0, tiled=True)] for x in (embed_own, later_mine)
        )
    pieces = len(embed_blocks)
    block = width // pieces

    part, keyvalue_blocks = pl.pallas_call(
        functools.partial(embed_kernel, pieces),
        out_shape=(shape((pieces, tokens, block), BF16), shape((pieces, block, DV), BF16)),
        in_specs=vspec(1 + pieces),
        out_specs=vspec(2),
        compiler_params=params(12),
        cost_estimate=cost(2 * tokens * half * width, 2 * half * width),
        name="embed",
    )(pooled, *embed_blocks)
    other_part = lax.ppermute(part, "col", swap)

    keyvalue, normed, embedded = pl.pallas_call(
        keyvalue_kernel,
        out_shape=(
            shape((DV, tokens), BF16),
            shape((pieces, tokens, block), BF16),
            shape((pieces, tokens, block), BF16),
        ),
        in_specs=vspec(4),
        out_specs=vspec(3),
        compiler_params=params(16),
        cost_estimate=cost(2 * tokens * width * DV, 2 * width * DV),
        name="keyvalue",
    )(part, other_part, attn_gain.reshape(pieces, 1, block), keyvalue_blocks)
    both_normed = [normed]
    if ring:
        turns = [[(2 * RING[k] + i, 2 * RING[(k + t) % 4] + i) for k in range(4) for i in range(2)] for t in (1, 3, 2)]
        turned = [lax.ppermute(keyvalue, "seq", turn) for turn in turns]
        both_normed.append(lax.ppermute(normed, "seq", pair_swap))
        q.at["step"] = after(q.at["step"], both_normed[1])
        q.along("step", "far")
        q.between("step", "cross")
        later_blocks = [q.at[name] for name in ("own", "step", "cross", "far")]
        row = jnp.stack([keyvalue] + after(turned, q.at["step"]))
        gathered = jnp.concatenate([row, lax.ppermute(row, "seq", pair_swap)])
    else:
        gathered = lax.all_gather(keyvalue, "seq", axis=0)
    gathered_other = lax.ppermute(gathered, "col", swap)

    queries = pl.pallas_call(
        functools.partial(query_kernel, sides),
        out_shape=shape((sides * tokens, features), BF16),
        in_specs=vspec(sides + len(later_blocks)),
        out_specs=pl.BlockSpec(memory_space=VMEM),
        compiler_params=params(12),
        cost_estimate=cost(2 * sides * tokens * width * features, 2 * width * features),
        name="query",
    )(*both_normed, *later_blocks)

    attended = pl.pallas_call(
        attend_kernel,
        out_shape=shape((heads, sides * tokens, DV), BF16),
        in_specs=vspec(3),
        out_specs=pl.BlockSpec(memory_space=VMEM),
        scratch_shapes=[pltpu.VMEM((DK, count * tokens), BF16), pltpu.VMEM((DV, count * tokens), BF16)],
        compiler_params=params(24),
        cost_estimate=cost(2 * tokens * heads * count * tokens * (DK + DV), 4 * count * tokens * DV),
        name="attend",
    )(queries, gathered, gathered_other)

    out_width = rowcol_weight.shape[1]
    own_rows, pair_rows = tokens // cols, tokens // PAIR_POOL
    kept = shape((sides * own_rows, width), BF16)
    keep, give, part_pair = pl.pallas_call(
        functools.partial(output_kernel, sides, features),
        out_shape=(kept, kept, shape((sides * pair_rows, out_width), BF16)),
        in_specs=vspec(3 + len(later_blocks)),
        out_specs=vspec(3),
        scratch_shapes=[pltpu.VMEM((pieces, sides * tokens, block), BF16)],
        compiler_params=params(16),
        cost_estimate=cost(2 * sides * tokens * heads * DV * width, 2 * heads * DV * width),
        name="output",
    )(attended, embedded, rowcol_weight, *later_blocks)

    def total(*parts):
        return sum(x.astype(F32) for x in parts).astype(BF16)

    if ring:
        turned = lax.ppermute(part_pair, "seq", pair_swap)
        part_pair = total(part_pair, jnp.concatenate([turned[pair_rows:], turned[:pair_rows]]))
    projected = total(part_pair, lax.ppermute(part_pair, "col", swap))
    sums = total(keep, lax.ppermute(give, "col", swap))

    if ring:
        sent = sums[own_rows:]
        crossed = lax.ppermute(sent, "seq", pair_swap)
        rows_all = after(projected, sent)
        rows_all = jnp.concatenate([rows_all, lax.ppermute(rows_all, "seq", [(i, i ^ 2) for i in range(count)])])
        rows_all = after(rows_all, crossed)
        pairs = [(i * cols + i // 4, (i ^ 4) * cols + i // 4) for i in range(count)]
        far_rows = lax.ppermute(rows_all, ("seq", "col"), pairs)
        rows_all = jnp.where(lax.axis_index("seq") // 4 == col, rows_all, far_rows)
    else:
        rows_all = lax.all_gather(projected, "seq", axis=0, tiled=True)

    parts = [sums[:own_rows]]
    if ring:
        parts.append(crossed)
    out_tokens = pl.pallas_call(
        token_kernel,
        out_shape=shape((own_rows, width), BF16),
        in_specs=vspec(1 + len(parts)),
        out_specs=pl.BlockSpec(memory_space=VMEM),
        compiler_params=params(12),
        cost_estimate=cost(3 * own_rows * width, 8 * own_rows * width),
        name="tokens",
    )(embedded, *parts)

    span = pair_rows * count // cols
    pair_features = pair_weight.shape[0]
    pair_out = pl.pallas_call(
        pair_kernel,
        out_shape=shape((pair_rows, span, pair_features), BF16),
        in_specs=vspec(3),
        out_specs=pl.BlockSpec(memory_space=VMEM),
        scratch_shapes=[pltpu.VMEM((span, pair_features), F32)],
        compiler_params=params(16),
        cost_estimate=cost(2 * pair_rows * span * pair_features**2, 2 * pair_rows * span * pair_features),
        name="pair",
    )(projected[:pair_rows], rows_all, pair_weight)
    return out_tokens, pair_out


def solution(mesh):
    placed = (
        P(("grp", "seq"), "col"),
        P(None, None, "col"),
        P(),
        P("col", "seq"),
        P(),
        P("seq", None),
        P("seq", None),
        P(None, "seq"),
        P(),
        P(),
    )
    return jax.shard_map(
        on_device,
        mesh=mesh,
        in_specs=placed,
        out_specs=(P(("grp", "seq", "col"), None), P(("grp", "seq"), "col", None)),
        check_vma=False,
    )
```

```python
import functools
import math

import jax
import jax.numpy as jnp
from jax import lax
from jax.experimental import pallas as pl
from jax.experimental.pallas import tpu as pltpu
from jax.sharding import PartitionSpec as P

DK = 128
DV = 192
POOL = 4
PAIR_POOL = 16
EPS = 1e-06
VMEM = pltpu.VMEM
F32 = jnp.float32
BF16 = jnp.bfloat16


def gelu(x):
    c = math.sqrt(2.0 / math.pi)
    half = 0.5 * x
    return half + half * jnp.tanh(x * (c + (0.044715 * c) * (x * x)))


def dot_nt(a, b):
    return lax.dot_general(a, b, (((1,), (1,)), ((), ())), preferred_element_type=F32)


def dot_nn(a, b):
    return lax.dot_general(a, b, (((1,), (0,)), ((), ())), preferred_element_type=F32)


def params(mib, **kw):
    return pltpu.CompilerParams(vmem_limit_bytes=mib << 20, **kw)


def vspec(n):
    return [pl.BlockSpec(memory_space=VMEM)] * n


def hspec(n):
    return [pl.BlockSpec(memory_space=pltpu.HBM)] * n


RING = (0, 1, 3, 2)


def planned(count, groups):
    return count == 2 * len(RING) and groups == 2


def pick(index, table):
    value = jnp.int32(table[0])
    for i, entry in enumerate(table[1:], 1):
        value = jnp.where(index == i, jnp.int32(entry), value)
    return value


def owners(count, groups):
    if not planned(count, groups):
        return [jnp.int32(0)]
    group, me = lax.axis_index("grp"), lax.axis_index("seq")
    side, place = me % 2, pick(me // 2, [RING.index(i) for i in range(4)])
    result = []
    for step in (0, 3 + 2 * group, 1 + 2 * group, 2):
        row = pick(lax.rem(place + step, 4), RING)
        result += [2 * row + side, 2 * row + 1 - side]
    return result


class Blocks:
    def __init__(self, own, count):
        self.count = count
        self.at = {"own": own}

    def along(self, source, target):
        pairs = []
        for group in range(2):
            for k in range(4):
                a, b = RING[k], RING[(k + 1) % 4]
                if group:
                    a, b = b, a
                pairs += [(group * self.count + 2 * a + i, group * self.count + 2 * b + i) for i in range(2)]
        self.at[target] = lax.ppermute(self.at[source], ("grp", "seq"), pairs)

    def across(self, source, target):
        self.at[target] = lax.ppermute(self.at[source], "seq", [(i, i ^ 1) for i in range(self.count)])

    def between(self, source, target):
        self.at[target] = lax.ppermute(self.at[source], "grp", [(0, 1), (1, 0)])

    def pieces(self):
        names = ("own", "own2", "step", "step2", "cross", "cross2", "far", "far2")
        return [self.at[name] for name in names]


def after(values, *done):
    return lax.optimization_barrier((values, done))[0]


def window_means(first_row, rows, tokens, taps, positions, columns):
    r = lax.broadcasted_iota(jnp.int32, (rows, columns), 0) + first_row
    k = lax.broadcasted_iota(jnp.int32, (rows, columns), 1)
    reach = taps // 2
    if columns != positions:
        k = jnp.where(k < 2 * reach, jnp.where(k < reach, k - reach, k - reach + positions), -positions)
    tap = r // tokens
    gap = k - (POOL * (r - tap * tokens) + tap - reach)
    return jnp.where((gap >= 0) & (gap < POOL), 1.0 / POOL, 0.0).astype(BF16)


def act_kernel(taps, own_ref, other_ref, gain_ref, out_ref, residual_ref, act, gaincol):
    channels, positions = act.shape
    half = own_ref.shape[0]
    col = lax.axis_index("col")
    gaincol[...] = jnp.broadcast_to(gain_ref[...], (8, channels)).T
    step = 64
    halves = ((own_ref, col), (other_ref, 1 - col))
    squares = jnp.zeros((8, positions), F32)
    for ref, _ in halves:
        for j in range(half // step):
            x = ref[j * step:(j + 1) * step, :].astype(F32)
            x = x * x
            for i in range(step // 8):
                squares = squares + x[i * 8:(i + 1) * 8]
    scale = lax.rsqrt(jnp.sum(squares, axis=0, keepdims=True) / channels + EPS)
    for ref, index in halves:
        for j in range(half // step):
            at = pl.multiple_of(index * half + j * step, step)
            x = ref[j * step:(j + 1) * step, :].astype(F32) * scale
            act[pl.ds(at, step), :] = gelu(x * gaincol[pl.ds(at, step), :1]).astype(BF16)
    rows, tokens = out_ref.shape[0], residual_ref.shape[0]
    means = window_means(0, rows, tokens, taps, positions, positions)
    out_ref[...] = dot_nt(means, act[...]).astype(BF16)
    middle = (taps // 2) * tokens
    residual_ref[...] = dot_nt(means[middle:middle + tokens], own_ref[...])


def conv_kernel(positions, windows_ref, residual_ref, halo_ref, gain_ref, weight_hbm, out_ref, weights, sems):
    taps, _, channels = weights.shape
    copies = [pltpu.make_async_copy(weight_hbm.at[t], weights.at[t], sems.at[t]) for t in range(taps)]
    ahead = 2
    for c in copies[:ahead]:
        c.start()
    tokens = out_ref.shape[0]
    h = halo_ref[...].astype(F32)
    h = h * lax.rsqrt(jnp.sum(h * h, axis=1, keepdims=True) / channels + EPS) * gain_ref[...]
    h = gelu(h).astype(BF16)
    total = residual_ref[...]
    for t in range(taps):
        window = windows_ref[t * tokens:(t + 1) * tokens]
        if t != taps // 2:
            edges = dot_nn(window_means(t * tokens, tokens, tokens, taps, positions, h.shape[0]), h)
            window = (window.astype(F32) + edges).astype(BF16)
        copies[t].wait()
        if t + ahead < taps:
            copies[t + ahead].start()
        total = total + dot_nt(window, weights[t])
    out_ref[...] = total.astype(BF16)


def block_owners():
    return owners(lax.axis_size("seq"), lax.axis_size("grp"))


def embed_kernel(pieces, pooled_ref, *refs):
    blocks, (out_ref, rest_ref) = refs[:pieces], refs[pieces:]
    half = pooled_ref.shape[1]
    for ref, owner in zip(blocks, block_owners()):
        out_ref[owner] = dot_nt(pooled_ref[...], ref[:, :half]).astype(BF16)
        rest_ref[owner] = ref[:, half:]


def keyvalue_kernel(part_ref, other_ref, gain_ref, weight_ref, kv_ref, normed_ref, embedded_ref):
    count, _, width = part_ref.shape
    e = (part_ref[...].astype(F32) + other_ref[...].astype(F32)).astype(BF16)
    embedded_ref[...] = e
    e = e.astype(F32)
    squares = jnp.sum(jnp.sum(e * e, axis=0), axis=1, keepdims=True)
    scale = lax.rsqrt(squares / (count * width) + EPS)
    normed_ref[...] = (e * scale[None] * gain_ref[...]).astype(BF16)
    total = 0.0
    for s in range(count):
        total = total + dot_nn(normed_ref[s], weight_ref[s])
    kv = total.T.astype(BF16)
    kv_ref[...] = kv


def later_blocks_of(refs):
    places = block_owners()
    per = len(places) // len(refs)
    rows = refs[0].shape[0] // per
    for i, place in enumerate(places):
        start = (i % per) * rows
        yield refs[i // per], slice(start, start + rows), place


def query_kernel(sides, *refs):
    normed, pieces, query_ref = refs[:sides], refs[sides:-1], refs[-1]
    features = query_ref.shape[1]
    tokens = normed[0].shape[1]
    totals = [0.0] * sides
    for ref, rows, place in later_blocks_of(pieces):
        weight = ref[rows, :features]
        totals = [t + dot_nn(n[place], weight) for t, n in zip(totals, normed)]
    for i, total in enumerate(totals):
        query_ref[i * tokens:(i + 1) * tokens] = (total * DK ** (-0.5)).astype(BF16)


def attend_kernel(query_ref, own_ref, other_ref, out_ref, keys, values):
    tokens, features = query_ref.shape
    blocks, _, each = own_ref.shape
    first = lax.axis_index("col") == 0
    for i in range(blocks):
        keys[:, i * each:(i + 1) * each] = jnp.where(first, own_ref[i][:DK], other_ref[i][:DK])
        values[:, i * each:(i + 1) * each] = jnp.where(first, other_ref[i], own_ref[i])
    for h in range(features // DK):
        scores = dot_nn(query_ref[:, h * DK:(h + 1) * DK], keys[...])
        weights = jnp.exp(scores - jnp.max(scores, axis=1, keepdims=True))
        total = jnp.sum(weights, axis=1, keepdims=True)
        out_ref[h] = (dot_nt(weights.astype(BF16), values[...]) / total).astype(BF16)


def output_kernel(sides, features, attended_ref, embedded_ref, pair_weight_ref, *refs):
    pieces, (keep_ref, give_ref, pair_ref, whole) = refs[:-4], refs[-4:]
    heads = attended_ref.shape[0]
    flat = jnp.concatenate([attended_ref[h] for h in range(heads)], axis=1)
    _, tokens, width = embedded_ref.shape
    col = lax.axis_index("col")
    share = jnp.where(col == 0, 1.0, 0.0)
    projected = 0.0
    for ref, rows, place in later_blocks_of(pieces):
        part = dot_nt(flat, ref[rows, features:])
        whole[place] = part.astype(BF16)
        pooled = jnp.mean(part.reshape(sides * tokens // PAIR_POOL, PAIR_POOL, width), axis=1)
        first = jnp.mean(embedded_ref[place].astype(F32).reshape(tokens // PAIR_POOL, PAIR_POOL, width), axis=1) * share
        if sides > 1:
            first = jnp.concatenate([first, jnp.zeros((pooled.shape[0] - first.shape[0], width), F32)], axis=0)
        weight = pair_weight_ref[pl.ds(pl.multiple_of(place * width, width), width)]
        projected = projected + dot_nn((pooled + first).astype(BF16), weight)
    pair_ref[...] = projected.astype(BF16)
    own = keep_ref.shape[0] // sides
    for i in range(sides):
        for ref, core in ((keep_ref, col), (give_ref, 1 - col)):
            rows = pl.ds(pl.multiple_of(i * tokens + core * own, own), own)
            ref[i * own:(i + 1) * own] = jnp.concatenate([whole[s, rows] for s in range(whole.shape[0])], axis=1)


def token_kernel(embedded_ref, *refs):
    parts, token_ref = refs[:-1], refs[-1]
    own = token_ref.shape[0]
    mine = pl.ds(pl.multiple_of(lax.axis_index("col") * own, own), own)
    embedded = jnp.concatenate([embedded_ref[s, mine] for s in range(embedded_ref.shape[0])], axis=1)
    token_ref[...] = (embedded.astype(F32) + sum(part[...].astype(F32) for part in parts)).astype(BF16)


def pair_kernel(own_ref, all_ref, weight_ref, out_ref, columns_here):
    seq, col = lax.axis_index("seq"), lax.axis_index("col")
    features, each = weight_ref.shape[0], own_ref.shape[0]
    span = columns_here.shape[0] // each
    rows = all_ref[...].astype(F32)[:, features:]
    if rows.shape[0] == columns_here.shape[0]:
        for j in range(span):
            at = pl.multiple_of((j ^ (seq % span)) * each, each)
            columns_here[pl.ds(at, each)] = rows[j * each:(j + 1) * each]
    else:
        half = columns_here.shape[0]
        columns_here[...] = jnp.where(col == 0, rows[:half], rows[half:])
    rows_here = own_ref[...].astype(F32)[:, :features]
    hidden = gelu(rows_here[:, None, :] + columns_here[...][None, :, :])
    r, c, f = hidden.shape
    out_ref[...] = dot_nn(hidden.reshape(r * c, f).astype(BF16), weight_ref[...]).reshape(r, c, f).astype(BF16)


def cost(flops, size):
    return pl.CostEstimate(flops=int(flops), bytes_accessed=int(size), transcendentals=0)


def on_device(signal, conv_weight, conv_gain, embed_weight, attn_gain, query_weight, keyvalue_weight,
              output_weight, rowcol_weight, pair_weight):
    col = lax.axis_index("col")
    count, cols = lax.axis_size("seq"), lax.axis_size("col")
    positions, half = signal.shape
    taps, channels, _ = conv_weight.shape
    reach = taps // 2
    tokens = positions // POOL
    width = embed_weight.shape[1] * count
    features = query_weight.shape[1] // cols
    heads = features // DK
    swap = [(i, (i + 1) % cols) for i in range(cols)]
    shape = jax.ShapeDtypeStruct

    embed_own = jnp.concatenate(
        [embed_weight.T, lax.dynamic_slice_in_dim(keyvalue_weight, col * DK, DV, 1)], axis=1
    )
    ring = planned(count, lax.axis_size("grp")) and cols == 2
    sides = 2 if ring else 1
    side = lax.axis_index("seq") % sides
    pair_swap = [(i, i ^ 1) for i in range(count)]
    heads, features = heads // sides, features // sides

    def later_part(which):
        place = col * sides + which
        return jnp.concatenate(
            [
                lax.dynamic_slice_in_dim(query_weight, place * features, features, 1),
                lax.dynamic_slice_in_dim(output_weight.T, place * heads * DV, heads * DV, 1),
            ],
            axis=1,
        )

    e = Blocks(embed_own, count)

    signal_t = signal.T
    up = [(i, i + 1) for i in range(count - 1)]
    if ring:
        e.along("own", "step")
        e.across("own", "own2")
    before = lax.ppermute(signal[positions - reach:], "seq", up)
    behind = lax.ppermute(signal[:reach], "seq", [(j, i) for i, j in up])
    later_mine, later_theirs = later_part(side), later_part(1 - side) if ring else None
    ready = signal_t
    if ring:
        ready = after(signal_t, e.at["step"], e.at["own2"], before, behind, later_mine, later_theirs)
    other_t = lax.ppermute(ready, "col", swap)
    own_halo = jnp.pad(jnp.concatenate([before, behind], axis=0), ((0, 16 - 2 * reach), (0, 0)))
    other_halo = lax.ppermute(own_halo, "col", swap)
    halo = jnp.where(
        col == 0, jnp.concatenate([own_halo, other_halo], axis=1), jnp.concatenate([other_halo, own_halo], axis=1)
    )
    gain_row = conv_gain.reshape(1, channels)
    windows, residual = pl.pallas_call(
        functools.partial(act_kernel, taps),
        out_shape=(shape((taps * tokens, channels), BF16), shape((tokens, half), F32)),
        in_specs=vspec(3),
        out_specs=vspec(2),
        scratch_shapes=[pltpu.VMEM((channels, positions), BF16), pltpu.VMEM((channels, 8), F32)],
        compiler_params=params(20),
        cost_estimate=cost(2 * taps * tokens * channels * positions, 4 * channels * positions),
        name="act",
    )(signal_t, other_t, gain_row)
    if ring:
        e.at["step"] = after(e.at["step"], e.at["own2"])
        e.along("step", "far")
        e.across("step", "step2")
        e.between("step", "cross")
    pooled = pl.pallas_call(
        functools.partial(conv_kernel, positions),
        out_shape=shape((tokens, half), BF16),
        in_specs=vspec(4) + hspec(1),
        out_specs=pl.BlockSpec(memory_space=VMEM),
        scratch_shapes=[pltpu.VMEM((taps, half, channels), BF16), pltpu.SemaphoreType.DMA((taps,))],
        compiler_params=params(50),
        cost_estimate=cost(2 * taps * tokens * channels * half, 2 * taps * channels * half),
        name="conv",
    )(windows, residual, halo, gain_row, conv_weight.transpose(0, 2, 1))
    if ring:
        e.at["far"] = after(e.at["far"], pooled, e.at["cross"])
        e.at["step2"] = after(e.at["step2"], pooled, e.at["cross"])
        e.along("step2", "far2")
        e.between("step2", "cross2")
        theirs = after(later_theirs, pooled, e.at["cross"])
        received = lax.ppermute(theirs, "seq", pair_swap)
        pooled = after(pooled, received)
        q = Blocks(jnp.concatenate([later_mine, received]), count)
        q.at["own"] = after(q.at["own"], e.at["far2"])
        q.along("own", "step")
        embed_blocks = e.pieces()
    else:
        embed_blocks, later_blocks = (
            [lax.all_gather(x, "seq", axis=0, tiled=True)] for x in (embed_own, later_mine)
        )
    pieces = len(embed_blocks)
    block = width // pieces

    part, keyvalue_blocks = pl.pallas_call(
        functools.partial(embed_kernel, pieces),
        out_shape=(shape((pieces, tokens, block), BF16), shape((pieces, block, DV), BF16)),
        in_specs=vspec(1 + pieces),
        out_specs=vspec(2),
        compiler_params=params(12),
        cost_estimate=cost(2 * tokens * half * width, 2 * half * width),
        name="embed",
    )(pooled, *embed_blocks)
    other_part = lax.ppermute(part, "col", swap)

    keyvalue, normed, embedded = pl.pallas_call(
        keyvalue_kernel,
        out_shape=(
            shape((DV, tokens), BF16),
            shape((pieces, tokens, block), BF16),
            shape((pieces, tokens, block), BF16),
        ),
        in_specs=vspec(4),
        out_specs=vspec(3),
        compiler_params=params(16),
        cost_estimate=cost(2 * tokens * width * DV, 2 * width * DV),
        name="keyvalue",
    )(part, other_part, attn_gain.reshape(pieces, 1, block), keyvalue_blocks)
    both_normed = [normed]
    if ring:
        turns = [[(2 * RING[k] + i, 2 * RING[(k + t) % 4] + i) for k in range(4) for i in range(2)] for t in (1, 3, 2)]
        turned = [lax.ppermute(keyvalue, "seq", turn) for turn in turns]
        both_normed.append(lax.ppermute(normed, "seq", pair_swap))
        q.along("step", "far")
        q.between("step", "cross")
        later_blocks = [q.at[name] for name in ("own", "step", "cross", "far")]
        row = jnp.stack([keyvalue] + after(turned, q.at["step"]))
        gathered = jnp.concatenate([row, lax.ppermute(row, "seq", pair_swap)])
    else:
        gathered = lax.all_gather(keyvalue, "seq", axis=0)
    gathered_other = lax.ppermute(gathered, "col", swap)

    queries = pl.pallas_call(
        functools.partial(query_kernel, sides),
        out_shape=shape((sides * tokens, features), BF16),
        in_specs=vspec(sides + len(later_blocks)),
        out_specs=pl.BlockSpec(memory_space=VMEM),
        compiler_params=params(12),
        cost_estimate=cost(2 * sides * tokens * width * features, 2 * width * features),
        name="query",
    )(*both_normed, *later_blocks)

    attended = pl.pallas_call(
        attend_kernel,
        out_shape=shape((heads, sides * tokens, DV), BF16),
        in_specs=vspec(3),
        out_specs=pl.BlockSpec(memory_space=VMEM),
        scratch_shapes=[pltpu.VMEM((DK, count * tokens), BF16), pltpu.VMEM((DV, count * tokens), BF16)],
        compiler_params=params(24),
        cost_estimate=cost(2 * tokens * heads * count * tokens * (DK + DV), 4 * count * tokens * DV),
        name="attend",
    )(queries, gathered, gathered_other)

    out_width = rowcol_weight.shape[1]
    own_rows, pair_rows = tokens // cols, tokens // PAIR_POOL
    kept = shape((sides * own_rows, width), BF16)
    keep, give, part_pair = pl.pallas_call(
        functools.partial(output_kernel, sides, features),
        out_shape=(kept, kept, shape((sides * pair_rows, out_width), BF16)),
        in_specs=vspec(3 + len(later_blocks)),
        out_specs=vspec(3),
        scratch_shapes=[pltpu.VMEM((pieces, sides * tokens, block), BF16)],
        compiler_params=params(16),
        cost_estimate=cost(2 * sides * tokens * heads * DV * width, 2 * heads * DV * width),
        name="output",
    )(attended, embedded, rowcol_weight, *later_blocks)

    def total(*parts):
        return sum(x.astype(F32) for x in parts).astype(BF16)

    if ring:
        turned = lax.ppermute(part_pair, "seq", pair_swap)
        part_pair = total(part_pair, jnp.concatenate([turned[pair_rows:], turned[:pair_rows]]))
    projected = total(part_pair, lax.ppermute(part_pair, "col", swap))
    sums = total(keep, lax.ppermute(give, "col", swap))

    if ring:
        sent = sums[own_rows:]
        crossed = lax.ppermute(sent, "seq", pair_swap)
        rows_all = after(projected, sent)
        rows_all = jnp.concatenate([rows_all, lax.ppermute(rows_all, "seq", [(i, i ^ 2) for i in range(count)])])
        rows_all = after(rows_all, crossed)
        pairs = [(i * cols + i // 4, (i ^ 4) * cols + i // 4) for i in range(count)]
        far_rows = lax.ppermute(rows_all, ("seq", "col"), pairs)
        rows_all = jnp.where(lax.axis_index("seq") // 4 == col, rows_all, far_rows)
    else:
        rows_all = lax.all_gather(projected, "seq", axis=0, tiled=True)

    parts = [sums[:own_rows]]
    if ring:
        parts.append(crossed)
    out_tokens = pl.pallas_call(
        token_kernel,
        out_shape=shape((own_rows, width), BF16),
        in_specs=vspec(1 + len(parts)),
        out_specs=pl.BlockSpec(memory_space=VMEM),
        compiler_params=params(12),
        cost_estimate=cost(3 * own_rows * width, 8 * own_rows * width),
        name="tokens",
    )(embedded, *parts)

    span = pair_rows * count // cols
    pair_features = pair_weight.shape[0]
    pair_out = pl.pallas_call(
        pair_kernel,
        out_shape=shape((pair_rows, span, pair_features), BF16),
        in_specs=vspec(3),
        out_specs=pl.BlockSpec(memory_space=VMEM),
        scratch_shapes=[pltpu.VMEM((span, pair_features), F32)],
        compiler_params=params(16),
        cost_estimate=cost(2 * pair_rows * span * pair_features**2, 2 * pair_rows * span * pair_features),
        name="pair",
    )(projected[:pair_rows], rows_all, pair_weight)
    return out_tokens, pair_out


def solution(mesh):
    placed = (
        P(("grp", "seq"), "col"),
        P(None, None, "col"),
        P(),
        P("col", "seq"),
        P(),
        P("seq", None),
        P("seq", None),
        P(None, "seq"),
        P(),
        P(),
    )
    return jax.shard_map(
        on_device,
        mesh=mesh,
        in_specs=placed,
        out_specs=(P(("grp", "seq", "col"), None), P(("grp", "seq"), "col", None)),
        check_vma=False,
    )
```

```python
import functools
import math

import jax
import jax.numpy as jnp
from jax import lax
from jax.experimental import pallas as pl
from jax.experimental.pallas import tpu as pltpu
from jax.sharding import PartitionSpec as P

DK = 128
DV = 192
POOL = 4
PAIR_POOL = 16
EPS = 1e-06
VMEM = pltpu.VMEM
F32 = jnp.float32
BF16 = jnp.bfloat16


def gelu(x):
    c = math.sqrt(2.0 / math.pi)
    half = 0.5 * x
    return half + half * jnp.tanh(x * (c + (0.044715 * c) * (x * x)))


def dot_nt(a, b):
    return lax.dot_general(a, b, (((1,), (1,)), ((), ())), preferred_element_type=F32)


def dot_nn(a, b):
    return lax.dot_general(a, b, (((1,), (0,)), ((), ())), preferred_element_type=F32)


def params(mib, **kw):
    return pltpu.CompilerParams(vmem_limit_bytes=mib << 20, **kw)


def vspec(n):
    return [pl.BlockSpec(memory_space=VMEM)] * n


def hspec(n):
    return [pl.BlockSpec(memory_space=pltpu.HBM)] * n


RING = (0, 1, 3, 2)


def planned(count, groups):
    return count == 2 * len(RING) and groups == 2


def pick(index, table):
    value = jnp.int32(table[0])
    for i, entry in enumerate(table[1:], 1):
        value = jnp.where(index == i, jnp.int32(entry), value)
    return value


def owners(count, groups):
    if not planned(count, groups):
        return [jnp.int32(0)]
    group, me = lax.axis_index("grp"), lax.axis_index("seq")
    side, place = me % 2, pick(me // 2, [RING.index(i) for i in range(4)])
    result = []
    for step in (0, 3 + 2 * group, 1 + 2 * group, 2):
        row = pick(lax.rem(place + step, 4), RING)
        result += [2 * row + side, 2 * row + 1 - side]
    return result


class Blocks:
    def __init__(self, own, count):
        self.count = count
        self.at = {"own": own}

    def along(self, source, target):
        pairs = []
        for group in range(2):
            for k in range(4):
                a, b = RING[k], RING[(k + 1) % 4]
                if group:
                    a, b = b, a
                pairs += [(group * self.count + 2 * a + i, group * self.count + 2 * b + i) for i in range(2)]
        self.at[target] = lax.ppermute(self.at[source], ("grp", "seq"), pairs)

    def across(self, source, target):
        self.at[target] = lax.ppermute(self.at[source], "seq", [(i, i ^ 1) for i in range(self.count)])

    def between(self, source, target):
        self.at[target] = lax.ppermute(self.at[source], "grp", [(0, 1), (1, 0)])

    def pieces(self):
        names = ("own", "own2", "step", "step2", "cross", "cross2", "far", "far2")
        return [self.at[name] for name in names]


def after(values, *done):
    return lax.optimization_barrier((values, done))[0]


def window_means(first_row, rows, tokens, taps, positions, columns):
    r = lax.broadcasted_iota(jnp.int32, (rows, columns), 0) + first_row
    k = lax.broadcasted_iota(jnp.int32, (rows, columns), 1)
    reach = taps // 2
    if columns != positions:
        k = jnp.where(k < 2 * reach, jnp.where(k < reach, k - reach, k - reach + positions), -positions)
    tap = r // tokens
    gap = k - (POOL * (r - tap * tokens) + tap - reach)
    return jnp.where((gap >= 0) & (gap < POOL), 1.0 / POOL, 0.0).astype(BF16)


def act_kernel(taps, own_ref, other_ref, gain_ref, out_ref, residual_ref, act, gaincol):
    channels, positions = act.shape
    half = own_ref.shape[0]
    col = lax.axis_index("col")
    gaincol[...] = jnp.broadcast_to(gain_ref[...], (8, channels)).T
    step = 64
    halves = ((own_ref, col), (other_ref, 1 - col))
    squares = jnp.zeros((8, positions), F32)
    for ref, _ in halves:
        for j in range(half // step):
            x = ref[j * step:(j + 1) * step, :].astype(F32)
            x = x * x
            for i in range(step // 8):
                squares = squares + x[i * 8:(i + 1) * 8]
    scale = lax.rsqrt(jnp.sum(squares, axis=0, keepdims=True) / channels + EPS)
    for ref, index in halves:
        for j in range(half // step):
            at = pl.multiple_of(index * half + j * step, step)
            x = ref[j * step:(j + 1) * step, :].astype(F32) * scale
            act[pl.ds(at, step), :] = gelu(x * gaincol[pl.ds(at, step), :1]).astype(BF16)
    rows, tokens = out_ref.shape[0], residual_ref.shape[0]
    means = window_means(0, rows, tokens, taps, positions, positions)
    out_ref[...] = dot_nt(means, act[...]).astype(BF16)
    middle = (taps // 2) * tokens
    residual_ref[...] = dot_nt(means[middle:middle + tokens], own_ref[...])


def conv_kernel(positions, windows_ref, residual_ref, halo_ref, gain_ref, weight_hbm, out_ref, weights, sems):
    taps, _, channels = weights.shape
    copies = [pltpu.make_async_copy(weight_hbm.at[t], weights.at[t], sems.at[t]) for t in range(taps)]
    ahead = 2
    for c in copies[:ahead]:
        c.start()
    tokens = out_ref.shape[0]
    h = halo_ref[...].astype(F32)
    h = h * lax.rsqrt(jnp.sum(h * h, axis=1, keepdims=True) / channels + EPS) * gain_ref[...]
    h = gelu(h).astype(BF16)
    total = residual_ref[...]
    for t in range(taps):
        window = windows_ref[t * tokens:(t + 1) * tokens]
        if t != taps // 2:
            edges = dot_nn(window_means(t * tokens, tokens, tokens, taps, positions, h.shape[0]), h)
            window = (window.astype(F32) + edges).astype(BF16)
        copies[t].wait()
        if t + ahead < taps:
            copies[t + ahead].start()
        total = total + dot_nt(window, weights[t])
    out_ref[...] = total.astype(BF16)


def block_owners():
    return owners(lax.axis_size("seq"), lax.axis_size("grp"))


def embed_kernel(pieces, pooled_ref, *refs):
    blocks, (out_ref, rest_ref) = refs[:pieces], refs[pieces:]
    half = pooled_ref.shape[1]
    for ref, owner in zip(blocks, block_owners()):
        out_ref[owner] = dot_nt(pooled_ref[...], ref[:, :half]).astype(BF16)
        rest_ref[owner] = ref[:, half:]


def keyvalue_kernel(part_ref, other_ref, gain_ref, weight_ref, kv_ref, normed_ref, embedded_ref, *send_ref):
    count, _, width = part_ref.shape
    e = (part_ref[...].astype(F32) + other_ref[...].astype(F32)).astype(BF16)
    embedded_ref[...] = e
    e = e.astype(F32)
    squares = jnp.sum(jnp.sum(e * e, axis=0), axis=1, keepdims=True)
    scale = lax.rsqrt(squares / (count * width) + EPS)
    normed_ref[...] = (e * scale[None] * gain_ref[...]).astype(BF16)
    total = 0.0
    for s in range(count):
        total = total + dot_nn(normed_ref[s], weight_ref[s])
    kv = total.T.astype(BF16)
    kv_ref[...] = kv
    for ref in send_ref:
        ref[...] = jnp.concatenate([normed_ref[s] for s in range(count)], axis=1)


def later_blocks_of(refs):
    places = block_owners()
    per = len(places) // len(refs)
    rows = refs[0].shape[0] // per
    for i, place in enumerate(places):
        start = (i % per) * rows
        yield refs[i // per], slice(start, start + rows), place


def query_kernel(sides, *refs):
    normed, pieces, query_ref = list(refs[:sides]), refs[sides:-sides], refs[-sides]
    features = query_ref.shape[1]
    count, tokens, width = normed[0].shape
    if sides > 1:
        for s in range(count):
            refs[-1][s] = normed[1][:, s * width:(s + 1) * width]
        normed[1] = refs[-1]
    totals = [0.0] * sides
    for ref, rows, place in later_blocks_of(pieces):
        weight = ref[rows, :features]
        totals = [t + dot_nn(n[place], weight) for t, n in zip(totals, normed)]
    for i, total in enumerate(totals):
        query_ref[i * tokens:(i + 1) * tokens] = (total * DK ** (-0.5)).astype(BF16)


def attend_kernel(query_ref, own_ref, other_ref, out_ref, keys, values):
    tokens, features = query_ref.shape
    blocks, _, each = own_ref.shape
    first = lax.axis_index("col") == 0
    for i in range(blocks):
        keys[:, i * each:(i + 1) * each] = jnp.where(first, own_ref[i][:DK], other_ref[i][:DK])
        values[:, i * each:(i + 1) * each] = jnp.where(first, other_ref[i], own_ref[i])
    for h in range(features // DK):
        scores = dot_nn(query_ref[:, h * DK:(h + 1) * DK], keys[...])
        weights = jnp.exp(scores - jnp.max(scores, axis=1, keepdims=True))
        total = jnp.sum(weights, axis=1, keepdims=True)
        out_ref[h] = (dot_nt(weights.astype(BF16), values[...]) / total).astype(BF16)


def output_kernel(sides, features, attended_ref, embedded_ref, pair_weight_ref, *refs):
    pieces, (keep_ref, give_ref, pair_ref, whole) = refs[:-4], refs[-4:]
    heads = attended_ref.shape[0]
    flat = jnp.concatenate([attended_ref[h] for h in range(heads)], axis=1)
    _, tokens, width = embedded_ref.shape
    col = lax.axis_index("col")
    share = jnp.where(col == 0, 1.0, 0.0)
    projected = 0.0
    for ref, rows, place in later_blocks_of(pieces):
        part = dot_nt(flat, ref[rows, features:])
        whole[place] = part.astype(BF16)
        pooled = jnp.mean(part.reshape(sides * tokens // PAIR_POOL, PAIR_POOL, width), axis=1)
        first = jnp.mean(embedded_ref[place].astype(F32).reshape(tokens // PAIR_POOL, PAIR_POOL, width), axis=1) * share
        if sides > 1:
            first = jnp.concatenate([first, jnp.zeros((pooled.shape[0] - first.shape[0], width), F32)], axis=0)
        weight = pair_weight_ref[pl.ds(pl.multiple_of(place * width, width), width)]
        projected = projected + dot_nn((pooled + first).astype(BF16), weight)
    pair_ref[...] = projected.astype(BF16)
    own = keep_ref.shape[0] // sides
    for i in range(sides):
        for ref, core in ((keep_ref, col), (give_ref, 1 - col)):
            rows = pl.ds(pl.multiple_of(i * tokens + core * own, own), own)
            ref[i * own:(i + 1) * own] = jnp.concatenate([whole[s, rows] for s in range(whole.shape[0])], axis=1)


def token_kernel(embedded_ref, *refs):
    parts, token_ref = refs[:-1], refs[-1]
    own = token_ref.shape[0]
    mine = pl.ds(pl.multiple_of(lax.axis_index("col") * own, own), own)
    embedded = jnp.concatenate([embedded_ref[s, mine] for s in range(embedded_ref.shape[0])], axis=1)
    token_ref[...] = (embedded.astype(F32) + sum(part[...].astype(F32) for part in parts)).astype(BF16)


def pair_kernel(own_ref, all_ref, weight_ref, out_ref, columns_here):
    seq, col = lax.axis_index("seq"), lax.axis_index("col")
    features, each = weight_ref.shape[0], own_ref.shape[0]
    span = columns_here.shape[0] // each
    rows = all_ref[...].astype(F32)[:, features:]
    if rows.shape[0] == columns_here.shape[0]:
        for j in range(span):
            at = pl.multiple_of((j ^ (seq % span)) * each, each)
            columns_here[pl.ds(at, each)] = rows[j * each:(j + 1) * each]
    else:
        half = columns_here.shape[0]
        columns_here[...] = jnp.where(col == 0, rows[:half], rows[half:])
    rows_here = own_ref[...].astype(F32)[:, :features]
    hidden = gelu(rows_here[:, None, :] + columns_here[...][None, :, :])
    r, c, f = hidden.shape
    out_ref[...] = dot_nn(hidden.reshape(r * c, f).astype(BF16), weight_ref[...]).reshape(r, c, f).astype(BF16)


def cost(flops, size):
    return pl.CostEstimate(flops=int(flops), bytes_accessed=int(size), transcendentals=0)


def on_device(signal, conv_weight, conv_gain, embed_weight, attn_gain, query_weight, keyvalue_weight,
              output_weight, rowcol_weight, pair_weight):
    col = lax.axis_index("col")
    count, cols = lax.axis_size("seq"), lax.axis_size("col")
    positions, half = signal.shape
    taps, channels, _ = conv_weight.shape
    reach = taps // 2
    tokens = positions // POOL
    width = embed_weight.shape[1] * count
    features = query_weight.shape[1] // cols
    heads = features // DK
    swap = [(i, (i + 1) % cols) for i in range(cols)]
    shape = jax.ShapeDtypeStruct

    embed_own = jnp.concatenate(
        [embed_weight.T, lax.dynamic_slice_in_dim(keyvalue_weight, col * DK, DV, 1)], axis=1
    )
    ring = planned(count, lax.axis_size("grp")) and cols == 2
    sides = 2 if ring else 1
    side = lax.axis_index("seq") % sides
    pair_swap = [(i, i ^ 1) for i in range(count)]
    heads, features = heads // sides, features // sides

    def later_part(which):
        place = col * sides + which
        return jnp.concatenate(
            [
                lax.dynamic_slice_in_dim(query_weight, place * features, features, 1),
                lax.dynamic_slice_in_dim(output_weight.T, place * heads * DV, heads * DV, 1),
            ],
            axis=1,
        )

    e = Blocks(embed_own, count)

    signal_t = signal.T
    up = [(i, i + 1) for i in range(count - 1)]
    if ring:
        e.along("own", "step")
        e.across("own", "own2")
    before = lax.ppermute(signal[positions - reach:], "seq", up)
    behind = lax.ppermute(signal[:reach], "seq", [(j, i) for i, j in up])
    later_mine, later_theirs = later_part(side), later_part(1 - side) if ring else None
    ready = signal_t
    if ring:
        ready = after(signal_t, e.at["step"], e.at["own2"], before, behind, later_mine, later_theirs)
    other_t = lax.ppermute(ready, "col", swap)
    own_halo = jnp.pad(jnp.concatenate([before, behind], axis=0), ((0, 16 - 2 * reach), (0, 0)))
    other_halo = lax.ppermute(own_halo, "col", swap)
    halo = jnp.where(
        col == 0, jnp.concatenate([own_halo, other_halo], axis=1), jnp.concatenate([other_halo, own_halo], axis=1)
    )
    gain_row = conv_gain.reshape(1, channels)
    windows, residual = pl.pallas_call(
        functools.partial(act_kernel, taps),
        out_shape=(shape((taps * tokens, channels), BF16), shape((tokens, half), F32)),
        in_specs=vspec(3),
        out_specs=vspec(2),
        scratch_shapes=[pltpu.VMEM((channels, positions), BF16), pltpu.VMEM((channels, 8), F32)],
        compiler_params=params(20),
        cost_estimate=cost(2 * taps * tokens * channels * positions, 4 * channels * positions),
        name="act",
    )(signal_t, other_t, gain_row)
    if ring:
        e.at["step"] = after(e.at["step"], e.at["own2"])
        e.along("step", "far")
        e.across("step", "step2")
        e.between("step", "cross")
    pooled = pl.pallas_call(
        functools.partial(conv_kernel, positions),
        out_shape=shape((tokens, half), BF16),
        in_specs=vspec(4) + hspec(1),
        out_specs=pl.BlockSpec(memory_space=VMEM),
        scratch_shapes=[pltpu.VMEM((taps, half, channels), BF16), pltpu.SemaphoreType.DMA((taps,))],
        compiler_params=params(50),
        cost_estimate=cost(2 * taps * tokens * channels * half, 2 * taps * channels * half),
        name="conv",
    )(windows, residual, halo, gain_row, conv_weight.transpose(0, 2, 1))
    if ring:
        e.at["far"] = after(e.at["far"], pooled, e.at["cross"])
        e.at["step2"] = after(e.at["step2"], pooled, e.at["cross"])
        e.along("step2", "far2")
        e.between("step2", "cross2")
        theirs = after(later_theirs, pooled, e.at["cross"])
        received = lax.ppermute(theirs, "seq", pair_swap)
        pooled = after(pooled, received)
        q = Blocks(jnp.concatenate([later_mine, received]), count)
        q.at["own"] = after(q.at["own"], e.at["far2"])
        q.along("own", "step")
        embed_blocks = e.pieces()
    else:
        embed_blocks, later_blocks = (
            [lax.all_gather(x, "seq", axis=0, tiled=True)] for x in (embed_own, later_mine)
        )
    pieces = len(embed_blocks)
    block = width // pieces

    part, keyvalue_blocks = pl.pallas_call(
        functools.partial(embed_kernel, pieces),
        out_shape=(shape((pieces, tokens, block), BF16), shape((pieces, block, DV), BF16)),
        in_specs=vspec(1 + pieces),
        out_specs=vspec(2),
        compiler_params=params(12),
        cost_estimate=cost(2 * tokens * half * width, 2 * half * width),
        name="embed",
    )(pooled, *embed_blocks)
    other_part = lax.ppermute(part, "col", swap)

    keyvalue, normed, embedded, *sending = pl.pallas_call(
        keyvalue_kernel,
        out_shape=(
            shape((DV, tokens), BF16),
            shape((pieces, tokens, block), BF16),
            shape((pieces, tokens, block), BF16),
        ) + (shape((tokens, width), BF16),) * (sides - 1),
        in_specs=vspec(4),
        out_specs=vspec(2 + sides),
        compiler_params=params(16),
        cost_estimate=cost(2 * tokens * width * DV, 2 * width * DV),
        name="keyvalue",
    )(part, other_part, attn_gain.reshape(pieces, 1, block), keyvalue_blocks)
    both_normed = [normed]
    if ring:
        turns = [[(2 * RING[k] + i, 2 * RING[(k + t) % 4] + i) for k in range(4) for i in range(2)] for t in (1, 3, 2)]
        turned = [lax.ppermute(keyvalue, "seq", turn) for turn in turns]
        both_normed.append(lax.ppermute(sending[0], "seq", pair_swap))
        q.at["step"] = after(q.at["step"], both_normed[1])
        q.along("step", "far")
        q.between("step", "cross")
        later_blocks = [q.at[name] for name in ("own", "step", "cross", "far")]
        row = jnp.stack([keyvalue] + after(turned, q.at["step"]))
        gathered = jnp.concatenate([row, lax.ppermute(row, "seq", pair_swap)])
    else:
        gathered = lax.all_gather(keyvalue, "seq", axis=0)
    gathered_other = lax.ppermute(gathered, "col", swap)

    queries = pl.pallas_call(
        functools.partial(query_kernel, sides),
        out_shape=shape((sides * tokens, features), BF16),
        in_specs=vspec(sides + len(later_blocks)),
        out_specs=pl.BlockSpec(memory_space=VMEM),
        scratch_shapes=[pltpu.VMEM((pieces, tokens, block), BF16)] * (sides - 1),
        compiler_params=params(12),
        cost_estimate=cost(2 * sides * tokens * width * features, 2 * width * features),
        name="query",
    )(*both_normed, *later_blocks)

    attended = pl.pallas_call(
        attend_kernel,
        out_shape=shape((heads, sides * tokens, DV), BF16),
        in_specs=vspec(3),
        out_specs=pl.BlockSpec(memory_space=VMEM),
        scratch_shapes=[pltpu.VMEM((DK, count * tokens), BF16), pltpu.VMEM((DV, count * tokens), BF16)],
        compiler_params=params(24),
        cost_estimate=cost(2 * tokens * heads * count * tokens * (DK + DV), 4 * count * tokens * DV),
        name="attend",
    )(queries, gathered, gathered_other)

    out_width = rowcol_weight.shape[1]
    own_rows, pair_rows = tokens // cols, tokens // PAIR_POOL
    kept = shape((sides * own_rows, width), BF16)
    keep, give, part_pair = pl.pallas_call(
        functools.partial(output_kernel, sides, features),
        out_shape=(kept, kept, shape((sides * pair_rows, out_width), BF16)),
        in_specs=vspec(3 + len(later_blocks)),
        out_specs=vspec(3),
        scratch_shapes=[pltpu.VMEM((pieces, sides * tokens, block), BF16)],
        compiler_params=params(16),
        cost_estimate=cost(2 * sides * tokens * heads * DV * width, 2 * heads * DV * width),
        name="output",
    )(attended, embedded, rowcol_weight, *later_blocks)

    def total(*parts):
        return sum(x.astype(F32) for x in parts).astype(BF16)

    if ring:
        turned = lax.ppermute(part_pair, "seq", pair_swap)
        part_pair = total(part_pair, jnp.concatenate([turned[pair_rows:], turned[:pair_rows]]))
    projected = total(part_pair, lax.ppermute(part_pair, "col", swap))
    sums = total(keep, lax.ppermute(give, "col", swap))

    if ring:
        sent = sums[own_rows:]
        crossed = lax.ppermute(sent, "seq", pair_swap)
        rows_all = after(projected, sent)
        rows_all = jnp.concatenate([rows_all, lax.ppermute(rows_all, "seq", [(i, i ^ 2) for i in range(count)])])
        rows_all = after(rows_all, crossed)
        pairs = [(i * cols + i // 4, (i ^ 4) * cols + i // 4) for i in range(count)]
        far_rows = lax.ppermute(rows_all, ("seq", "col"), pairs)
        rows_all = jnp.where(lax.axis_index("seq") // 4 == col, rows_all, far_rows)
    else:
        rows_all = lax.all_gather(projected, "seq", axis=0, tiled=True)

    parts = [sums[:own_rows]]
    if ring:
        parts.append(crossed)
    out_tokens = pl.pallas_call(
        token_kernel,
        out_shape=shape((own_rows, width), BF16),
        in_specs=vspec(1 + len(parts)),
        out_specs=pl.BlockSpec(memory_space=VMEM),
        compiler_params=params(12),
        cost_estimate=cost(3 * own_rows * width, 8 * own_rows * width),
        name="tokens",
    )(embedded, *parts)

    span = pair_rows * count // cols
    pair_features = pair_weight.shape[0]
    pair_out = pl.pallas_call(
        pair_kernel,
        out_shape=shape((pair_rows, span, pair_features), BF16),
        in_specs=vspec(3),
        out_specs=pl.BlockSpec(memory_space=VMEM),
        scratch_shapes=[pltpu.VMEM((span, pair_features), F32)],
        compiler_params=params(16),
        cost_estimate=cost(2 * pair_rows * span * pair_features**2, 2 * pair_rows * span * pair_features),
        name="pair",
    )(projected[:pair_rows], rows_all, pair_weight)
    return out_tokens, pair_out


def solution(mesh):
    placed = (
        P(("grp", "seq"), "col"),
        P(None, None, "col"),
        P(),
        P("col", "seq"),
        P(),
        P("seq", None),
        P("seq", None),
        P(None, "seq"),
        P(),
        P(),
    )
    return jax.shard_map(
        on_device,
        mesh=mesh,
        in_specs=placed,
        out_specs=(P(("grp", "seq", "col"), None), P(("grp", "seq"), "col", None)),
        check_vma=False,
    )
```

```python
import functools
import math

import jax
import jax.numpy as jnp
from jax import lax
from jax.experimental import pallas as pl
from jax.experimental.pallas import tpu as pltpu
from jax.sharding import PartitionSpec as P

DK = 128
DV = 192
POOL = 4
PAIR_POOL = 16
EPS = 1e-06
VMEM = pltpu.VMEM
F32 = jnp.float32
BF16 = jnp.bfloat16


def gelu(x):
    c = math.sqrt(2.0 / math.pi)
    half = 0.5 * x
    return half + half * jnp.tanh(x * (c + (0.044715 * c) * (x * x)))


def dot_nt(a, b):
    return lax.dot_general(a, b, (((1,), (1,)), ((), ())), preferred_element_type=F32)


def dot_nn(a, b):
    return lax.dot_general(a, b, (((1,), (0,)), ((), ())), preferred_element_type=F32)


def params(mib, **kw):
    return pltpu.CompilerParams(vmem_limit_bytes=mib << 20, **kw)


def vspec(n):
    return [pl.BlockSpec(memory_space=VMEM)] * n


def hspec(n):
    return [pl.BlockSpec(memory_space=pltpu.HBM)] * n


RING = (0, 1, 3, 2)


def planned(count, groups):
    return count == 2 * len(RING) and groups == 2


def pick(index, table):
    value = jnp.int32(table[0])
    for i, entry in enumerate(table[1:], 1):
        value = jnp.where(index == i, jnp.int32(entry), value)
    return value


def owners(count, groups):
    if not planned(count, groups):
        return [jnp.int32(0)]
    group, me = lax.axis_index("grp"), lax.axis_index("seq")
    side, place = me % 2, pick(me // 2, [RING.index(i) for i in range(4)])
    result = []
    for step in (0, 3 + 2 * group, 1 + 2 * group, 2):
        row = pick(lax.rem(place + step, 4), RING)
        result += [2 * row + side, 2 * row + 1 - side]
    return result


class Blocks:
    def __init__(self, own, count):
        self.count = count
        self.at = {"own": own}

    def along(self, source, target):
        pairs = []
        for group in range(2):
            for k in range(4):
                a, b = RING[k], RING[(k + 1) % 4]
                if group:
                    a, b = b, a
                pairs += [(group * self.count + 2 * a + i, group * self.count + 2 * b + i) for i in range(2)]
        self.at[target] = lax.ppermute(self.at[source], ("grp", "seq"), pairs)

    def across(self, source, target):
        self.at[target] = lax.ppermute(self.at[source], "seq", [(i, i ^ 1) for i in range(self.count)])

    def between(self, source, target):
        self.at[target] = lax.ppermute(self.at[source], "grp", [(0, 1), (1, 0)])

    def pieces(self):
        names = ("own", "own2", "step", "step2", "cross", "cross2", "far", "far2")
        return [self.at[name] for name in names]


def after(values, *done):
    return lax.optimization_barrier((values, done))[0]


def window_means(first_row, rows, tokens, taps, positions, columns):
    r = lax.broadcasted_iota(jnp.int32, (rows, columns), 0) + first_row
    k = lax.broadcasted_iota(jnp.int32, (rows, columns), 1)
    reach = taps // 2
    if columns != positions:
        k = jnp.where(k < 2 * reach, jnp.where(k < reach, k - reach, k - reach + positions), -positions)
    tap = r // tokens
    gap = k - (POOL * (r - tap * tokens) + tap - reach)
    return jnp.where((gap >= 0) & (gap < POOL), 1.0 / POOL, 0.0).astype(BF16)


def act_kernel(taps, own_ref, other_ref, gain_ref, out_ref, residual_ref, act, gaincol):
    channels, positions = act.shape
    half = own_ref.shape[0]
    col = lax.axis_index("col")
    gaincol[...] = jnp.broadcast_to(gain_ref[...], (8, channels)).T
    step = 64
    halves = ((own_ref, col), (other_ref, 1 - col))
    squares = jnp.zeros((8, positions), F32)
    for ref, _ in halves:
        for j in range(half // step):
            x = ref[j * step:(j + 1) * step, :].astype(F32)
            x = x * x
            for i in range(step // 8):
                squares = squares + x[i * 8:(i + 1) * 8]
    scale = lax.rsqrt(jnp.sum(squares, axis=0, keepdims=True) / channels + EPS)
    for ref, index in halves:
        for j in range(half // step):
            at = pl.multiple_of(index * half + j * step, step)
            x = ref[j * step:(j + 1) * step, :].astype(F32) * scale
            act[pl.ds(at, step), :] = gelu(x * gaincol[pl.ds(at, step), :1]).astype(BF16)
    rows, tokens = out_ref.shape[0], residual_ref.shape[0]
    means = window_means(0, rows, tokens, taps, positions, positions)
    out_ref[...] = dot_nt(means, act[...]).astype(BF16)
    middle = (taps // 2) * tokens
    residual_ref[...] = dot_nt(means[middle:middle + tokens], own_ref[...])


def conv_kernel(positions, windows_ref, residual_ref, halo_ref, gain_ref, weight_hbm, out_ref, weights, sems):
    taps, _, channels = weights.shape
    copies = [pltpu.make_async_copy(weight_hbm.at[t], weights.at[t], sems.at[t]) for t in range(taps)]
    ahead = 2
    for c in copies[:ahead]:
        c.start()
    tokens = out_ref.shape[0]
    h = halo_ref[...].astype(F32)
    h = h * lax.rsqrt(jnp.sum(h * h, axis=1, keepdims=True) / channels + EPS) * gain_ref[...]
    h = gelu(h).astype(BF16)
    total = residual_ref[...]
    for t in range(taps):
        window = windows_ref[t * tokens:(t + 1) * tokens]
        if t != taps // 2:
            edges = dot_nn(window_means(t * tokens, tokens, tokens, taps, positions, h.shape[0]), h)
            window = (window.astype(F32) + edges).astype(BF16)
        copies[t].wait()
        if t + ahead < taps:
            copies[t + ahead].start()
        total = total + dot_nt(window, weights[t])
    out_ref[...] = total.astype(BF16)


def block_owners():
    return owners(lax.axis_size("seq"), lax.axis_size("grp"))


def embed_kernel(pieces, pooled_ref, *refs):
    blocks, (out_ref, rest_ref) = refs[:pieces], refs[pieces:]
    half = pooled_ref.shape[1]
    for ref, owner in zip(blocks, block_owners()):
        out_ref[owner] = dot_nt(pooled_ref[...], ref[:, :half]).astype(BF16)
        rest_ref[owner] = ref[:, half:]


def keyvalue_kernel(part_ref, other_ref, gain_ref, weight_ref, kv_ref, normed_ref, embedded_ref, *send_ref):
    count, _, width = part_ref.shape
    e = (part_ref[...].astype(F32) + other_ref[...].astype(F32)).astype(BF16)
    embedded_ref[...] = e
    e = e.astype(F32)
    squares = jnp.sum(jnp.sum(e * e, axis=0), axis=1, keepdims=True)
    scale = lax.rsqrt(squares / (count * width) + EPS)
    normed_ref[...] = (e * scale[None] * gain_ref[...]).astype(BF16)
    total = 0.0
    for s in range(count):
        total = total + dot_nn(normed_ref[s], weight_ref[s])
    kv = total.T.astype(BF16)
    kv_ref[...] = kv
    for ref in send_ref:
        ref[...] = jnp.concatenate([normed_ref[s] for s in range(count)], axis=1)


def later_blocks_of(refs):
    places = block_owners()
    per = len(places) // len(refs)
    rows = refs[0].shape[0] // per
    for i, place in enumerate(places):
        start = (i % per) * rows
        yield refs[i // per], slice(start, start + rows), place


def query_kernel(sides, *refs):
    normed, pieces, query_ref = list(refs[:sides]), refs[sides:-sides], refs[-sides]
    features = query_ref.shape[1]
    count, tokens, width = normed[0].shape
    if sides > 1:
        for s in range(count):
            refs[-1][s] = normed[1][:, s * width:(s + 1) * width]
        normed[1] = refs[-1]
    totals = [0.0] * sides
    for ref, rows, place in later_blocks_of(pieces):
        weight = ref[rows, :features]
        totals = [t + dot_nn(n[place], weight) for t, n in zip(totals, normed)]
    for i, total in enumerate(totals):
        query_ref[i * tokens:(i + 1) * tokens] = (total * DK ** (-0.5)).astype(BF16)


def attend_kernel(query_ref, own_ref, other_ref, out_ref, keys, values):
    tokens, features = query_ref.shape
    blocks, _, each = own_ref.shape
    first = lax.axis_index("col") == 0
    for i in range(blocks):
        keys[:, i * each:(i + 1) * each] = jnp.where(first, own_ref[i][:DK], other_ref[i][:DK])
        values[:, i * each:(i + 1) * each] = jnp.where(first, other_ref[i], own_ref[i])
    for h in range(features // DK):
        scores = dot_nn(query_ref[:, h * DK:(h + 1) * DK], keys[...])
        weights = jnp.exp(scores - jnp.max(scores, axis=1, keepdims=True))
        total = jnp.sum(weights, axis=1, keepdims=True)
        out_ref[h] = (dot_nt(weights.astype(BF16), values[...]) / total).astype(BF16)


def output_kernel(sides, features, attended_ref, embedded_ref, pair_weight_ref, *refs):
    pieces, (keep_ref, give_ref, pair_ref, whole) = refs[:-4], refs[-4:]
    heads = attended_ref.shape[0]
    flat = jnp.concatenate([attended_ref[h] for h in range(heads)], axis=1)
    _, tokens, width = embedded_ref.shape
    col = lax.axis_index("col")
    share = jnp.where(col == 0, 1.0, 0.0)
    projected = 0.0
    for ref, rows, place in later_blocks_of(pieces):
        part = dot_nt(flat, ref[rows, features:])
        whole[place] = part.astype(BF16)
        pooled = jnp.mean(part.reshape(sides * tokens // PAIR_POOL, PAIR_POOL, width), axis=1)
        first = jnp.mean(embedded_ref[place].astype(F32).reshape(tokens // PAIR_POOL, PAIR_POOL, width), axis=1) * share
        if sides > 1:
            first = jnp.concatenate([first, jnp.zeros((pooled.shape[0] - first.shape[0], width), F32)], axis=0)
        weight = pair_weight_ref[pl.ds(pl.multiple_of(place * width, width), width)]
        projected = projected + dot_nn((pooled + first).astype(BF16), weight)
    pair_ref[...] = projected.astype(BF16)
    own = keep_ref.shape[0] // sides
    for i in range(sides):
        for ref, core in ((keep_ref, col), (give_ref, 1 - col)):
            rows = pl.ds(pl.multiple_of(i * tokens + core * own, own), own)
            ref[i * own:(i + 1) * own] = jnp.concatenate([whole[s, rows] for s in range(whole.shape[0])], axis=1)


def token_kernel(embedded_ref, *refs):
    parts, token_ref = refs[:-1], refs[-1]
    own = token_ref.shape[0]
    mine = pl.ds(pl.multiple_of(lax.axis_index("col") * own, own), own)
    embedded = jnp.concatenate([embedded_ref[s, mine] for s in range(embedded_ref.shape[0])], axis=1)
    token_ref[...] = (embedded.astype(F32) + sum(part[...].astype(F32) for part in parts)).astype(BF16)


def pair_kernel(own_ref, all_ref, weight_ref, out_ref, columns_here):
    seq, col = lax.axis_index("seq"), lax.axis_index("col")
    features, each = weight_ref.shape[0], own_ref.shape[0]
    span = columns_here.shape[0] // each
    rows = all_ref[...].astype(F32)[:, features:]
    if rows.shape[0] == columns_here.shape[0]:
        for j in range(span):
            at = pl.multiple_of((j ^ (seq % span)) * each, each)
            columns_here[pl.ds(at, each)] = rows[j * each:(j + 1) * each]
    else:
        half = columns_here.shape[0]
        columns_here[...] = jnp.where(col == 0, rows[:half], rows[half:])
    rows_here = own_ref[...].astype(F32)[:, :features]
    hidden = gelu(rows_here[:, None, :] + columns_here[...][None, :, :])
    r, c, f = hidden.shape
    out_ref[...] = dot_nn(hidden.reshape(r * c, f).astype(BF16), weight_ref[...]).reshape(r, c, f).astype(BF16)


def cost(flops, size):
    return pl.CostEstimate(flops=int(flops), bytes_accessed=int(size), transcendentals=0)


def on_device(signal, conv_weight, conv_gain, embed_weight, attn_gain, query_weight, keyvalue_weight,
              output_weight, rowcol_weight, pair_weight):
    col = lax.axis_index("col")
    count, cols = lax.axis_size("seq"), lax.axis_size("col")
    positions, half = signal.shape
    taps, channels, _ = conv_weight.shape
    reach = taps // 2
    tokens = positions // POOL
    width = embed_weight.shape[1] * count
    features = query_weight.shape[1] // cols
    heads = features // DK
    swap = [(i, (i + 1) % cols) for i in range(cols)]
    shape = jax.ShapeDtypeStruct

    embed_own = jnp.concatenate(
        [embed_weight.T, lax.dynamic_slice_in_dim(keyvalue_weight, col * DK, DV, 1)], axis=1
    )
    ring = planned(count, lax.axis_size("grp")) and cols == 2
    sides = 2 if ring else 1
    side = lax.axis_index("seq") % sides
    pair_swap = [(i, i ^ 1) for i in range(count)]
    heads, features = heads // sides, features // sides

    def later_part(which):
        place = col * sides + which
        return jnp.concatenate(
            [
                lax.dynamic_slice_in_dim(query_weight, place * features, features, 1),
                lax.dynamic_slice_in_dim(output_weight.T, place * heads * DV, heads * DV, 1),
            ],
            axis=1,
        )

    e = Blocks(embed_own, count)

    signal_t = signal.T
    up = [(i, i + 1) for i in range(count - 1)]
    if ring:
        e.along("own", "step")
        e.across("own", "own2")
    before = lax.ppermute(signal[positions - reach:], "seq", up)
    behind = lax.ppermute(signal[:reach], "seq", [(j, i) for i, j in up])
    later_mine, later_theirs = later_part(side), later_part(1 - side) if ring else None
    ready = signal_t
    if ring:
        ready = after(signal_t, e.at["step"], e.at["own2"], before, behind, later_mine, later_theirs)
    other_t = lax.ppermute(ready, "col", swap)
    own_halo = jnp.pad(jnp.concatenate([before, behind], axis=0), ((0, 16 - 2 * reach), (0, 0)))
    other_halo = lax.ppermute(own_halo, "col", swap)
    halo = jnp.where(
        col == 0, jnp.concatenate([own_halo, other_halo], axis=1), jnp.concatenate([other_halo, own_halo], axis=1)
    )
    gain_row = conv_gain.reshape(1, channels)
    windows, residual = pl.pallas_call(
        functools.partial(act_kernel, taps),
        out_shape=(shape((taps * tokens, channels), BF16), shape((tokens, half), F32)),
        in_specs=vspec(3),
        out_specs=vspec(2),
        scratch_shapes=[pltpu.VMEM((channels, positions), BF16), pltpu.VMEM((channels, 8), F32)],
        compiler_params=params(12),
        cost_estimate=cost(2 * taps * tokens * channels * positions, 4 * channels * positions),
        name="act",
    )(signal_t, other_t, gain_row)
    if ring:
        e.at["step"] = after(e.at["step"], e.at["own2"])
        e.along("step", "far")
        e.across("step", "step2")
        e.between("step", "cross")
    pooled = pl.pallas_call(
        functools.partial(conv_kernel, positions),
        out_shape=shape((tokens, half), BF16),
        in_specs=vspec(4) + hspec(1),
        out_specs=pl.BlockSpec(memory_space=VMEM),
        scratch_shapes=[pltpu.VMEM((taps, half, channels), BF16), pltpu.SemaphoreType.DMA((taps,))],
        compiler_params=params(50),
        cost_estimate=cost(2 * taps * tokens * channels * half, 2 * taps * channels * half),
        name="conv",
    )(windows, residual, halo, gain_row, conv_weight.transpose(0, 2, 1))
    if ring:
        e.at["far"] = after(e.at["far"], pooled, e.at["cross"])
        e.at["step2"] = after(e.at["step2"], pooled, e.at["cross"])
        e.along("step2", "far2")
        e.between("step2", "cross2")
        theirs = after(later_theirs, pooled, e.at["cross"])
        received = lax.ppermute(theirs, "seq", pair_swap)
        pooled = after(pooled, received)
        q = Blocks(jnp.concatenate([later_mine, received]), count)
        q.at["own"] = after(q.at["own"], e.at["far2"])
        q.along("own", "step")
        embed_blocks = e.pieces()
    else:
        embed_blocks, later_blocks = (
            [lax.all_gather(x, "seq", axis=0, tiled=True)] for x in (embed_own, later_mine)
        )
    pieces = len(embed_blocks)
    block = width // pieces

    part, keyvalue_blocks = pl.pallas_call(
        functools.partial(embed_kernel, pieces),
        out_shape=(shape((pieces, tokens, block), BF16), shape((pieces, block, DV), BF16)),
        in_specs=vspec(1 + pieces),
        out_specs=vspec(2),
        compiler_params=params(12),
        cost_estimate=cost(2 * tokens * half * width, 2 * half * width),
        name="embed",
    )(pooled, *embed_blocks)
    other_part = lax.ppermute(part, "col", swap)

    keyvalue, normed, embedded, *sending = pl.pallas_call(
        keyvalue_kernel,
        out_shape=(
            shape((DV, tokens), BF16),
            shape((pieces, tokens, block), BF16),
            shape((pieces, tokens, block), BF16),
        ) + (shape((tokens, width), BF16),) * (sides - 1),
        in_specs=vspec(4),
        out_specs=vspec(2 + sides),
        compiler_params=params(12),
        cost_estimate=cost(2 * tokens * width * DV, 2 * width * DV),
        name="keyvalue",
    )(part, other_part, attn_gain.reshape(pieces, 1, block), keyvalue_blocks)
    both_normed = [normed]
    if ring:
        turns = [[(2 * RING[k] + i, 2 * RING[(k + t) % 4] + i) for k in range(4) for i in range(2)] for t in (1, 3, 2)]
        turned = [lax.ppermute(keyvalue, "seq", turn) for turn in turns]
        both_normed.append(lax.ppermute(sending[0], "seq", pair_swap))
        q.at["step"] = after(q.at["step"], both_normed[1])
        q.along("step", "far")
        q.between("step", "cross")
        later_blocks = [q.at[name] for name in ("own", "step", "cross", "far")]
        row = jnp.stack([keyvalue] + after(turned, q.at["step"]))
        gathered = jnp.concatenate([row, lax.ppermute(row, "seq", pair_swap)])
    else:
        gathered = lax.all_gather(keyvalue, "seq", axis=0)
    gathered_other = lax.ppermute(gathered, "col", swap)

    queries = pl.pallas_call(
        functools.partial(query_kernel, sides),
        out_shape=shape((sides * tokens, features), BF16),
        in_specs=vspec(sides + len(later_blocks)),
        out_specs=pl.BlockSpec(memory_space=VMEM),
        scratch_shapes=[pltpu.VMEM((pieces, tokens, block), BF16)] * (sides - 1),
        compiler_params=params(12),
        cost_estimate=cost(2 * sides * tokens * width * features, 2 * width * features),
        name="query",
    )(*both_normed, *later_blocks)

    attended = pl.pallas_call(
        attend_kernel,
        out_shape=shape((heads, sides * tokens, DV), BF16),
        in_specs=vspec(3),
        out_specs=pl.BlockSpec(memory_space=VMEM),
        scratch_shapes=[pltpu.VMEM((DK, count * tokens), BF16), pltpu.VMEM((DV, count * tokens), BF16)],
        compiler_params=params(24),
        cost_estimate=cost(2 * tokens * heads * count * tokens * (DK + DV), 4 * count * tokens * DV),
        name="attend",
    )(queries, gathered, gathered_other)

    out_width = rowcol_weight.shape[1]
    own_rows, pair_rows = tokens // cols, tokens // PAIR_POOL
    kept = shape((sides * own_rows, width), BF16)
    keep, give, part_pair = pl.pallas_call(
        functools.partial(output_kernel, sides, features),
        out_shape=(kept, kept, shape((sides * pair_rows, out_width), BF16)),
        in_specs=vspec(3 + len(later_blocks)),
        out_specs=vspec(3),
        scratch_shapes=[pltpu.VMEM((pieces, sides * tokens, block), BF16)],
        compiler_params=params(12),
        cost_estimate=cost(2 * sides * tokens * heads * DV * width, 2 * heads * DV * width),
        name="output",
    )(attended, embedded, rowcol_weight, *later_blocks)

    def total(*parts):
        return sum(x.astype(F32) for x in parts).astype(BF16)

    if ring:
        turned = lax.ppermute(part_pair, "seq", pair_swap)
        part_pair = total(part_pair, jnp.concatenate([turned[pair_rows:], turned[:pair_rows]]))
    projected = total(part_pair, lax.ppermute(part_pair, "col", swap))
    sums = total(keep, lax.ppermute(give, "col", swap))

    if ring:
        sent = sums[own_rows:]
        crossed = lax.ppermute(sent, "seq", pair_swap)
        rows_all = after(projected, sent)
        rows_all = jnp.concatenate([rows_all, lax.ppermute(rows_all, "seq", [(i, i ^ 2) for i in range(count)])])
        rows_all = after(rows_all, crossed)
        pairs = [(i * cols + i // 4, (i ^ 4) * cols + i // 4) for i in range(count)]
        far_rows = lax.ppermute(rows_all, ("seq", "col"), pairs)
        rows_all = jnp.where(lax.axis_index("seq") // 4 == col, rows_all, far_rows)
    else:
        rows_all = lax.all_gather(projected, "seq", axis=0, tiled=True)

    parts = [sums[:own_rows]]
    if ring:
        parts.append(crossed)
    out_tokens = pl.pallas_call(
        token_kernel,
        out_shape=shape((own_rows, width), BF16),
        in_specs=vspec(1 + len(parts)),
        out_specs=pl.BlockSpec(memory_space=VMEM),
        compiler_params=params(12),
        cost_estimate=cost(3 * own_rows * width, 8 * own_rows * width),
        name="tokens",
    )(embedded, *parts)

    span = pair_rows * count // cols
    pair_features = pair_weight.shape[0]
    pair_out = pl.pallas_call(
        pair_kernel,
        out_shape=shape((pair_rows, span, pair_features), BF16),
        in_specs=vspec(3),
        out_specs=pl.BlockSpec(memory_space=VMEM),
        scratch_shapes=[pltpu.VMEM((span, pair_features), F32)],
        compiler_params=params(12),
        cost_estimate=cost(2 * pair_rows * span * pair_features**2, 2 * pair_rows * span * pair_features),
        name="pair",
    )(projected[:pair_rows], rows_all, pair_weight)
    return out_tokens, pair_out


def solution(mesh):
    placed = (
        P(("grp", "seq"), "col"),
        P(None, None, "col"),
        P(),
        P("col", "seq"),
        P(),
        P("seq", None),
        P("seq", None),
        P(None, "seq"),
        P(),
        P(),
    )
    return jax.shard_map(
        on_device,
        mesh=mesh,
        in_specs=placed,
        out_specs=(P(("grp", "seq", "col"), None), P(("grp", "seq"), "col", None)),
        check_vma=False,
    )
```
